128 devices in a mesh: dp: 4 (over y), context: 8 (over z, x_hi), tensor: 4 (over x_lo, core).
Axes of the slice: x: 4 (x_hi: 2, x_lo: 2; x = x_hi * 2 + x_lo), y: 4, z: 4, core: 2. Of those that a mesh axis runs over, the one named last changes fastest.
Arguments:
- tokens: bfloat16 [8, 1024, 2048], P('dp', 'context'), may hold values from -6 to 6
- attn_gain: bfloat16 [2048], replicated, may hold values from 0.5 to 1.5
- w_query: bfloat16 [2048, 2048], P(None, 'tensor'), may hold values from -0.125 to 0.125
- w_key: bfloat16 [2048, 1024], P(None, 'tensor'), may hold values from -0.125 to 0.125
- w_value: bfloat16 [2048, 1024], P(None, 'tensor'), may hold values from -0.125 to 0.125
- query_gain: bfloat16 [128], replicated, may hold values from 0.25 to 1.75
- key_gain: bfloat16 [128], replicated, may hold values from 0.25 to 1.75
- w_out: bfloat16 [2048, 2048], P('tensor'), may hold values from -1.5 to 1.5
- mlp_gain: bfloat16 [2048], replicated, may hold values from 0.5 to 1.5
- w_gate: bfloat16 [2048, 6144], P(None, 'tensor'), may hold values from -0.125 to 0.125
- w_up: bfloat16 [2048, 6144], P(None, 'tensor'), may hold values from -0.125 to 0.125
- w_down: bfloat16 [6144, 2048], P('tensor'), may hold values from -0.078125 to 0.078125
- out_grad: bfloat16 [8, 1024, 2048], P('dp', 'context'), may hold values from -6 to 6
Outputs:
- block_out: bfloat16 [8, 1024, 2048], P('dp', 'context')
- tokens_grad: bfloat16 [8, 1024, 2048], P('dp', 'context')
- attn_gain_grad: float32 [2048], replicated
- w_query_grad: float32 [2048, 2048], P(('dp', 'context'), 'tensor')
- w_key_grad: float32 [2048, 1024], P(('dp', 'context'), 'tensor')
- w_value_grad: float32 [2048, 1024], P(('dp', 'context'), 'tensor')
- query_gain_grad: float32 [128], replicated
- key_gain_grad: float32 [128], replicated
- w_out_grad: float32 [2048, 2048], P('tensor', ('dp', 'context'))
- mlp_gain_grad: float32 [2048], replicated
- w_gate_grad: float32 [2048, 6144], P(('dp', 'context'), 'tensor')
- w_up_grad: float32 [2048, 6144], P(('dp', 'context'), 'tensor')
- w_down_grad: float32 [6144, 2048], P('tensor', ('dp', 'context'))
The draws below stay inside these ranges and needn't reach their ends.
All inputs are finite; a program needn't handle non-finite values.
Results may differ from the reference program's by a relative error of at most 0.029.
Values may be sent and summed in bfloat16 or wider, within the bound.
A program may use at most 256 MiB of HBM per device.

```python
import jax
import jax.numpy as jnp
from jax import lax

D = 2048
HQ = 16
HK = 8
HD = 128
FF = 6144
LENGTH = 1024
BATCH = 8


def shard_levels(stream_key, extent, pieces, least, top_value):
    gain, own = 1.0, jax.random.fold_in(stream_key, 6)
    for dim, parts in pieces:
        draws = jnp.exp(jax.random.uniform(jax.random.fold_in(own, dim), (parts,), jnp.float32, least / len(pieces), top_value / len(pieces)))
        gain = gain * jnp.repeat(draws, extent[dim] // parts).reshape([-1 if axis == dim else 1 for axis in range(len(extent))])
    return gain


def centred(stream_key, extent, deviation, limit, pieces=(), dtype=jnp.bfloat16):
    gain = shard_levels(stream_key, extent, pieces, -0.22, 0.18) if pieces else 1.0
    values = jax.random.normal(stream_key, extent, jnp.float32) * deviation * gain
    return jnp.minimum(jnp.maximum(values, -limit), limit).astype(dtype)


def setup_inputs(seed: int = 0) -> dict:
    key_of = jax.random.split(jax.random.key(seed), 14)
    return {
        "tokens": centred(key_of[0], (BATCH, LENGTH, D), 1.0, 6.0, ((0, 4), (1, 8))),
        "attn_gain": jnp.clip(1.0 + 0.1 * jax.random.normal(key_of[1], (D,), jnp.float32), 0.5, 1.5).astype(jnp.bfloat16),
        "w_query": centred(key_of[2], (D, HQ * HD), D ** -0.5, 0.125, ((1, 4),)),
        "w_key": centred(key_of[3], (D, HK * HD), D ** -0.5, 0.125, ((1, 4),)),
        "w_value": centred(key_of[4], (D, HK * HD), D ** -0.5, 0.125, ((1, 4),)),
        "query_gain": jnp.clip(1.0 + 0.15 * jax.random.normal(key_of[5], (HD,), jnp.float32), 0.25, 1.75).astype(jnp.bfloat16),
        "key_gain": jnp.clip(1.0 + 0.15 * jax.random.normal(key_of[6], (HD,), jnp.float32), 0.25, 1.75).astype(jnp.bfloat16),
        "w_out": centred(key_of[7], (HQ * HD, D), (max(HQ * HD // 128, 1)) ** -0.5, 1.5, ((0, 4),)),
        "mlp_gain": jnp.clip(1.0 + 0.1 * jax.random.normal(key_of[8], (D,), jnp.float32), 0.5, 1.5).astype(jnp.bfloat16),
        "w_gate": centred(key_of[9], (D, FF), D ** -0.5, 0.125, ((1, 4),)),
        "w_up": centred(key_of[10], (D, FF), D ** -0.5, 0.125, ((1, 4),)),
        "w_down": centred(key_of[11], (FF, D), FF ** -0.5, 0.078125, ((0, 4),)),
        "out_grad": centred(key_of[12], (BATCH, LENGTH, D), 1.0, 6.0, ((0, 4), (1, 8))),
    }


EPSILON = 1e-06
ROPE_BASE = 1000000.0
PRECISE = lax.Precision.HIGHEST

@jax.custom_vjp
def low(v):
    return lax.optimization_barrier(v.astype(jnp.bfloat16)).astype(jnp.float32)

@jax.custom_vjp
def low_back(v):
    return v

def low_keep(v):
    return (low(v), None)

def low_pass(kept, grad):
    return (grad,)

def back_keep(v):
    return (v, None)

def back_low(kept, grad):
    return (low(grad),)
low.defvjp(low_keep, low_pass)
low_back.defvjp(back_keep, back_low)

def matmul(left_op, right_op):
    return jnp.dot(left_op, right_op, precision=PRECISE, preferred_element_type=jnp.float32)

def rms_norm(values, gain_vec):
    return values * lax.rsqrt(lax.optimization_barrier(jnp.mean(values * values, axis=-1, keepdims=True)) + EPSILON) * gain_vec

def rope_tables(length, head_dim):
    places = jnp.arange(length).astype(jnp.float32)
    frequency = ROPE_BASE ** (-jnp.arange(0, head_dim, 2).astype(jnp.float32) / head_dim)
    angles = places[:, None] * frequency[None, :]
    return (jnp.cos(angles), jnp.sin(angles))

def rotate(values, cosine, sine_table):
    halfway = values.shape[-1] // 2
    front_part = values[..., :halfway]
    back_part = values[..., halfway:]
    cosine = cosine[:, None, :]
    sine_table = sine_table[:, None, :]
    return jnp.concatenate([front_part * cosine - back_part * sine_table, back_part * cosine + front_part * sine_table], axis=-1)

def attend(queries, key_rows, value_rows):
    length = queries.shape[0]
    grouped = queries.reshape(length, HK, HQ // HK, HD)
    scores = jnp.einsum('ikgd,jkd->kgij', grouped, key_rows, precision=PRECISE) * HD ** (-0.5)
    scores = low_back(scores)
    places = jnp.arange(length)
    allowed = places[:, None] >= places[None, :]
    masked = jnp.where(allowed, scores, -1e+30)
    row_max = lax.optimization_barrier(jnp.max(masked, axis=-1, keepdims=True))
    exponent = jnp.exp(masked - row_max)
    probability = low(exponent / lax.optimization_barrier(jnp.sum(exponent, axis=-1, keepdims=True)))
    mixture = jnp.einsum('kgij,jkd->ikgd', probability, value_rows, precision=PRECISE)
    return mixture.reshape(length, HQ * HD)

def forward_layer(params, sequence):
    attn_scale, query_weight, key_weight, value_weight, query_scale, key_scale, out_weight, mlp_scale, gate_weight, up_weight, down_weight = params
    length = sequence.shape[0]
    normed_one = low(rms_norm(sequence, attn_scale))
    queries = low_back(matmul(normed_one, query_weight)).reshape(length, HQ, HD)
    key_rows = low_back(matmul(normed_one, key_weight)).reshape(length, HK, HD)
    value_rows = low(low_back(matmul(normed_one, value_weight))).reshape(length, HK, HD)
    cosine, sine_table = rope_tables(length, HD)
    queries = low(rotate(rms_norm(queries, query_scale), cosine, sine_table))
    key_rows = low(rotate(rms_norm(key_rows, key_scale), cosine, sine_table))
    mixture = low(low_back(jax.checkpoint(attend)(queries, key_rows, value_rows)))
    middle = sequence + low_back(matmul(mixture, out_weight))
    normed_two = low(rms_norm(middle, mlp_scale))
    gate_rows = low_back(matmul(normed_two, gate_weight))
    up_rows = low_back(matmul(normed_two, up_weight))
    hidden = low(jax.nn.silu(gate_rows) * up_rows)
    return middle + matmul(hidden, down_weight)

def reference(tokens, attn_gain, w_query, w_key, w_value, query_gain, key_gain, w_out, mlp_gain, w_gate, w_up, w_down, out_grad):
    params = tuple((member.astype(jnp.float32) for member in (attn_gain, w_query, w_key, w_value, query_gain, key_gain, w_out, mlp_gain, w_gate, w_up, w_down)))

    def advance(running, element):
        sequence, cotangent = element
        outputs, pullback = jax.vjp(forward_layer, params, sequence)
        param_grads, input_grads = pullback(cotangent)
        running = tuple((member + addend for member, addend in zip(running, param_grads)))
        return (running, (outputs.astype(jnp.bfloat16), input_grads.astype(jnp.bfloat16)))
    initial = tuple((jnp.zeros_like(member) for member in params))
    running, (outputs, input_grads) = lax.scan(advance, initial, (tokens.astype(jnp.float32), out_grad.astype(jnp.float32)))
    return (outputs, input_grads, running[0], running[1], running[2], running[3], running[4], running[5], running[6], running[7], running[8], running[9], running[10])
```

```python
import jax
import jax.numpy as jnp
from jax import lax
from jax.experimental import pallas as pl
from jax.experimental.pallas import tpu as pltpu
from jax.sharding import PartitionSpec as P

MESH = pl.DeviceIdType.MESH
BF=jnp.bfloat16; F32=jnp.float32
ORDERS=(("y0","z0","y1","z1","xh"),("z0","y1","z1","y0","xh"),("y1","z1","y0","z0","xh"),("z1","y0","z0","y1","xh"))

def me_place():
    c=lax.axis_index("context")
    return (lax.axis_index("dp"), c//2, c%2, lax.axis_index("tensor"))
def flip4(v, which):
    return v+1-2*(v%2) if which=="0" else 3-v
def partner(place, dim):
    y,z,h,t=place
    if dim=="xh": return (y,z,1-h,t)
    if dim[0]=="y": return (flip4(y,dim[1]),z,h,t)
    return (y,flip4(z,dim[1]),h,t)
def dev(place):
    y,z,h,t=place
    return (y,z*2+h,t)
def runs(base, remaining):
    y,z,h,_=base
    def ring(v,a):
        both=(a+"0" in remaining, a+"1" in remaining)
        if all(both): return None
        if both[0]: return [v,flip4(v,"0")]
        if both[1]: return [v,flip4(v,"1")]
        return [v]
    ys=ring(y,"y"); zs=ring(z,"z")
    ys=[0,1,2,3] if ys is None else ys
    out=[]
    for yy in ys:
        if zs is None:
            out.append((yy*512,512))
        else:
            for zz in zs:
                if "xh" in remaining: out.append((yy*512+zz*128,128))
                else: out.append((yy*512+zz*128+h*64,64))
    return out

def send_step(acc, recv, ssem, rsem, b, k, s, me):
    dim=ORDERS[k][s]; rem=ORDERS[k][s+1:]
    p=partner(me,dim); off=0
    for row,n in runs(p,rem):
        pltpu.make_async_remote_copy(src_ref=acc.at[b,k,pl.ds(pl.multiple_of(row,64),n)],dst_ref=recv[s].at[b,k,pl.ds(off,n)],
            send_sem=ssem.at[b,k,s],recv_sem=rsem.at[b,k,s],device_id=dev(p),device_id_type=MESH).start()
        off+=n
def add_step(acc, recv, ssem, rsem, b, k, s, me, out=None):
    rem=ORDERS[k][s+1:]
    pltpu.make_async_copy(recv[s].at[b,k],recv[s].at[b,k],rsem.at[b,k,s]).wait()
    off=0
    for row,n in runs(me,rem):
        step=min(n,128)
        def body(i,_,row=row,off=off,step=step):
            r=pl.ds(pl.multiple_of(row+i*step,64),step)
            v=acc[b,k,r].astype(F32)+recv[s][b,k,pl.ds(pl.multiple_of(off+i*step,64),step)].astype(F32)
            if out is None: acc[b,k,r]=v.astype(BF)
            else: out[b,:,k*384:(k+1)*384]=v
            return 0
        if n//step==1: body(0,0)
        else: lax.fori_loop(0,n//step,body,0)
        off+=n
def wait_send(acc,recv,ssem,b,k,s):
    pltpu.make_async_copy(recv[s].at[b,k],recv[s].at[b,k],ssem.at[b,k,s]).wait()

def rs_kernel(*refs):
    ins=refs[:7]; out=refs[7]; acc,r1,r2,r3,r4,r5,lsem,ssem,rsem=refs[8:]
    recv=(r1,r2,r3,r4,r5)
    me=me_place()
    bar=pltpu.get_barrier_semaphore()
    for d in ORDERS[0]:
        pl.semaphore_signal(bar,inc=1,device_id=dev(partner(me,d)),device_id_type=MESH)
    pieces=[]
    for b in range(3):
        for k in range(4):
            pieces.append((b,k,0,ins[b],k*384,384))
    col=0
    for r in ins[3:]:
        w=r.shape[1]; c=0
        while c<w:
            k=(col+c)//384; o=(col+c)%384; n=min(384-o,w-c)
            pieces.append((3,k,o,r,c,n)); c+=n
        col+=w
    cps={}
    for b,k,o,r,c,n in pieces:
        cp=pltpu.make_async_copy(r.at[:,c:c+n],acc.at[b,k,:,o:o+n],lsem.at[len(cps)])
        cp.start(); cps[(b,k,o)]=cp
    pl.semaphore_wait(bar,5)
    for b in range(4):
        for key,cp in cps.items():
            if key[0]==b: cp.wait()
        for k in range(4): send_step(acc,recv,ssem,rsem,b,k,0,me)
    for w in range(4+4):
        for b in range(4):
            s=w-b
            if 0<=s<5:
                for k in range(4):
                    add_step(acc,recv,ssem,rsem,b,k,s,me,out if s==4 else None)
                    if s<4: send_step(acc,recv,ssem,rsem,b,k,s+1,me)
    for b in range(4):
        for k in range(4):
            for s in range(5): wait_send(acc,recv,ssem,b,k,s)

def reduce_weights(parts):
    npieces=12+sum(1 for _ in range(6))
    return pl.pallas_call(rs_kernel,out_shape=jax.ShapeDtypeStruct((4,64,1536),F32),
      in_specs=[pl.BlockSpec(memory_space=pl.ANY)]*7,out_specs=pl.BlockSpec(memory_space=pltpu.VMEM),
      scratch_shapes=[pltpu.VMEM((4,4,2048,384),BF)]+[pltpu.VMEM((4,4,1024>>s,384),BF) for s in range(5)]+
        [pltpu.SemaphoreType.DMA((24,)),pltpu.SemaphoreType.DMA((4,4,5)),pltpu.SemaphoreType.DMA((4,4,5))],
      compiler_params=pltpu.CompilerParams(collective_id=1,has_side_effects=True,vmem_limit_bytes=62*2**20))(*parts)

EPSILON = 1e-06
ROPE_BASE = 1000000.0


def matmul(left_op, right_op):
    return jnp.dot(left_op, right_op, preferred_element_type=jnp.float32)


def matmul_tn(left_op, right_op):
    return lax.dot_general(
        left_op, right_op, (((0,), (0,)), ((), ())), preferred_element_type=jnp.float32
    )


def matmul_nt(left_op, right_op):
    return lax.dot_general(
        left_op, right_op, (((1,), (1,)), ((), ())), preferred_element_type=jnp.float32
    )


def rms_scale(values):
    return lax.rsqrt(jnp.mean(values * values, axis=-1, keepdims=True) + EPSILON)


def rms_back(grad_normed, normed, inverse):
    return inverse * (grad_normed - normed * jnp.mean(grad_normed * normed, axis=-1, keepdims=True))


def rope_tables(first_place, length, head_dim):
    places = (first_place + jnp.arange(length, dtype=jnp.int32)).astype(jnp.float32)
    frequency = ROPE_BASE ** (-jnp.arange(0, head_dim, 2).astype(jnp.float32) / head_dim)
    angles = places[:, None] * frequency[None, :]
    return (jnp.cos(angles), jnp.sin(angles))


def rotate(values, cosine, sine_table):
    halfway = values.shape[-1] // 2
    front_part = values[..., :halfway]
    back_part = values[..., halfway:]
    cosine = cosine[:, None, :]
    sine_table = sine_table[:, None, :]
    return jnp.concatenate(
        [
            front_part * cosine - back_part * sine_table,
            back_part * cosine + front_part * sine_table,
        ],
        axis=-1,
    )


def local(
    tokens,
    attn_gain,
    w_query,
    w_key,
    w_value,
    query_gain,
    key_gain,
    w_out,
    mlp_gain,
    w_gate,
    w_up,
    w_down,
    out_grad,
):
    sequences, local_len, model_width = tokens.shape
    head_dim = query_gain.shape[0]
    kv_local = w_key.shape[1] // head_dim
    group_size = w_query.shape[1] // head_dim // kv_local
    row_count = sequences * local_len
    length = local_len * lax.axis_size("context")
    first_place = lax.axis_index("context") * local_len
    quarter = row_count // lax.axis_size("tensor")
    quarter_start = lax.axis_index("tensor") * quarter
    score_scale = head_dim ** (-0.5)
    inputs = tokens.reshape(row_count, model_width).astype(jnp.float32)
    gain_one = attn_gain.astype(jnp.float32)
    gain_two = mlp_gain.astype(jnp.float32)
    gain_query = query_gain.astype(jnp.float32)
    gain_key = key_gain.astype(jnp.float32)
    inverse_one = rms_scale(inputs)
    normed_one = inputs * inverse_one
    normed_one_b = (normed_one * gain_one).astype(jnp.bfloat16)
    query_proj = matmul(normed_one_b, w_query).reshape(row_count, kv_local * group_size, head_dim)
    key_proj = matmul(normed_one_b, w_key).reshape(row_count, kv_local, head_dim)
    value_rows = matmul(normed_one_b, w_value).astype(jnp.bfloat16)
    cosine, sine_table = rope_tables(first_place, local_len, head_dim)
    cos_rows = jnp.tile(cosine, (sequences, 1))
    sin_rows = jnp.tile(sine_table, (sequences, 1))
    inverse_query = rms_scale(query_proj)
    query_hat = query_proj * inverse_query
    query_rot = rotate(query_hat * gain_query, cos_rows, sin_rows).astype(jnp.bfloat16)
    inverse_key = rms_scale(key_proj)
    key_hat = key_proj * inverse_key
    key_rot = rotate(key_hat * gain_key, cos_rows, sin_rows).astype(jnp.bfloat16)
    grouped = query_rot.reshape(sequences, local_len, kv_local, group_size, head_dim)
    key_local = key_rot.reshape(sequences, local_len, kv_local * head_dim)
    value_local = value_rows.reshape(sequences, local_len, kv_local * head_dim)
    key_full, value_full = (
        lax.all_gather(key_local, "context", axis=1, tiled=True),
        lax.all_gather(value_local, "context", axis=1, tiled=True),
    )
    key_heads = key_full.reshape(sequences, length, kv_local, head_dim)
    value_heads = value_full.reshape(sequences, length, kv_local, head_dim)
    query_places = first_place + jnp.arange(local_len, dtype=jnp.int32)
    key_places = jnp.arange(length, dtype=jnp.int32)
    allowed = query_places[:, None] >= key_places[None, :]
    scores = (
        jnp.einsum("sikgd,sjkd->skgij", grouped, key_heads, preferred_element_type=jnp.float32)
        * score_scale
    )
    masked = jnp.where(allowed, scores, -1e30)
    row_max = jnp.max(masked, axis=-1, keepdims=True)
    exponent = jnp.exp(masked - row_max)
    totals = jnp.sum(exponent, axis=-1, keepdims=True)
    log_total = row_max + jnp.log(totals)
    probability_b = (exponent / totals).astype(jnp.bfloat16)
    mixture = jnp.einsum(
        "skgij,sjkd->sikgd", probability_b, value_heads, preferred_element_type=jnp.float32
    )
    mixture = mixture.reshape(row_count, kv_local * group_size * head_dim).astype(jnp.bfloat16)
    attention_out = lax.psum(matmul(mixture, w_out), "tensor")
    middle = inputs + attention_out
    inverse_two = rms_scale(middle)
    normed_two = middle * inverse_two
    normed_two_b = (normed_two * gain_two).astype(jnp.bfloat16)
    gate_rows = matmul(normed_two_b, w_gate)
    up_rows = matmul(normed_two_b, w_up)
    sigmoid_gate = jax.nn.sigmoid(gate_rows)
    silu_gate = gate_rows * sigmoid_gate
    hidden = (silu_gate * up_rows).astype(jnp.bfloat16)
    feed_out = lax.psum(matmul(hidden, w_down).astype(jnp.bfloat16), "tensor").astype(jnp.float32)
    block_out = (middle + feed_out).astype(jnp.bfloat16).reshape(sequences, local_len, model_width)
    grad_rows = out_grad.reshape(row_count, model_width)
    grad_hidden = matmul_nt(grad_rows, w_down)
    down_grad = matmul_tn(grad_rows, hidden)
    grad_gate = (
        grad_hidden * up_rows * sigmoid_gate * (1.0 + gate_rows * (1.0 - sigmoid_gate))
    ).astype(jnp.bfloat16)
    grad_up = (grad_hidden * silu_gate).astype(jnp.bfloat16)
    gate_grad = matmul_tn(normed_two_b, grad_gate)
    up_grad = matmul_tn(normed_two_b, grad_up)
    grad_normed_two = lax.psum(
        (matmul_nt(grad_gate, w_gate) + matmul_nt(grad_up, w_up)).astype(jnp.bfloat16), "tensor"
    ).astype(jnp.float32)
    gain_two_term = jnp.sum(
        lax.dynamic_slice_in_dim(grad_normed_two * normed_two, quarter_start, quarter, 0), axis=0
    )
    grad_middle = grad_rows.astype(jnp.float32) + rms_back(
        grad_normed_two * gain_two, normed_two, inverse_two
    )
    grad_branch = grad_middle.astype(jnp.bfloat16)
    out_weight_grad = matmul_tn(grad_branch, mixture)
    grad_mixture = matmul_nt(grad_branch, w_out).astype(jnp.bfloat16)
    grad_mixture = grad_mixture.reshape(sequences, local_len, kv_local, group_size, head_dim)
    scores_again = (
        jnp.einsum("sikgd,sjkd->skgij", grouped, key_heads, preferred_element_type=jnp.float32)
        * score_scale
    )
    probability = jnp.exp(jnp.where(allowed, scores_again, -1e30) - log_total)
    grad_prob = jnp.einsum(
        "sikgd,sjkd->skgij", grad_mixture, value_heads, preferred_element_type=jnp.float32
    )
    inner_sum = jnp.sum(probability * grad_prob, axis=-1, keepdims=True)
    grad_scores = (probability * (grad_prob - inner_sum)).astype(jnp.bfloat16)
    grad_query = (
        jnp.einsum("skgij,sjkd->sikgd", grad_scores, key_heads, preferred_element_type=jnp.float32)
        * score_scale
    )
    grad_key_full = (
        jnp.einsum("skgij,sikgd->sjkd", grad_scores, grouped, preferred_element_type=jnp.float32)
        * score_scale
    )
    grad_value_full = jnp.einsum(
        "skgij,sikgd->sjkd",
        probability.astype(jnp.bfloat16),
        grad_mixture,
        preferred_element_type=jnp.float32,
    )
    grad_key_own, grad_value_own = (
        lax.psum_scatter(
            grad_key_full.reshape(sequences, length, kv_local * head_dim).astype(jnp.bfloat16),
            "context",
            scatter_dimension=1,
            tiled=True,
        ).astype(jnp.float32),
        lax.psum_scatter(
            grad_value_full.reshape(sequences, length, kv_local * head_dim).astype(jnp.bfloat16),
            "context",
            scatter_dimension=1,
            tiled=True,
        ).astype(jnp.float32),
    )
    grad_query_normed = rotate(
        grad_query.reshape(row_count, kv_local * group_size, head_dim), cos_rows, -sin_rows
    )
    query_gain_term = jnp.sum(grad_query_normed * query_hat, axis=(0, 1))
    grad_query_proj = (
        rms_back(grad_query_normed * gain_query, query_hat, inverse_query)
        .reshape(row_count, -1)
        .astype(jnp.bfloat16)
    )
    grad_key_normed = rotate(
        grad_key_own.reshape(row_count, kv_local, head_dim), cos_rows, -sin_rows
    )
    key_gain_term = jnp.sum(grad_key_normed * key_hat, axis=(0, 1))
    grad_key_proj = (
        rms_back(grad_key_normed * gain_key, key_hat, inverse_key)
        .reshape(row_count, -1)
        .astype(jnp.bfloat16)
    )
    grad_value_b = grad_value_own.reshape(row_count, kv_local * head_dim).astype(jnp.bfloat16)
    grad_normed_one = lax.psum(
        (
            matmul_nt(grad_query_proj, w_query)
            + matmul_nt(grad_key_proj, w_key)
            + matmul_nt(grad_value_b, w_value)
        ).astype(jnp.bfloat16),
        "tensor",
    ).astype(jnp.float32)
    gain_one_term = jnp.sum(
        lax.dynamic_slice_in_dim(grad_normed_one * normed_one, quarter_start, quarter, 0), axis=0
    )
    tokens_grad = (
        grad_middle + rms_back(grad_normed_one * gain_one, normed_one, inverse_one)
    ).astype(jnp.bfloat16)
    tokens_grad = tokens_grad.reshape(sequences, local_len, model_width)
    query_grad = matmul_tn(normed_one_b, grad_query_proj)
    key_grad = matmul_tn(normed_one_b, grad_key_proj)
    value_grad = matmul_tn(normed_one_b, grad_value_b)
    gain_grads = lax.psum(
        (gain_one_term, query_gain_term, key_gain_term, gain_two_term), ("dp", "context", "tensor")
    )
    low = lambda v: v.astype(jnp.bfloat16)
    summed = reduce_weights(
        (low(down_grad), low(gate_grad), low(up_grad), low(out_weight_grad), low(query_grad), low(key_grad), low(value_grad))
    )
    down_part, gate_part, up_part = summed[0], summed[1], summed[2]
    out_part, query_part = summed[3, :, :512], summed[3, :, 512:1024]
    key_part, value_part = summed[3, :, 1024:1280], summed[3, :, 1280:]
    return (
        block_out,
        tokens_grad,
        gain_grads[0],
        query_part,
        key_part,
        value_part,
        gain_grads[1],
        gain_grads[2],
        out_part.T,
        gain_grads[3],
        gate_part,
        up_part,
        down_part.T,
    )


def solution(mesh):
    in_specs = (
        P("dp", "context", None),
        P(),
        P(None, "tensor"),
        P(None, "tensor"),
        P(None, "tensor"),
        P(),
        P(),
        P("tensor", None),
        P(),
        P(None, "tensor"),
        P(None, "tensor"),
        P("tensor", None),
        P("dp", "context", None),
    )
    out_specs = (
        P("dp", "context", None),
        P("dp", "context", None),
        P(),
        P(("dp", "context"), "tensor"),
        P(("dp", "context"), "tensor"),
        P(("dp", "context"), "tensor"),
        P(),
        P(),
        P("tensor", ("dp", "context")),
        P(),
        P(("dp", "context"), "tensor"),
        P(("dp", "context"), "tensor"),
        P("tensor", ("dp", "context")),
    )
    return jax.shard_map(local, mesh=mesh, in_specs=in_specs, out_specs=out_specs, check_vma=False)
```

```python
import functools
import numpy as np
import jax
import jax.numpy as jnp
from jax import lax
from jax.experimental import pallas as pl
from jax.experimental.pallas import tpu as pltpu
from jax.sharding import PartitionSpec as P

MESH = pl.DeviceIdType.MESH
BF = jnp.bfloat16
F32 = jnp.float32
EPSILON = 1e-06
ROPE_BASE = 1000000.0
SCALE = 128 ** (-0.5)


def me_place():
    c = lax.axis_index("context")
    return (lax.axis_index("dp"), c // 2, c % 2, lax.axis_index("tensor"))


def dev(place):
    y, z, h, t = place
    return (y, z * 2 + h, t)


def core_partner(place):
    y, z, h, t = place
    return (y, z, h, t + 1 - 2 * (t % 2))


def xlo_partner(place):
    y, z, h, t = place
    return (y, z, h, (t + 2) % 4)


def dot(a, b):
    return jnp.dot(a, b, preferred_element_type=F32)


def dot_nt(a, b):
    return lax.dot_general(a, b, (((1,), (1,)), ((), ())), preferred_element_type=F32)


def dot_tn(a, b):
    return lax.dot_general(a, b, (((0,), (0,)), ((), ())), preferred_element_type=F32)


def rows_at(start, n):
    return pl.ds(pl.multiple_of(start, 64), n)


class TensorSum:
    def __init__(self, me, part, low, recv_core, send_x, recv_x, sems, chunks):
        self.me, self.part, self.low = me, part, low
        self.recv_core, self.send_x, self.recv_x, self.sems = recv_core, send_x, recv_x, sems
        self.chunks, self.width = chunks, 2048 // chunks
        t = me[3]
        self.xl, self.core = t // 2, t % 2

    def cols(self, j):
        return pl.ds(j * self.width, self.width)

    def core_copies(self, j):
        other = 1 - self.core
        return [
            pltpu.make_async_remote_copy(
                src_ref=self.low.at[rows_at(a * 128 + other * 64, 64), self.cols(j)],
                dst_ref=self.recv_core.at[a, :, self.cols(j)],
                send_sem=self.sems.at[0, j, a], recv_sem=self.sems.at[1, j, a],
                device_id=dev(core_partner(self.me)), device_id_type=MESH)
            for a in range(2)
        ]

    def x_copy(self, j):
        return pltpu.make_async_remote_copy(
            src_ref=self.send_x.at[:, self.cols(j)], dst_ref=self.recv_x.at[:, self.cols(j)],
            send_sem=self.sems.at[2, j, 0], recv_sem=self.sems.at[2, j, 1],
            device_id=dev(xlo_partner(self.me)), device_id_type=MESH)

    def put(self, j, value):
        self.part[:, self.cols(j)] = value
        self.low[:, self.cols(j)] = value.astype(BF)
        for cp in self.core_copies(j):
            cp.start()

    def send_on(self, j):
        for cp in self.core_copies(j):
            cp.wait_recv()
        away = 1 - self.xl
        summed = self.part[rows_at(away * 128 + self.core * 64, 64), self.cols(j)]
        summed = summed + self.recv_core[away, :, self.cols(j)].astype(F32)
        self.send_x[:, self.cols(j)] = summed.astype(BF)
        self.x_copy(j).start()

    def take(self, j):
        self.x_copy(j).wait_recv()
        own = self.part[rows_at(self.xl * 128 + self.core * 64, 64), self.cols(j)]
        return own + self.recv_core[self.xl, :, self.cols(j)].astype(F32) + self.recv_x[:, self.cols(j)].astype(F32)

    def finish(self):
        for j in range(self.chunks):
            for cp in self.core_copies(j):
                cp.wait_send()
            self.x_copy(j).wait_send()


class TensorGather:
    def __init__(self, me, full, sems, chunks=2):
        self.me, self.full, self.sems, self.chunks = me, full, sems, chunks
        self.width = 2048 // chunks

    def copy(self, kind, j):
        t = self.me[3]
        x_rows = (t + 2) % 4
        target = xlo_partner(self.me) if kind == 0 else core_partner(self.me)
        row = x_rows if kind == 2 else t
        view = self.full.at[rows_at(row * 64, 64), pl.ds(j * self.width, self.width)]
        return pltpu.make_async_remote_copy(
            src_ref=view, dst_ref=view, send_sem=self.sems.at[kind, j, 0],
            recv_sem=self.sems.at[kind, j, 1], device_id=dev(target), device_id_type=MESH)

    def start(self):
        for j in range(self.chunks):
            self.copy(0, j).start()
        for j in range(self.chunks):
            self.copy(1, j).start()

    def forward(self):
        for j in range(self.chunks):
            self.copy(0, j).wait_recv()
            self.copy(2, j).start()

    def finish(self):
        for j in range(self.chunks):
            self.copy(1, j).wait_recv()
            self.copy(2, j).wait_recv()
            for kind in range(3):
                self.copy(kind, j).wait_send()


def rope_constants():
    frequency = np.float32(ROPE_BASE) ** (-np.arange(0, 128, 2).astype(np.float32) / np.float32(128))
    angles = np.arange(1024, dtype=np.float32)[:, None] * frequency.astype(np.float32)[None, :]
    cosine, sine = np.cos(angles), np.sin(angles)
    return (np.concatenate([cosine, cosine], 1).astype(np.float32),
            np.concatenate([-sine, sine], 1).astype(np.float32))


def half_turn(v):
    return pltpu.roll(v, 64, axis=1)


def front_kernel(x_ref, gain1, wq_h, wk_h, wv_h, qg, kg, wo_h, gain2, cos_h, sin_h,
                 n1_ref, n2_ref, mid_ref, q_ref, kv_ref, p_ref, mix_ref, proj_ref,
                 wq, wk, wv, wo, cosv, sinv, part, low, recv_core, send_x, recv_x,
                 lsem, kvs, kvr, tsem, gsem):
    me = me_place()
    ctx = lax.axis_index("context")
    loads = [pltpu.make_async_copy(s, d, lsem.at[i]) for i, (s, d) in enumerate(
        [(wk_h, wk), (wv_h, wv), (wq_h, wq), (wo_h, wo),
         (cos_h.at[rows_at(ctx * 128, 128)], cosv), (sin_h.at[rows_at(ctx * 128, 128)], sinv)])]
    for cp in loads:
        cp.start()
    bar = pltpu.get_barrier_semaphore()
    for d in range(1, 8):
        pl.semaphore_signal(bar, inc=1, device_id=(me[0], (ctx + d) % 8, me[3]), device_id_type=MESH)
    pl.semaphore_signal(bar, inc=1, device_id=dev(core_partner(me)), device_id_type=MESH)
    pl.semaphore_signal(bar, inc=1, device_id=dev(xlo_partner(me)), device_id_type=MESH)

    g1 = gain1[...].astype(F32)

    def norm_rows(i, _):
        r = pl.ds(pl.multiple_of(i * 32, 32), 32)
        xv = x_ref[r, :].astype(F32)
        inv = lax.rsqrt(jnp.mean(xv * xv, axis=-1, keepdims=True) + EPSILON)
        n1_ref[r, :] = (xv * inv * g1).astype(BF)
        return 0

    lax.fori_loop(0, 8, norm_rows, 0)
    for cp in loads[4:]:
        cp.wait()
    cos2 = jnp.concatenate([cosv[...], cosv[...]], axis=0)
    sin2 = jnp.concatenate([sinv[...], sinv[...]], axis=0)
    gq = qg[...].astype(F32)
    gk = kg[...].astype(F32)

    def turned(v, gain):
        hat = v * lax.rsqrt(jnp.mean(v * v, axis=-1, keepdims=True) + EPSILON)
        hat = hat * gain
        return (hat * cos2 + half_turn(hat) * sin2).astype(BF)

    n1 = n1_ref[...]
    loads[0].wait()
    kp = dot(n1, wk[...])
    proj_ref[:, 512:768] = kp
    loads[1].wait()
    kv_ref[ctx, :, 256:512] = dot(n1, wv[...]).astype(BF)
    for h in range(2):
        kv_ref[ctx, :, h * 128:(h + 1) * 128] = turned(kp[:, h * 128:(h + 1) * 128], gk)
    pl.semaphore_wait(bar, 9)

    def kv_copy(d):
        return pltpu.make_async_remote_copy(
            src_ref=kv_ref.at[ctx], dst_ref=kv_ref.at[ctx], send_sem=kvs.at[d], recv_sem=kvr.at[ctx],
            device_id=(me[0], (ctx + d) % 8, me[3]), device_id_type=MESH)

    for d in range(1, 8):
        @pl.when(ctx + d < 8)
        def _():
            kv_copy(d).start()

    for j in range(1, 8):
        @pl.when(j > ctx)
        def _():
            kv_ref[j] = jnp.zeros((256, 512), BF)

    loads[2].wait()
    qp = dot(n1, wq[...])
    proj_ref[:, 0:512] = qp
    for h in range(4):
        rot = turned(qp[:, h * 128:(h + 1) * 128], gq)
        for s in range(2):
            q_ref[s, h // 2, (h % 2) * 128:(h % 2 + 1) * 128, :] = rot[s * 128:(s + 1) * 128]
    loads[3].wait()

    for j in range(7):
        @pl.when(j < ctx)
        def _():
            pltpu.make_async_copy(kv_ref.at[j], kv_ref.at[j], kvr.at[j]).wait()

    place = lax.broadcasted_iota(jnp.int32, (256, 1024), 0) % 128 + ctx * 128
    allowed = place >= lax.broadcasted_iota(jnp.int32, (256, 1024), 1)
    for s in range(2):
        for kh in range(2):
            keys = kv_ref[:, s * 128:(s + 1) * 128, kh * 128:(kh + 1) * 128].reshape(1024, 128)
            values = kv_ref[:, s * 128:(s + 1) * 128, 256 + kh * 128:256 + (kh + 1) * 128].reshape(1024, 128)
            scores = jnp.where(allowed, dot_nt(q_ref[s, kh], keys) * SCALE, -1e30)
            top = jnp.max(scores, axis=-1, keepdims=True)
            e = jnp.exp(scores - top)
            prob = (e / jnp.sum(e, axis=-1, keepdims=True)).astype(BF)
            p_ref[s, kh] = prob
            mixed = dot(prob, values).astype(BF)
            for g in range(2):
                h = kh * 2 + g
                mix_ref[s * 128:(s + 1) * 128, h * 128:(h + 1) * 128] = mixed[g * 128:(g + 1) * 128]

    chunks = 4
    ts = TensorSum(me, part, low, recv_core, send_x, recv_x, tsem, chunks)
    mix = mix_ref[...]
    for j in range(chunks):
        ts.put(j, dot(mix, wo[:, ts.cols(j)]))
        if j:
            ts.send_on(j - 1)
    ts.send_on(chunks - 1)
    own = rows_at(me[3] * 64, 64)
    for j in range(chunks):
        mid_ref[:, ts.cols(j)] = x_ref[own, ts.cols(j)].astype(F32) + ts.take(j)
    g2 = gain2[...].astype(F32)
    mid = mid_ref[...]
    inv = lax.rsqrt(jnp.mean(mid * mid, axis=-1, keepdims=True) + EPSILON)
    n2_ref[own, :] = (mid * inv * g2).astype(BF)
    tg = TensorGather(me, n2_ref, gsem)
    tg.start()
    tg.forward()
    tg.finish()
    ts.finish()
    for d in range(1, 8):
        @pl.when(ctx + d < 8)
        def _():
            kv_copy(d).wait_send()


def front(x, gain1, wq, wk, wv, qg, kg, wo, gain2):
    cos_t, sin_t = rope_constants()
    V = pl.BlockSpec(memory_space=pltpu.VMEM)
    A = pl.BlockSpec(memory_space=pl.ANY)
    S = jax.ShapeDtypeStruct
    D = pltpu.SemaphoreType.DMA
    return pl.pallas_call(
        front_kernel,
        out_shape=(S((256, 2048), BF), S((256, 2048), BF), S((64, 2048), F32), S((2, 2, 256, 128), BF),
                   S((8, 256, 512), BF), S((2, 2, 256, 1024), BF), S((256, 512), BF), S((256, 768), F32)),
        in_specs=[V, V, A, A, A, V, V, A, V, A, A],
        out_specs=(V,) * 8,
        scratch_shapes=[
            pltpu.VMEM((2048, 512), BF), pltpu.VMEM((2048, 256), BF), pltpu.VMEM((2048, 256), BF),
            pltpu.VMEM((512, 2048), BF), pltpu.VMEM((128, 128), F32), pltpu.VMEM((128, 128), F32),
            pltpu.VMEM((256, 2048), F32), pltpu.VMEM((256, 2048), BF), pltpu.VMEM((2, 64, 2048), BF),
            pltpu.VMEM((64, 2048), BF), pltpu.VMEM((64, 2048), BF),
            D((6,)), D((8,)), D((8,)), D((3, 4, 2)), D((3, 2, 2))],
        compiler_params=pltpu.CompilerParams(collective_id=2, has_side_effects=True, vmem_limit_bytes=60 * 2**20),
    )(x, gain1.reshape(1, -1), wq, wk, wv, qg.reshape(1, -1), kg.reshape(1, -1), wo, gain2.reshape(1, -1),
      jnp.asarray(cos_t), jnp.asarray(sin_t))


ORDERS = (("y0", "z0", "y1", "z1", "xh"), ("z0", "y1", "z1", "y0", "xh"),
          ("y1", "z1", "y0", "z0", "xh"), ("z1", "y0", "z0", "y1", "xh"))


def flip4(v, which):
    return v + 1 - 2 * (v % 2) if which == "0" else 3 - v


def partner(place, dim):
    y, z, h, t = place
    if dim == "core":
        return core_partner(place)
    if dim == "xl":
        return xlo_partner(place)
    if dim == "xh":
        return (y, z, 1 - h, t)
    if dim[0] == "y":
        return (flip4(y, dim[1]), z, h, t)
    return (y, flip4(z, dim[1]), h, t)


def owner_runs(base, remaining):
    y, z, h, _ = base

    def ring(v, axis):
        both = (axis + "0" in remaining, axis + "1" in remaining)
        if all(both):
            return None
        if both[0]:
            return [v, flip4(v, "0")]
        if both[1]:
            return [v, flip4(v, "1")]
        return [v]

    ys, zs = ring(y, "y"), ring(z, "z")
    found = []
    for yy in [0, 1, 2, 3] if ys is None else ys:
        if zs is None:
            found.append((yy * 512, 512))
            continue
        for zz in zs:
            if "xh" in remaining:
                found.append((yy * 512 + zz * 128, 128))
            else:
                found.append((yy * 512 + zz * 128 + h * 64, 64))
    return found


def windows(first, count):
    found, done = [], 0
    while done < count:
        piece, off = divmod(first + done, 384)
        n = min(384 - off, count - done)
        found.append((piece, off, done, n))
        done += n
    return found


class WeightSum:
    def __init__(self, me, acc, recv, stage, ssem, rsem, lsem, outs):
        self.me, self.acc, self.recv, self.stage = me, acc, recv, stage
        self.ssem, self.rsem, self.lsem, self.outs = ssem, rsem, lsem, outs

    def put(self, b, first, row, value):
        low = value.astype(BF)
        n = value.shape[0]
        for piece, off, src, w in windows(first, value.shape[1]):
            self.acc[b, piece, row:row + n, off:off + w] = low[:, src:src + w]

    def send(self, b, k, s):
        dim, rest = ORDERS[k][s], ORDERS[k][s + 1:]
        to, off = partner(self.me, dim), 0
        for row, n in owner_runs(to, rest):
            pltpu.make_async_remote_copy(
                src_ref=self.acc.at[b, k, rows_at(row, n)], dst_ref=self.recv[s].at[b, k, pl.ds(off, n)],
                send_sem=self.ssem.at[b, k, s], recv_sem=self.rsem.at[b, k, s],
                device_id=dev(to), device_id_type=MESH).start()
            off += n

    def start(self, b):
        for k in range(4):
            self.send(b, k, 0)

    def arrived(self, b, k, s):
        view = self.recv[s].at[b, k]
        pltpu.make_async_copy(view, view, self.rsem.at[b, k, s]).wait()

    def staged(self, b, k, s):
        n = 1024 >> s
        return pltpu.make_async_copy(self.recv[s].at[b, k], self.stage.at[k % 2, pl.ds(0, n)], self.lsem.at[k % 2])

    def add(self, b, k, s, view):
        off = 0
        for row, n in owner_runs(self.me, ORDERS[k][s + 1:]):
            step = min(n, 128)

            def body(i, _, row=row, off=off, step=step):
                r = rows_at(row + i * step, step)
                v = self.acc[b, k, r].astype(F32) + view[pl.ds(pl.multiple_of(off + i * step, 64), step)].astype(F32)
                if s < 4:
                    self.acc[b, k, r] = v.astype(BF)
                else:
                    for out, col, first, n in self.outs[b]:
                        for piece, o, src, w in windows(first, n):
                            if piece == k:
                                out[:, col + src:col + src + w] = v[:, o:o + w]
                return 0

            if n == step:
                body(0, 0)
            else:
                lax.fori_loop(0, n // step, body, 0)
            off += n

    def advance(self, b, s):
        if s < 3:
            self.arrived(b, 0, s)
            self.staged(b, 0, s).start()
        for k in range(4):
            if s < 3:
                if k < 3:
                    self.arrived(b, k + 1, s)
                    self.staged(b, k + 1, s).start()
                self.staged(b, k, s).wait()
                self.add(b, k, s, self.stage.at[k % 2])
            else:
                self.arrived(b, k, s)
                self.add(b, k, s, self.recv[s].at[b, k])
            if s < 4:
                self.send(b, k, s + 1)

    def finish(self):
        for b in range(4):
            for k in range(4):
                for s in range(5):
                    view = self.recv[s].at[b, k]
                    pltpu.make_async_copy(view, view, self.ssem.at[b, k, s]).wait()


GAIN_DIMS = ("core", "xl", "xh", "y0", "z0", "y1", "z1")


class GainSum:
    def __init__(self, me, held, recv, sems):
        self.me, self.held, self.recv, self.sems = me, held, recv, sems

    def copy(self, i):
        return pltpu.make_async_remote_copy(
            src_ref=self.held.at[i], dst_ref=self.recv.at[i], send_sem=self.sems.at[i, 0], recv_sem=self.sems.at[i, 1],
            device_id=dev(partner(self.me, GAIN_DIMS[i])), device_id_type=MESH)

    def start(self):
        self.copy(0).start()

    def advance(self, i):
        self.copy(i).wait_recv()
        self.held[i + 1] = self.held[i] + self.recv[i]
        if i < 6:
            self.copy(i + 1).start()

    def finish(self):
        for i in range(7):
            self.copy(i).wait_send()


def back_kernel(n1_ref, n2_ref, mid_ref, q_ref, kv_h, p_ref, mix_ref, proj_ref, g_ref, x_h, gain1, gain2, qg, kg,
                wq_h, wk_h, wv_h, wo_h, wg_h, wu_h, wd_h, cos_h, sin_h,
                block_ref, tok_ref, gains_ref, down_o, gate_o, up_o, out_o, q_o, k_o, v_o, recv0, recv1, recv2,
                acc, recv3, recv4, stage, turned_a, turned_b, wgb, wub, wdb, gn2, feed,
                low_a, core_a, core_b, sx_a, sx_b, rx_a, rx_b, gb, gmid, kv, dkv_recv, gqkv,
                x_own, cosv, sinv, held, grecv,
                wsem, lsem, ssem, rsem, stsem, ts2, tsf, ts1, tgb, tgo, tgt, dks, dkr, gsem):
    me = me_place()
    ctx = lax.axis_index("context")
    own = rows_at(me[3] * 64, 64)
    dq_ref, dtot = feed.at[:, 0:512], feed.at[:, 512:1024]
    loads = [pltpu.make_async_copy(s, d, lsem.at[i]) for i, (s, d) in enumerate(
        [(kv_h, kv), (x_h.at[own], x_own), (cos_h.at[rows_at(ctx * 128, 128)], cosv),
         (sin_h.at[rows_at(ctx * 128, 128)], sinv)])]

    def tile_loads(j):
        b = j % 2
        c = pl.ds(j * 256, 256)
        return [pltpu.make_async_copy(wg_h.at[:, c], wgb.at[b], wsem.at[b, 0]),
                pltpu.make_async_copy(wu_h.at[:, c], wub.at[b], wsem.at[b, 1]),
                pltpu.make_async_copy(wd_h.at[c], wdb.at[b], wsem.at[b, 2])]

    def late_loads(b):
        c = pl.ds(b * 256, 256)
        return [pltpu.make_async_copy(wq_h.at[:, c], wgb.at[b], wsem.at[b, 0]),
                pltpu.make_async_copy((wk_h, wv_h)[b], wub.at[b], wsem.at[b, 1]),
                pltpu.make_async_copy(wo_h.at[c], wdb.at[b], wsem.at[b, 2])]

    for j in range(2):
        for cp in tile_loads(j):
            cp.start()
    for cp in loads:
        cp.start()
    bar = pltpu.get_barrier_semaphore()
    for d in range(1, 8):
        pl.semaphore_signal(bar, inc=1, device_id=(me[0], (ctx + d) % 8, me[3]), device_id_type=MESH)
    for d in ("core", "xl", "y0", "y1"):
        pl.semaphore_signal(bar, inc=1, device_id=dev(partner(me, d)), device_id_type=MESH)

    outs = [[(down_o, b * 512, 0, 512), (gate_o, b * 512, 512, 512), (up_o, b * 512, 1024, 512)] for b in range(3)]
    outs.append([(out_o, 0, 0, 512), (q_o, 0, 512, 512), (k_o, 0, 1024, 256), (v_o, 0, 1280, 256)])
    ws = WeightSum(me, acc, (recv0, recv1, recv2, recv3, recv4), stage, ssem, rsem, stsem, outs)

    def turn(src, dst):
        for i in range(8):
            dst[i * 256:(i + 1) * 256, :] = src[:, i * 256:(i + 1) * 256].T

    def outer(b, first, left, right):
        for i in range(4):
            ws.put(b, first, i * 512, dot(left[i * 512:(i + 1) * 512, :], right))

    turn(n2_ref, turned_a)
    turn(g_ref, turned_b)
    for j in range(6):
        b = j % 2
        for cp in tile_loads(j):
            cp.wait()
        n2 = n2_ref[...]
        gate = dot(n2, wgb[b])
        up = dot(n2, wub[b])
        gh = dot_nt(g_ref[...], wdb[b])
        sig = 1.0 / (1.0 + jnp.exp(-gate))
        silu = gate * sig
        hid = (silu * up).astype(BF)
        gg = (gh * up * sig * (1.0 + gate * (1.0 - sig))).astype(BF)
        gu = (gh * silu).astype(BF)
        for i in range(4):
            c = slice(i * 512, (i + 1) * 512)
            back = dot_nt(gg, wgb[b, c, :]) + dot_nt(gu, wub[b, c, :])
            forth = dot(hid, wdb[b, :, c])
            if j == 0:
                gn2[:, c] = back
                feed[:, c] = forth
            else:
                gn2[:, c] += back
                feed[:, c] += forth
        for cp in (tile_loads(j + 2) if j < 4 else late_loads(b)):
            cp.start()
        outer(j // 2, b * 256, turned_b, hid)
        outer(j // 2, 512 + b * 256, turned_a, gg)
        outer(j // 2, 1024 + b * 256, turned_a, gu)
        if j == 1:
            pl.semaphore_wait(bar, 11)
        if b == 1:
            ws.start(j // 2)

    chunks = 4
    sum2 = TensorSum(me, gn2, low_a, core_a, sx_a, rx_a, ts2, chunks)
    sumf = TensorSum(me, feed, tok_ref, core_b, sx_b, rx_b, tsf, chunks)
    for j in range(chunks):
        sum2.put(j, gn2[:, sum2.cols(j)])
        if j:
            sum2.send_on(j - 1)
    sum2.send_on(chunks - 1)
    for j in range(chunks):
        sumf.put(j, feed[:, sumf.cols(j)])
    turn(n1_ref, turned_a)
    mid = mid_ref[...]
    inv2 = lax.rsqrt(jnp.mean(mid * mid, axis=-1, keepdims=True) + EPSILON)
    for j in range(chunks):
        gmid[:, sum2.cols(j)] = sum2.take(j)
    grad = gmid[...]
    hat2 = mid * inv2
    held[0] = jnp.zeros((8, 2048), F32)
    held[0, 1:2, :] = jnp.sum(grad * hat2, axis=0, keepdims=True)
    u = grad * gain2[...].astype(F32)
    grad = g_ref[own, :].astype(F32) + inv2 * (u - hat2 * jnp.mean(u * hat2, axis=-1, keepdims=True))
    gmid[...] = grad
    gb[own, :] = grad.astype(BF)
    gather_b = TensorGather(me, gb, tgb)
    gather_b.start()
    for j in range(chunks):
        sumf.send_on(j)
    gather_b.forward()
    for j in range(chunks):
        block_ref[own, sumf.cols(j)] = (mid_ref[:, sumf.cols(j)] + sumf.take(j)).astype(BF)
    gather_b.finish()
    gather_o = TensorGather(me, block_ref, tgo)
    gather_o.start()

    for b in range(2):
        for cp in late_loads(b):
            cp.wait()
    gb_all = gb[...]
    gmix = [dot_nt(gb_all, wdb[b]).astype(BF) for b in range(2)]
    for cp in loads:
        cp.wait()
    for s in range(2):
        for kh in range(2):
            ks = (slice(None), slice(s * 128, (s + 1) * 128), slice(kh * 128, (kh + 1) * 128))
            vs = (slice(None), slice(s * 128, (s + 1) * 128), slice(256 + kh * 128, 256 + (kh + 1) * 128))
            keys = kv[ks].reshape(1024, 128)
            values = kv[vs].reshape(1024, 128)
            both = gmix[kh][s * 128:(s + 1) * 128]
            gm = jnp.concatenate([both[:, :128], both[:, 128:]], axis=0)
            prob = p_ref[s, kh]
            gp = dot_nt(gm, values)
            prob32 = prob.astype(F32)
            inner = jnp.sum(prob32 * gp, axis=-1, keepdims=True)
            gs = (prob32 * (gp - inner)).astype(BF)
            dq = dot(gs, keys) * SCALE
            for g in range(2):
                h = kh * 2 + g
                dq_ref[s * 128:(s + 1) * 128, h * 128:(h + 1) * 128] = dq[g * 128:(g + 1) * 128]
            kv[ks] = (dot_tn(gs, q_ref[s, kh]) * SCALE).astype(BF).reshape(8, 128, 128)
            kv[vs] = dot_tn(prob, gm).astype(BF).reshape(8, 128, 128)

    def dkv_copy(j):
        return pltpu.make_async_remote_copy(
            src_ref=kv.at[j], dst_ref=dkv_recv.at[ctx], send_sem=dks.at[j], recv_sem=dkr.at[ctx],
            device_id=(me[0], j, me[3]), device_id_type=MESH)

    for j in range(7):
        @pl.when(j < ctx)
        def _():
            dkv_copy(j).start()

    gather_o.forward()
    cos2 = jnp.concatenate([cosv[...], cosv[...]], axis=0)
    sin2 = jnp.concatenate([sinv[...], sinv[...]], axis=0)
    gqf = qg[...].astype(F32)
    gkf = kg[...].astype(F32)

    def through_norm(grad_rot, proj, gain):
        grad_normed = grad_rot * cos2 - half_turn(grad_rot) * sin2
        inv = lax.rsqrt(jnp.mean(proj * proj, axis=-1, keepdims=True) + EPSILON)
        hat = proj * inv
        u = grad_normed * gain
        grad_proj = inv * (u - hat * jnp.mean(u * hat, axis=-1, keepdims=True))
        return grad_proj.astype(BF), jnp.sum(grad_normed * hat, axis=0, keepdims=True)

    gain_sum = jnp.zeros((1, 128), F32)
    for h in range(4):
        c = slice(h * 128, (h + 1) * 128)
        gqkv[:, c], term = through_norm(dq_ref[:, c], proj_ref[:, c], gqf)
        gain_sum = gain_sum + term
    held[0, 2:3, 0:128] = gain_sum
    turn(gb, turned_b)
    outer(3, 0, turned_b, mix_ref[...])
    outer(3, 512, turned_a, gqkv[:, 0:512])
    dtot[...] = kv[ctx].astype(F32)
    for j in range(1, 8):
        @pl.when(j > ctx)
        def _():
            pltpu.make_async_copy(dkv_recv.at[j], dkv_recv.at[j], dkr.at[j]).wait()
            dtot[...] += dkv_recv[j].astype(F32)
    gain_sum = jnp.zeros((1, 128), F32)
    for h in range(2):
        c = slice(h * 128, (h + 1) * 128)
        gqkv[:, 512 + h * 128:640 + h * 128], term = through_norm(
            dtot[:, c], proj_ref[:, 512 + h * 128:640 + h * 128], gkf)
        gain_sum = gain_sum + term
    held[0, 2:3, 128:256] = gain_sum
    gqkv[:, 768:1024] = dtot[:, 256:512].astype(BF)

    sum1 = TensorSum(me, gn2, low_a, core_a, sx_a, rx_a, ts1, chunks)
    sum2.finish()
    sumf.finish()
    for j in range(chunks):
        r = slice(j * 512, (j + 1) * 512)
        value = dot_nt(gqkv[:, 0:256], wgb[0, r, :]) + dot_nt(gqkv[:, 256:512], wgb[1, r, :])
        value = value + dot_nt(gqkv[:, 512:768], wub[0, r, :]) + dot_nt(gqkv[:, 768:1024], wub[1, r, :])
        sum1.put(j, value)
        if j:
            sum1.send_on(j - 1)
    sum1.send_on(chunks - 1)
    outer(3, 1024, turned_a, gqkv[:, 512:1024])
    ws.start(3)
    xo = x_own[...].astype(F32)
    inv1 = lax.rsqrt(jnp.mean(xo * xo, axis=-1, keepdims=True) + EPSILON)
    hat1 = xo * inv1
    for j in range(chunks):
        gn2[0:64, sum1.cols(j)] = sum1.take(j)
    grad = gn2[0:64, :]
    held[0, 0:1, :] = jnp.sum(grad * hat1, axis=0, keepdims=True)
    gains = GainSum(me, held, grecv, gsem)
    gains.start()
    u = grad * gain1[...].astype(F32)
    tok_ref[own, :] = (gmid[...] + inv1 * (u - hat1 * jnp.mean(u * hat1, axis=-1, keepdims=True))).astype(BF)
    gather_t = TensorGather(me, tok_ref, tgt)
    gather_t.start()
    ws.advance(0, 0)
    gather_t.forward()
    order = [(b, s) for w in range(8) for b in range(4) for s in [w - b] if 0 <= s < 5 and (b, s) != (0, 0)]
    for i, (b, s) in enumerate(order):
        ws.advance(b, s)
        if i < 7:
            gains.advance(i)
    gains_ref[...] = held[7]
    gather_o.finish()
    gather_t.finish()
    gains.finish()
    sum1.finish()
    for j in range(7):
        @pl.when(j < ctx)
        def _():
            dkv_copy(j).wait_send()
    ws.finish()


def back(n1, n2, mid, q, kv, p, mix, proj, g, x, gain1, gain2, qg, kg, wq, wk, wv, wo, wg, wu, wd):
    cos_t, sin_t = rope_constants()
    V = pl.BlockSpec(memory_space=pltpu.VMEM)
    A = pl.BlockSpec(memory_space=pl.ANY)
    S = jax.ShapeDtypeStruct
    D = pltpu.SemaphoreType.DMA
    M = pltpu.VMEM
    return pl.pallas_call(
        back_kernel,
        out_shape=(S((256, 2048), BF), S((256, 2048), BF), S((8, 2048), F32),
                   S((64, 1536), F32), S((64, 1536), F32), S((64, 1536), F32), S((64, 512), F32), S((64, 512), F32),
                   S((64, 256), F32), S((64, 256), F32), S((4, 4, 1024, 384), BF), S((4, 4, 512, 384), BF),
                   S((4, 4, 256, 384), BF)),
        in_specs=[V, V, V, V, A, V, V, V, V, A, V, V, V, V] + [A] * 9,
        out_specs=(V,) * 10 + (A, A, A),
        scratch_shapes=[
            M((4, 4, 2048, 384), BF), M((4, 4, 128, 384), BF), M((4, 4, 64, 384), BF),
            M((2, 1024, 384), BF), M((2048, 256), BF), M((2048, 256), BF),
            M((2, 2048, 256), BF), M((2, 2048, 256), BF), M((2, 256, 2048), BF),
            M((256, 2048), F32), M((256, 2048), F32), M((256, 2048), BF),
            M((2, 64, 2048), BF), M((2, 64, 2048), BF), M((64, 2048), BF), M((64, 2048), BF),
            M((64, 2048), BF), M((64, 2048), BF), M((256, 2048), BF), M((64, 2048), F32),
            M((8, 256, 512), BF), M((8, 256, 512), BF), M((256, 1024), BF),
            M((64, 2048), BF), M((128, 128), F32), M((128, 128), F32), M((8, 8, 2048), F32), M((7, 8, 2048), F32),
            D((2, 3)), D((4,)), D((4, 4, 5)), D((4, 4, 5)), D((2,)), D((3, 4, 2)), D((3, 4, 2)), D((3, 4, 2)),
            D((3, 2, 2)), D((3, 2, 2)), D((3, 2, 2)), D((8,)), D((8,)), D((7, 2))],
        compiler_params=pltpu.CompilerParams(collective_id=3, has_side_effects=True, vmem_limit_bytes=63 * 2**20),
    )(n1, n2, mid, q, kv, p, mix, proj, g, x, gain1.reshape(1, -1), gain2.reshape(1, -1), qg.reshape(1, -1),
      kg.reshape(1, -1), wq, wk, wv, wo, wg, wu, wd, jnp.asarray(cos_t), jnp.asarray(sin_t))


def local(tokens, attn_gain, w_query, w_key, w_value, query_gain, key_gain, w_out, mlp_gain, w_gate, w_up, w_down, out_grad):
    x = tokens.reshape(256, 2048)
    n1, n2, mid, q, kv, p, mix, proj = front(x, attn_gain, w_query, w_key, w_value, query_gain, key_gain, w_out, mlp_gain)
    block, tok, gains, down, gate, up, out, qq, kk, vv, *_ = back(
        n1, n2, mid, q, kv, p, mix, proj, out_grad.reshape(256, 2048), x, attn_gain, mlp_gain, query_gain, key_gain,
        w_query, w_key, w_value, w_out, w_gate, w_up, w_down)
    return (block.reshape(2, 128, 2048), tok.reshape(2, 128, 2048), gains[0], qq, kk, vv, gains[2, :128], gains[2, 128:256],
            out.T, gains[1], gate, up, down.T)


def solution(mesh):
    in_specs = (
        P("dp", "context", None),
        P(),
        P(None, "tensor"),
        P(None, "tensor"),
        P(None, "tensor"),
        P(),
        P(),
        P("tensor", None),
        P(),
        P(None, "tensor"),
        P(None, "tensor"),
        P("tensor", None),
        P("dp", "context", None),
    )
    out_specs = (
        P("dp", "context", None),
        P("dp", "context", None),
        P(),
        P(("dp", "context"), "tensor"),
        P(("dp", "context"), "tensor"),
        P(("dp", "context"), "tensor"),
        P(),
        P(),
        P("tensor", ("dp", "context")),
        P(),
        P(("dp", "context"), "tensor"),
        P(("dp", "context"), "tensor"),
        P("tensor", ("dp", "context")),
    )
    return jax.shard_map(local, mesh=mesh, in_specs=in_specs, out_specs=out_specs, check_vma=False)
```

```python
import numpy as np
import jax
import jax.numpy as jnp
from jax import lax
from jax.experimental import pallas as pl
from jax.experimental.pallas import tpu as pltpu
from jax.sharding import PartitionSpec as P

MESH = pl.DeviceIdType.MESH
BF = jnp.bfloat16
F32 = jnp.float32
EPSILON = 1e-06
ROPE_BASE = 1000000.0
SCALE = 128 ** (-0.5)


def me_place():
    c = lax.axis_index("context")
    return (lax.axis_index("dp"), c // 2, c % 2, lax.axis_index("tensor"))


def dev(place):
    y, z, h, t = place
    return (y, z * 2 + h, t)


def flip4(v, which):
    return v + 1 - 2 * (v % 2) if which == "0" else 3 - v


def pair_bit(y):
    return ((y + 1) // 2) % 2


def partner(place, dim):
    y, z, h, t = place
    if dim == "core":
        return (y, z, h, t + 1 - 2 * (t % 2))
    if dim == "xl":
        return (y, z, h, (t + 2) % 4)
    if dim == "xh":
        return (y, z, 1 - h, t)
    if dim[0] == "y":
        return (flip4(y, dim[1]), z, h, t)
    return (y, flip4(z, dim[1]), h, t)


def dot(a, b):
    return jnp.dot(a, b, preferred_element_type=F32)


def dot_nt(a, b):
    return lax.dot_general(a, b, (((1,), (1,)), ((), ())), preferred_element_type=F32)


def dot_tn(a, b):
    return lax.dot_general(a, b, (((0,), (0,)), ((), ())), preferred_element_type=F32)


def row_of(ref):
    return ref[...].astype(F32).reshape(1, -1)


def rows_at(start, n):
    return pl.ds(pl.multiple_of(start, 64), n)


def remote(src, dst, send_sem, recv_sem, place):
    return pltpu.make_async_remote_copy(src_ref=src, dst_ref=dst, send_sem=send_sem, recv_sem=recv_sem,
                                        device_id=dev(place), device_id_type=MESH)


def wait_bytes(view, sem):
    pltpu.make_async_copy(view, view, sem).wait()


def subsets(dims, place):
    found = [place]
    for dim in dims:
        found = found + [partner(p, dim) for p in found]
    return found


class GroupSum:
    CHUNKS = 4
    WIDTH = 512

    def __init__(self, me, low, recvs, sems, wide):
        self.me, self.low, self.recvs, self.sems, self.wide = me, low, recvs, sems, wide

    def cols(self, j):
        return pl.ds(j * self.WIDTH, self.WIDTH)

    def row(self, place):
        y, _, _, t = place
        return rows_at(pair_bit(y) * 256 + t * 64 if self.wide else t * 64, 64)

    def order(self, j):
        if not self.wide:
            return ("core", "xl")
        return ("core", "xl", "y0") if j < self.CHUNKS // 2 else ("core", "y0", "xl")

    def copies(self, j, s):
        dims = self.order(j)
        to = partner(self.me, dims[s])
        return [remote(self.low.at[self.row(block), self.cols(j)], self.recvs[s].at[i, :, self.cols(j)],
                       self.sems.at[s, j, i, 0], self.sems.at[s, j, i, 1], to)
                for i, block in enumerate(subsets(dims[s + 1:], to))]

    def send(self, j, s):
        for cp in self.copies(j, s):
            cp.start()

    def put(self, j, value):
        self.low[:, self.cols(j)] = value.astype(BF)
        self.send(j, 0)

    def step(self, j, s):
        dims = self.order(j)
        for cp in self.copies(j, s):
            cp.wait_recv()
        for i, block in enumerate(subsets(dims[s + 1:], self.me)):
            r = self.row(block)
            v = self.low[r, self.cols(j)].astype(F32) + self.recvs[s][i, :, self.cols(j)].astype(F32)
            if s == len(dims) - 1:
                return v
            self.low[r, self.cols(j)] = v.astype(BF)
        self.send(j, s + 1)

    def steps(self, s):
        for j in range(self.CHUNKS):
            self.step(j, s)

    def finish(self):
        for j in range(self.CHUNKS):
            for s in range(len(self.order(j))):
                for cp in self.copies(j, s):
                    cp.wait_send()


class TensorGather:
    def __init__(self, me, full, sems, chunks=2):
        self.me, self.full, self.sems, self.chunks = me, full, sems, chunks
        self.width = 2048 // chunks

    def copy(self, kind, j):
        t = self.me[3]
        row = (t + 2) % 4 if kind == 2 else t
        view = self.full.at[rows_at(row * 64, 64), pl.ds(j * self.width, self.width)]
        return remote(view, view, self.sems.at[kind, j, 0], self.sems.at[kind, j, 1],
                      partner(self.me, "xl" if kind == 0 else "core"))

    def start(self):
        for j in range(self.chunks):
            self.copy(0, j).start()
        for j in range(self.chunks):
            self.copy(1, j).start()

    def forward(self):
        for j in range(self.chunks):
            self.copy(0, j).wait_recv()
            self.copy(2, j).start()

    def finish(self):
        for j in range(self.chunks):
            self.copy(1, j).wait_recv()
            self.copy(2, j).wait_recv()
            for kind in range(3):
                self.copy(kind, j).wait_send()


class PairGather:
    MOVES = (((), "xl", 0, 2048), ((), "y0", 0, 2048), ((), "core", 0, 2048),
             (("y0",), "xl", 0, 1024), (("xl",), "y0", 1024, 1024),
             (("y0",), "core", 0, 2048), (("xl",), "core", 0, 2048),
             (("xl", "y0"), "core", 0, 1024), (("xl", "y0"), "core", 1024, 1024))

    def __init__(self, me, full, sems):
        self.me, self.full, self.sems = me, full, sems

    def copy(self, i):
        via, dim, col, width = self.MOVES[i]
        block = self.me
        for d in via:
            block = partner(block, d)
        view = self.full.at[rows_at(pair_bit(block[0]) * 256 + block[3] * 64, 64), pl.ds(col, width)]
        return remote(view, view, self.sems.at[i, 0], self.sems.at[i, 1], partner(self.me, dim))

    def run(self):
        for i in (0, 1, 2):
            self.copy(i).start()
        self.copy(1).wait_recv()
        self.copy(3).start()
        self.copy(5).start()
        self.copy(0).wait_recv()
        self.copy(4).start()
        self.copy(6).start()
        self.copy(3).wait_recv()
        self.copy(7).start()
        self.copy(4).wait_recv()
        self.copy(8).start()
        for i in (2, 5, 6, 7, 8):
            self.copy(i).wait_recv()

    def finish(self):
        for i in range(9):
            self.copy(i).wait_send()


def owner_runs(base, remaining):
    y, z, h, _ = base

    def ring(v, axis):
        both = (axis + "0" in remaining, axis + "1" in remaining)
        if all(both):
            return None
        if both[0]:
            return [v, flip4(v, "0")]
        if both[1]:
            return [v, flip4(v, "1")]
        return [v]

    ys, zs = ring(y, "y"), ring(z, "z")
    found = []
    for yy in [0, 1, 2, 3] if ys is None else ys:
        if zs is None:
            found.append((yy * 512, 512))
            continue
        for zz in zs:
            if "xh" in remaining:
                found.append((yy * 512 + zz * 128, 128))
            else:
                found.append((yy * 512 + zz * 128 + h * 64, 64))
    return found


class Piece:
    def __init__(self, me, acc, order, keep, recvs, ssem, rsem, emit, stage=None, lsem=None):
        self.me, self.acc, self.order, self.keep, self.recvs = me, acc, order, keep, recvs
        self.ssem, self.rsem, self.emit, self.stage, self.lsem = ssem, rsem, emit, stage, lsem

    def rest(self, s):
        return self.order[s + 1:] + self.keep

    def send(self, s):
        to, off = partner(self.me, self.order[s]), 0
        for row, n in owner_runs(to, self.rest(s)):
            remote(self.acc(rows_at(row, n)), self.recvs[s].at[pl.ds(off, n)], self.ssem.at[s], self.rsem.at[s], to).start()
            off += n

    def arrived(self, s):
        wait_bytes(self.recvs[s], self.rsem.at[s])

    def load(self, s):
        return pltpu.make_async_copy(self.recvs[s], self.stage.at[pl.ds(0, 1024 >> s)], self.lsem)

    def add(self, s):
        view = self.recvs[s]
        if s < 2 and self.stage is not None:
            view = self.stage
        off = 0
        for i, (row, n) in enumerate(owner_runs(self.me, self.rest(s))):
            step = min(n, 128)

            def body(m, _, row=row, off=off, step=step, i=i):
                acc = self.acc(rows_at(row + m * step, step))
                v = acc[...].astype(F32) + view[pl.ds(pl.multiple_of(off + m * step, 64), step), :].astype(F32)
                if s == len(self.order) - 1:
                    self.emit(i, v)
                else:
                    acc[...] = v.astype(BF)
                return 0

            if n == step:
                body(0, 0)
            else:
                lax.fori_loop(0, n // step, body, 0)
            off += n
        if s < len(self.order) - 1:
            self.send(s + 1)

    def finish(self):
        for s in range(len(self.order)):
            wait_bytes(self.recvs[s], self.ssem.at[s])


def advance(pieces, s):
    if s < 2 and pieces[0].stage is not None:
        pieces[0].arrived(s)
        pieces[0].load(s).start()
        for i, piece in enumerate(pieces):
            if i + 1 < len(pieces):
                pieces[i + 1].arrived(s)
                pieces[i + 1].load(s).start()
            piece.load(s).wait()
            piece.add(s)
        return
    for piece in pieces:
        piece.arrived(s)
        piece.add(s)


GAIN_DIMS = ("core", "xl", "xh", "y0", "z0", "y1", "z1")


class GainSum:
    def __init__(self, me, held, recv, sems):
        self.me, self.held, self.recv, self.sems = me, held, recv, sems

    def copy(self, i):
        return remote(self.held.at[i], self.recv.at[i], self.sems.at[i, 0], self.sems.at[i, 1],
                      partner(self.me, GAIN_DIMS[i]))

    def start(self):
        self.copy(0).start()

    def advance(self, i):
        self.copy(i).wait_recv()
        self.held[i + 1] = self.held[i] + self.recv[i]
        if i < 6:
            self.copy(i + 1).start()

    def finish(self):
        for i in range(7):
            self.copy(i).wait_send()


def rope_constants():
    frequency = np.float32(ROPE_BASE) ** (-np.arange(0, 128, 2).astype(np.float32) / np.float32(128))
    angles = np.arange(1024, dtype=np.float32)[:, None] * frequency.astype(np.float32)[None, :]
    cosine, sine = np.cos(angles), np.sin(angles)
    return (np.concatenate([cosine, cosine], 1).astype(np.float32),
            np.concatenate([-sine, sine], 1).astype(np.float32))


def half_turn(v):
    return pltpu.roll(v, 64, axis=1)


MLP_ORDERS = (("y1", "z0", "z1", "xh"), ("z0", "z1", "y1", "xh"), ("z1", "y1", "z0", "xh"))
ATT_ORDERS = (("y0", "z0", "y1", "z1", "xh"), ("z0", "y1", "z1", "y0", "xh"),
              ("y1", "z1", "y0", "z0", "xh"), ("z1", "y0", "z0", "y1", "xh"))


def layer_kernel(x_h, g_h, gain1, gain2, qg, kg, wq_h, wk_h, wv_h, wo_h, wg_h, wu_h, wd_h, cos_h, sin_h,
                 block_ref, tok_ref, gains_ref, down_o, gate_o, up_o, out_o, q_o, k_o, v_o, p_h, mrecv0, mrecv1, dkv_recv,
                 x, n1, n2, g2, wq, wk, wv, wo, wgt, wut, wdt, low_a, low_b, ra1, ra2, ra3, rb1, rb2, rb3, hidden,
                 kv, q_ref, mix, proj, gqkv, dq, mid_ref, gmid, x_own, cosv, sinv,
                 macc, mrecv2, mrecv3, stage, xsend, xrecv,
                 areca0, areca1, areca2, areca3, areca4, arecb0, arecb1, arecb2, arecb3, arecb4, held, grecv,
                 lsem, psem, kvs, kvr, s_out, s_n2, s_gn2, s_feed, s_gb, s_blk, s_gn1, s_tok, g_sem,
                 mss, mrs, stsem, xs, ass, ars, bss, brs, dks, dkr, dkl, gsem):
    me = me_place()
    ctx = lax.axis_index("context")
    pair = pair_bit(me[0])
    own = rows_at(me[3] * 64, 64)
    own_wide = rows_at(pair * 256 + me[3] * 64, 64)
    mine = rows_at(pair * 256, 256)
    half = pl.multiple_of(pair * 768, 256)

    def load(i, src, dst):
        return pltpu.make_async_copy(src, dst, lsem.at[i])

    first = [load(0, x_h, x), load(1, wk_h, wk), load(2, wv_h, wv),
             load(3, cos_h.at[rows_at(ctx * 128, 128)], cosv), load(4, sin_h.at[rows_at(ctx * 128, 128)], sinv),
             load(5, wq_h, wq), load(6, g_h, g2.at[mine]), load(7, wo_h, wo)]
    down_load = load(8, wd_h.at[pl.ds(half, 768)], wdt)
    tiles = []
    for i in range(3):
        c = pl.ds(pl.multiple_of(half + i * 256, 256), 256)
        tiles.append((load(9 + i, wg_h.at[:, c], wgt.at[i]), load(12 + i, wu_h.at[:, c], wut.at[i])))
    for cp in first:
        cp.start()
    bar = pltpu.get_barrier_semaphore()
    for d in range(1, 8):
        pl.semaphore_signal(bar, inc=1, device_id=(me[0], (ctx + d) % 8, me[3]), device_id_type=MESH)
    for d in ("core", "xl", "y0", "y1"):
        pl.semaphore_signal(bar, inc=1, device_id=dev(partner(me, d)), device_id_type=MESH)

    first[0].wait()
    g1 = row_of(gain1)

    def norm_rows(i, _):
        r = pl.ds(pl.multiple_of(i * 32, 32), 32)
        xv = x[r, :].astype(F32)
        inv = lax.rsqrt(jnp.mean(xv * xv, axis=-1, keepdims=True) + EPSILON)
        n1[r, :] = (xv * inv * g1).astype(BF)
        return 0

    lax.fori_loop(0, 8, norm_rows, 0)
    x_own[...] = x[own, :]
    for i in (1, 2, 3, 4):
        first[i].wait()
    cos2 = jnp.concatenate([cosv[...], cosv[...]], axis=0)
    sin2 = jnp.concatenate([sinv[...], sinv[...]], axis=0)
    gqf, gkf = row_of(qg), row_of(kg)

    def turned(v, gain):
        hat = v * lax.rsqrt(jnp.mean(v * v, axis=-1, keepdims=True) + EPSILON) * gain
        return (hat * cos2 + half_turn(hat) * sin2).astype(BF)

    kp = dot(n1[...], wk[...])
    proj[:, 512:768] = kp
    kv[ctx, :, 256:512] = dot(n1[...], wv[...]).astype(BF)
    for h in range(2):
        kv[ctx, :, h * 128:(h + 1) * 128] = turned(kp[:, h * 128:(h + 1) * 128], gkf)
    pl.semaphore_wait(bar, 11)

    def kv_copy(d):
        return pltpu.make_async_remote_copy(
            src_ref=kv.at[ctx], dst_ref=kv.at[ctx], send_sem=kvs.at[d], recv_sem=kvr.at[ctx],
            device_id=(me[0], (ctx + d) % 8, me[3]), device_id_type=MESH)

    for d in range(1, 8):
        @pl.when(ctx + d < 8)
        def _():
            kv_copy(d).start()

    first[6].wait()
    g_copy = remote(g2.at[mine], g2.at[mine], g_sem.at[0], g_sem.at[1], partner(me, "y0"))
    g_copy.start()
    down_load.start()
    for pair_loads in tiles:
        for cp in pair_loads:
            cp.start()

    for j in range(1, 8):
        @pl.when(j > ctx)
        def _():
            kv[j] = jnp.zeros((256, 512), BF)

    first[5].wait()
    qp = dot(n1[...], wq[...])
    proj[:, 0:512] = qp
    for h in range(4):
        rot = turned(qp[:, h * 128:(h + 1) * 128], gqf)
        for s in range(2):
            q_ref[s, h // 2, (h % 2) * 128:(h % 2 + 1) * 128, :] = rot[s * 128:(s + 1) * 128]
    first[7].wait()
    for j in range(7):
        @pl.when(j < ctx)
        def _():
            wait_bytes(kv.at[j], kvr.at[j])

    def head_views(s, kh):
        r = slice(s * 128, (s + 1) * 128)
        return ((slice(None), r, slice(kh * 128, (kh + 1) * 128)),
                (slice(None), r, slice(256 + kh * 128, 256 + (kh + 1) * 128)))

    place = lax.broadcasted_iota(jnp.int32, (256, 1024), 0) % 128 + ctx * 128
    allowed = place >= lax.broadcasted_iota(jnp.int32, (256, 1024), 1)
    for s in range(2):
        for kh in range(2):
            ks, vs = head_views(s, kh)
            scores = jnp.where(allowed, dot_nt(q_ref[s, kh], kv[ks].reshape(1024, 128)) * SCALE, -1e30)
            top = jnp.max(scores, axis=-1, keepdims=True)
            e = jnp.exp(scores - top)
            prob = (e / jnp.sum(e, axis=-1, keepdims=True)).astype(BF)
            for b in range(4):
                hidden[s * 4 + kh * 2 + b // 2, (b % 2) * 256:(b % 2 + 1) * 256, :] = prob[:, b * 256:(b + 1) * 256]
            mixed = dot(prob, kv[vs].reshape(1024, 128)).astype(BF)
            for g in range(2):
                h = kh * 2 + g
                mix[s * 128:(s + 1) * 128, h * 128:(h + 1) * 128] = mixed[g * 128:(g + 1) * 128]
    p_out = pltpu.make_async_copy(hidden.at[pl.ds(0, 8)], p_h, psem.at[0])
    p_out.start()

    four = range(4)
    sum_o = GroupSum(me, low_a.at[0:256], (ra1, ra2), s_out, False)
    for j in four:
        sum_o.put(j, dot(mix[...], wo[:, sum_o.cols(j)]))
    sum_o.steps(0)
    g_copy.wait_recv()
    down_load.wait()
    p_out.wait()
    for i in range(3):
        hidden[6 + i] = dot_nt(g2[...], wdt[i * 256:(i + 1) * 256, :]).astype(BF)
    for j in four:
        mid_ref[:, sum_o.cols(j)] = x_own[:, sum_o.cols(j)].astype(F32) + sum_o.step(j, 1)
    mid = mid_ref[...]
    inv2 = lax.rsqrt(jnp.mean(mid * mid, axis=-1, keepdims=True) + EPSILON)
    n2[own_wide, :] = (mid * inv2 * row_of(gain2)).astype(BF)
    gather_n = PairGather(me, n2, s_n2)
    gather_n.run()
    sum_o.finish()

    for i in range(3):
        for cp in tiles[i]:
            cp.wait()
        gate = dot(n2[...], wgt[i])
        up = dot(n2[...], wut[i])
        gh = hidden[6 + i].astype(F32)
        sig = 1.0 / (1.0 + jnp.exp(-gate))
        silu = gate * sig
        hidden[i] = (silu * up).astype(BF)
        hidden[3 + i] = (gh * up * sig * (1.0 + gate * (1.0 - sig))).astype(BF)
        hidden[6 + i] = (gh * silu).astype(BF)
    sum2 = GroupSum(me, low_a, (ra1, ra2, ra3), s_gn2, True)
    sumf = GroupSum(me, low_b, (rb1, rb2, rb3), s_feed, True)
    for j in four:
        r = slice(j * 512, (j + 1) * 512)
        v = dot_nt(hidden[3], wgt[0, r, :]) + dot_nt(hidden[6], wut[0, r, :])
        for i in (1, 2):
            v = v + dot_nt(hidden[3 + i], wgt[i, r, :]) + dot_nt(hidden[6 + i], wut[i, r, :])
        sum2.put(j, v)
    for j in four:
        c = slice(j * 512, (j + 1) * 512)
        v = dot(hidden[0], wdt[0:256, c])
        for i in (1, 2):
            v = v + dot(hidden[i], wdt[i * 256:(i + 1) * 256, c])
        sumf.put(j, v)
        sum2.step(j, 0)

    mlp = []
    for i in range(3):
        for k in range(3):
            n = i * 3 + k
            out = (down_o, gate_o, up_o)[k]

            def emit(m, v, out=out, i=i, n=n):
                if m == 0:
                    out[pair, :, i * 256:(i + 1) * 256] = v
                else:
                    xsend[n] = v.astype(BF)

            mlp.append(Piece(me, lambda r, n=n: macc.at[n, r], MLP_ORDERS[k], ("y0",),
                             (mrecv0.at[n], mrecv1.at[n], mrecv2.at[n], mrecv3.at[n]), mss.at[n], mrs.at[n], emit,
                             stage.at[n % 2], stsem.at[n % 2]))
    for j in four:
        c = slice(j * 512, (j + 1) * 512)
        gt = g2[:, c].T
        nt = n2[:, c].T
        for i in range(3):
            macc[i * 3, c, :] = dot(gt, hidden[i]).astype(BF)
        for i in range(3):
            macc[i * 3 + 1, c, :] = dot(nt, hidden[3 + i]).astype(BF)
            macc[i * 3 + 2, c, :] = dot(nt, hidden[6 + i]).astype(BF)
        sum2.step(j, 1)
    for piece in mlp:
        piece.send(0)
    p_in = pltpu.make_async_copy(p_h, hidden.at[pl.ds(0, 8)], psem.at[1])
    p_in.start()

    hat2 = mid_ref[...] * inv2
    for j in four:
        gmid[:, sum2.cols(j)] = sum2.step(j, 2)
    grad = gmid[...]
    held[0] = jnp.zeros((8, 2048), F32)
    held[0, 1:2, :] = jnp.sum(grad * hat2, axis=0, keepdims=True)
    u = grad * row_of(gain2)
    grad = g2[own_wide, :].astype(F32) + inv2 * (u - hat2 * jnp.mean(u * hat2, axis=-1, keepdims=True))
    gmid[...] = grad
    gb = x
    gb[own, :] = grad.astype(BF)
    gather_b = TensorGather(me, gb, s_gb)
    gather_b.start()
    sumf.steps(0)
    gather_b.forward()
    sumf.steps(1)
    gather_b.finish()

    gmix = [dot_nt(gb[...], wo[b * 256:(b + 1) * 256, :]).astype(BF) for b in range(2)]
    for d in range(1, 8):
        @pl.when(ctx + d < 8)
        def _():
            kv_copy(d).wait_send()
    p_in.wait()
    for s in range(2):
        for kh in range(2):
            ks, vs = head_views(s, kh)
            keys = kv[ks].reshape(1024, 128)
            values = kv[vs].reshape(1024, 128)
            both = gmix[kh][s * 128:(s + 1) * 128]
            gm = jnp.concatenate([both[:, :128], both[:, 128:]], axis=0)
            prob = jnp.concatenate(
                [hidden[s * 4 + kh * 2 + b // 2, (b % 2) * 256:(b % 2 + 1) * 256, :] for b in range(4)], axis=1)
            gp = dot_nt(gm, values)
            prob32 = prob.astype(F32)
            inner = jnp.sum(prob32 * gp, axis=-1, keepdims=True)
            gs = (prob32 * (gp - inner)).astype(BF)
            gq = dot(gs, keys) * SCALE
            for g in range(2):
                h = kh * 2 + g
                dq[s * 128:(s + 1) * 128, h * 128:(h + 1) * 128] = gq[g * 128:(g + 1) * 128]
            kv[ks] = (dot_tn(gs, q_ref[s, kh]) * SCALE).astype(BF).reshape(8, 128, 128)
            kv[vs] = dot_tn(prob, gm).astype(BF).reshape(8, 128, 128)

    def dkv_copy(j):
        return pltpu.make_async_remote_copy(
            src_ref=kv.at[j], dst_ref=dkv_recv.at[ctx], send_sem=dks.at[j], recv_sem=dkr.at[ctx],
            device_id=(me[0], j, me[3]), device_id_type=MESH)

    for j in range(7):
        @pl.when(j < ctx)
        def _():
            dkv_copy(j).start()

    for j in four:
        block_ref[own, sumf.cols(j)] = (mid_ref[:, sumf.cols(j)] + sumf.step(j, 2)).astype(BF)
    gather_o = TensorGather(me, block_ref, s_blk)
    gather_o.start()
    sumf.finish()

    def through_norm(grad_rot, pre, gain):
        grad_normed = grad_rot * cos2 - half_turn(grad_rot) * sin2
        inv = lax.rsqrt(jnp.mean(pre * pre, axis=-1, keepdims=True) + EPSILON)
        hat = pre * inv
        u = grad_normed * gain
        grad_pre = inv * (u - hat * jnp.mean(u * hat, axis=-1, keepdims=True))
        return grad_pre.astype(BF), jnp.sum(grad_normed * hat, axis=0, keepdims=True)

    gain_sum = jnp.zeros((1, 128), F32)
    for h in range(4):
        c = slice(h * 128, (h + 1) * 128)
        gqkv[:, c], term = through_norm(dq[:, c], proj[:, c], gqf)
        gain_sum = gain_sum + term
    held[0, 2:3, 0:128] = gain_sum

    att_a, att_b = [], []
    homes = [(lambda r, i=i: (wgt.at[i, r] if i < 3 else wut.at[0, r])) for i in range(4)]
    homes += [(lambda r, i=i: wut.at[1 + i // 2, r, pl.ds((i % 2) * 128, 128)]) for i in range(4)]
    for i in range(4):
        def emit_a(m, v, i=i):
            (out_o, q_o)[i // 2][:, (i % 2) * 256:(i % 2 + 1) * 256] = v

        def emit_b(m, v, i=i):
            (k_o, v_o)[i // 2][:, (i % 2) * 128:(i % 2 + 1) * 128] = v

        att_a.append(Piece(me, homes[i], ATT_ORDERS[i], (), tuple(r.at[i] for r in (areca0, areca1, areca2, areca3, areca4)),
                           ass.at[i], ars.at[i], emit_a))
        att_b.append(Piece(me, homes[4 + i], ATT_ORDERS[i], (), tuple(r.at[i] for r in (arecb0, arecb1, arecb2, arecb3, arecb4)),
                           bss.at[i], brs.at[i], emit_b))
    for j in four:
        c = slice(j * 512, (j + 1) * 512)
        gt = gb[:, c].T
        nt = n1[:, c].T
        v = dot(gt, mix[...]).astype(BF)
        wgt[0, c, :] = v[:, 0:256]
        wgt[1, c, :] = v[:, 256:512]
        v = dot(nt, gqkv[:, 0:512]).astype(BF)
        wgt[2, c, :] = v[:, 0:256]
        wut[0, c, :] = v[:, 256:512]
    for piece in att_a:
        piece.send(0)
    gather_o.forward()

    dtot = dq

    def late(j):
        return pltpu.make_async_copy(dkv_recv.at[j], low_b.at[rows_at((j // 4) * 256, 256), pl.ds((j % 4) * 512, 512)],
                                     dkl.at[j])

    for j in range(7, 0, -1):
        @pl.when(j > ctx)
        def _():
            wait_bytes(dkv_recv.at[j], dkr.at[j])
            late(j).start()
    dtot[...] = kv[ctx].astype(F32)
    for j in range(7, 0, -1):
        @pl.when(j > ctx)
        def _():
            late(j).wait()
            dtot[...] += low_b[(j // 4) * 256:(j // 4 + 1) * 256, (j % 4) * 512:(j % 4 + 1) * 512].astype(F32)
    gain_sum = jnp.zeros((1, 128), F32)
    for h in range(2):
        c = slice(h * 128, (h + 1) * 128)
        gqkv[:, 512 + h * 128:640 + h * 128], term = through_norm(dtot[:, c], proj[:, 512 + h * 128:640 + h * 128], gkf)
        gain_sum = gain_sum + term
    held[0, 2:3, 128:256] = gain_sum
    gqkv[:, 768:1024] = dtot[:, 256:512].astype(BF)

    sum2.finish()
    sum1 = GroupSum(me, low_a.at[0:256], (ra1, ra2), s_gn1, False)
    for j in four:
        r = slice(j * 512, (j + 1) * 512)
        v = dot_nt(gqkv[:, 0:512], wq[r, :]) + dot_nt(gqkv[:, 512:768], wk[r, :]) + dot_nt(gqkv[:, 768:1024], wv[r, :])
        sum1.put(j, v)
    for j in four:
        c = slice(j * 512, (j + 1) * 512)
        v = dot(n1[:, c].T, gqkv[:, 512:1024]).astype(BF)
        wut[1, c, :] = v[:, 0:256]
        wut[2, c, :] = v[:, 256:512]
        sum1.step(j, 0)
    for piece in att_b:
        piece.send(0)
    advance(mlp, 0)
    xo = x_own[...].astype(F32)
    inv1 = lax.rsqrt(jnp.mean(xo * xo, axis=-1, keepdims=True) + EPSILON)
    hat1 = xo * inv1
    for j in four:
        mid_ref[:, sum1.cols(j)] = sum1.step(j, 1)
    grad = mid_ref[...]
    held[0, 0:1, :] = jnp.sum(grad * hat1, axis=0, keepdims=True)
    gains = GainSum(me, held, grecv, gsem)
    gains.start()
    u = grad * row_of(gain1)
    tok_ref[own, :] = (gmid[...] + inv1 * (u - hat1 * jnp.mean(u * hat1, axis=-1, keepdims=True))).astype(BF)
    gather_t = TensorGather(me, tok_ref, s_tok)
    gather_t.start()
    advance(att_a, 0)
    gains.advance(0)
    advance(mlp, 1)
    gather_t.forward()
    gains.advance(1)
    advance(att_a, 1)
    advance(att_b, 0)
    gains.advance(2)
    advance(mlp, 2)
    advance(att_b, 1)
    gains.advance(3)
    advance(att_a, 2)
    advance(mlp, 3)
    swap = [remote(xsend.at[n], xrecv.at[n], xs.at[n, 0], xs.at[n, 1], partner(me, "y0")) for n in range(9)]
    for cp in swap:
        cp.start()
    advance(att_b, 2)
    gains.advance(4)
    advance(att_a, 3)
    advance(att_b, 3)
    gains.advance(5)
    advance(att_a, 4)
    advance(att_b, 4)
    gains.advance(6)
    gains_ref[...] = held[7]
    for n, cp in enumerate(swap):
        cp.wait_recv()
        (down_o, gate_o, up_o)[n % 3][1 - pair, :, (n // 3) * 256:(n // 3 + 1) * 256] = xrecv[n].astype(F32)

    for cp in swap:
        cp.wait_send()
    gather_o.finish()
    gather_t.finish()
    gather_n.finish()
    gains.finish()
    sum1.finish()
    g_copy.wait_send()
    for j in range(7):
        @pl.when(j < ctx)
        def _():
            dkv_copy(j).wait_send()
    for piece in mlp + att_a + att_b:
        piece.finish()


def layer(x, g, gain1, gain2, qg, kg, wq, wk, wv, wo, wg, wu, wd):
    cos_t, sin_t = rope_constants()
    V = pl.BlockSpec(memory_space=pltpu.VMEM)
    A = pl.BlockSpec(memory_space=pl.ANY)
    S = jax.ShapeDtypeStruct
    D = pltpu.SemaphoreType.DMA
    M = pltpu.VMEM
    return pl.pallas_call(
        layer_kernel,
        out_shape=(S((256, 2048), BF), S((256, 2048), BF), S((8, 2048), F32),
                   S((2, 64, 768), F32), S((2, 64, 768), F32), S((2, 64, 768), F32), S((64, 512), F32), S((64, 512), F32),
                   S((64, 256), F32), S((64, 256), F32), S((8, 512, 256), BF), S((9, 1024, 256), BF), S((9, 512, 256), BF),
                   S((8, 256, 512), BF)),
        in_specs=[A, A, V, V, V, V] + [A] * 9,
        out_specs=(V,) * 10 + (A, A, A, A),
        scratch_shapes=[
            M((256, 2048), BF), M((256, 2048), BF), M((512, 2048), BF), M((512, 2048), BF),
            M((2048, 512), BF), M((2048, 256), BF), M((2048, 256), BF), M((512, 2048), BF),
            M((3, 2048, 256), BF), M((3, 2048, 256), BF), M((768, 2048), BF),
            M((512, 2048), BF), M((512, 2048), BF),
            M((4, 64, 2048), BF), M((2, 64, 2048), BF), M((1, 64, 2048), BF),
            M((4, 64, 2048), BF), M((2, 64, 2048), BF), M((1, 64, 2048), BF), M((9, 512, 256), BF),
            M((8, 256, 512), BF), M((2, 2, 256, 128), BF), M((256, 512), BF), M((256, 768), F32),
            M((256, 1024), BF), M((256, 512), F32), M((64, 2048), F32), M((64, 2048), F32),
            M((64, 2048), BF), M((128, 128), F32), M((128, 128), F32),
            M((9, 2048, 256), BF), M((9, 256, 256), BF), M((9, 128, 256), BF),
            M((2, 1024, 256), BF), M((9, 64, 256), BF), M((9, 64, 256), BF)]
        + [M((4, 1024 >> s, 256), BF) for s in range(5)] + [M((4, 1024 >> s, 128), BF) for s in range(5)]
        + [M((8, 8, 2048), F32), M((7, 8, 2048), F32),
           D((15,)), D((2,)), D((8,)), D((8,)), D((2, 4, 2, 2)), D((9, 2)), D((3, 4, 4, 2)), D((3, 4, 4, 2)),
           D((3, 2, 2)), D((3, 2, 2)), D((2, 4, 2, 2)), D((3, 2, 2)), D((2,)),
           D((9, 4)), D((9, 4)), D((2,)), D((9, 2)), D((4, 5)), D((4, 5)), D((4, 5)), D((4, 5)), D((8,)), D((8,)),
           D((8,)), D((7, 2))],
        compiler_params=pltpu.CompilerParams(collective_id=3, has_side_effects=True, vmem_limit_bytes=63 * 2**20),
    )(x, g, gain1, gain2, qg, kg, wq, wk, wv, wo, wg, wu, wd, jnp.asarray(cos_t), jnp.asarray(sin_t))


def tail_kernel(block_h, tok_h, gains, down_h, gate_h, up_h, out_h, q_h, k_h, v_h,
                block_o, tok_o, gain1_o, q_o, k_o, v_o, qg_o, kg_o, out_o, gain2_o, gate_o, up_o, down_o, sems):
    pairs = [(block_h, block_o), (tok_h, tok_o), (q_h, q_o), (k_h, k_o), (v_h, v_o), (out_h, out_o)]
    for i in range(2):
        c = pl.ds(i * 768, 768)
        pairs += [(down_h.at[i], down_o.at[:, c]), (gate_h.at[i], gate_o.at[:, c]), (up_h.at[i], up_o.at[:, c])]
    copies = [pltpu.make_async_copy(s, d, sems.at[i]) for i, (s, d) in enumerate(pairs)]
    for cp in copies:
        cp.start()
    gain1_o[...] = gains[0, :]
    gain2_o[...] = gains[1, :]
    qg_o[...] = gains[2, 0:128]
    kg_o[...] = gains[2, 128:256]
    for cp in copies:
        cp.wait()


def tail(block, tok, gains, down, gate, up, out, q, k, v):
    V = pl.BlockSpec(memory_space=pltpu.VMEM)
    A = pl.BlockSpec(memory_space=pl.ANY)
    S = jax.ShapeDtypeStruct
    return pl.pallas_call(
        tail_kernel,
        out_shape=(S((256, 2048), BF), S((256, 2048), BF), S((2048,), F32), S((64, 512), F32), S((64, 256), F32),
                   S((64, 256), F32), S((128,), F32), S((128,), F32), S((64, 512), F32), S((2048,), F32),
                   S((64, 1536), F32), S((64, 1536), F32), S((64, 1536), F32)),
        in_specs=[A, A, V, A, A, A, A, A, A, A],
        out_specs=(V,) * 13,
        scratch_shapes=[pltpu.SemaphoreType.DMA((12,))],
        compiler_params=pltpu.CompilerParams(vmem_limit_bytes=62 * 2**20),
    )(block, tok, gains, down, gate, up, out, q, k, v)


def local(tokens, attn_gain, w_query, w_key, w_value, query_gain, key_gain, w_out, mlp_gain, w_gate, w_up, w_down, out_grad):
    results = layer(tokens.reshape(256, 2048), out_grad.reshape(256, 2048), attn_gain, mlp_gain, query_gain, key_gain,
                    w_query, w_key, w_value, w_out, w_gate, w_up, w_down)
    block, tok, g1, q, k, v, qg, kg, out, g2, gate, up, down = tail(*results[:10])
    return (block.reshape(2, 128, 2048), tok.reshape(2, 128, 2048), g1, q, k, v, qg, kg, out.T, g2, gate, up, down.T)


def solution(mesh):
    in_specs = (
        P("dp", "context", None),
        P(),
        P(None, "tensor"),
        P(None, "tensor"),
        P(None, "tensor"),
        P(),
        P(),
        P("tensor", None),
        P(),
        P(None, "tensor"),
        P(None, "tensor"),
        P("tensor", None),
        P("dp", "context", None),
    )
    out_specs = (
        P("dp", "context", None),
        P("dp", "context", None),
        P(),
        P(("dp", "context"), "tensor"),
        P(("dp", "context"), "tensor"),
        P(("dp", "context"), "tensor"),
        P(),
        P(),
        P("tensor", ("dp", "context")),
        P(),
        P(("dp", "context"), "tensor"),
        P(("dp", "context"), "tensor"),
        P("tensor", ("dp", "context")),
    )
    return jax.shard_map(local, mesh=mesh, in_specs=in_specs, out_specs=out_specs, check_vma=False)
```

```python
import numpy as np
import jax
import jax.numpy as jnp
from jax import lax
from jax.experimental import pallas as pl
from jax.experimental.pallas import tpu as pltpu
from jax.sharding import PartitionSpec as P

MESH = pl.DeviceIdType.MESH
BF = jnp.bfloat16
F32 = jnp.float32
EPSILON = 1e-06
ROPE_BASE = 1000000.0
SCALE = 128 ** (-0.5)


def me_place():
    c = lax.axis_index("context")
    return (lax.axis_index("dp"), c // 2, c % 2, lax.axis_index("tensor"))


def dev(place):
    y, z, h, t = place
    return (y, z * 2 + h, t)


def flip4(v, which):
    return v + 1 - 2 * (v % 2) if which == "0" else 3 - v


def pair_bit(y):
    return ((y + 1) // 2) % 2


def partner(place, dim):
    y, z, h, t = place
    if dim == "core":
        return (y, z, h, t + 1 - 2 * (t % 2))
    if dim == "xl":
        return (y, z, h, (t + 2) % 4)
    if dim == "xh":
        return (y, z, 1 - h, t)
    if dim[0] == "y":
        return (flip4(y, dim[1]), z, h, t)
    return (y, flip4(z, dim[1]), h, t)


def dot(a, b):
    return jnp.dot(a, b, preferred_element_type=F32)


def dot_nt(a, b):
    return lax.dot_general(a, b, (((1,), (1,)), ((), ())), preferred_element_type=F32)


def dot_tn(a, b):
    return lax.dot_general(a, b, (((0,), (0,)), ((), ())), preferred_element_type=F32)


def row_of(ref):
    return ref[...].astype(F32).reshape(1, -1)


def rows_at(start, n):
    return pl.ds(pl.multiple_of(start, min(n, 64)), n)


def own_rows(place, chunk, wide):
    y, _, _, t = place
    return rows_at(chunk * 256 + pair_bit(y) * 128 + t * 32 if wide else chunk * 128 + t * 32, 32)


def remote(src, dst, send_sem, recv_sem, place):
    return pltpu.make_async_remote_copy(src_ref=src, dst_ref=dst, send_sem=send_sem, recv_sem=recv_sem,
                                        device_id=dev(place), device_id_type=MESH)


def wait_bytes(view, sem):
    pltpu.make_async_copy(view, view, sem).wait()


def subsets(dims, place):
    found = [place]
    for dim in dims:
        found = found + [partner(p, dim) for p in found]
    return found


class GroupSum:
    def __init__(self, me, low, recvs, sems, wide):
        self.me, self.low, self.recvs, self.sems, self.wide = me, low, recvs, sems, wide

    def order(self, j):
        if not self.wide:
            return ("core", "xl")
        return (("core", "xl", "y0"), ("core", "y0", "xl"))[j]

    def copies(self, j, s):
        dims = self.order(j)
        to = partner(self.me, dims[s])
        return [remote(self.low.at[own_rows(block, j, self.wide)], self.recvs[s].at[j, i],
                       self.sems.at[s, j, i, 0], self.sems.at[s, j, i, 1], to)
                for i, block in enumerate(subsets(dims[s + 1:], to))]

    def send(self, j, s=0):
        for cp in self.copies(j, s):
            cp.start()

    def step(self, j, s):
        dims = self.order(j)
        for cp in self.copies(j, s):
            cp.wait_recv()
        for i, block in enumerate(subsets(dims[s + 1:], self.me)):
            r = own_rows(block, j, self.wide)
            v = self.low[r, :].astype(F32) + self.recvs[s][j, i].astype(F32)
            if s == len(dims) - 1:
                return v
            self.low[r, :] = v.astype(BF)
        self.send(j, s + 1)

    def finish(self):
        for j in range(2):
            for s in range(len(self.order(j))):
                for cp in self.copies(j, s):
                    cp.wait_send()


class Gather:
    TENSOR = (((), "xl", 0, 2048), ((), "core", 0, 2048), (("xl",), "core", 0, 2048))
    PAIR = (((), "xl", 0, 2048), ((), "y0", 0, 2048), ((), "core", 0, 2048),
            (("y0",), "xl", 0, 1024), (("xl",), "y0", 1024, 1024),
            (("y0",), "core", 0, 2048), (("xl",), "core", 0, 2048),
            (("xl", "y0"), "core", 0, 1024), (("xl", "y0"), "core", 1024, 1024))

    def __init__(self, me, full, sems, wide):
        self.me, self.full, self.sems, self.wide = me, full, sems, wide
        self.moves = self.PAIR if wide else self.TENSOR

    def copy(self, j, i):
        via, dim, col, width = self.moves[i]
        block = self.me
        for d in via:
            block = partner(block, d)
        view = self.full.at[own_rows(block, j, self.wide), pl.ds(col, width)]
        return remote(view, view, self.sems.at[j, i, 0], self.sems.at[j, i, 1], partner(self.me, dim))

    def start(self, j):
        for i in range(3 if self.wide else 2):
            self.copy(j, i).start()

    def relay(self, j):
        if not self.wide:
            self.copy(j, 0).wait_recv()
            self.copy(j, 2).start()
            return
        for came, onward in ((1, (3, 5)), (0, (4, 6)), (3, (7,)), (4, (8,))):
            self.copy(j, came).wait_recv()
            for i in onward:
                self.copy(j, i).start()

    def wait(self, j):
        for i in (2, 5, 6, 7, 8) if self.wide else (1, 2):
            self.copy(j, i).wait_recv()

    def finish(self):
        for j in range(2):
            for i in range(len(self.moves)):
                self.copy(j, i).wait_send()


def owner_runs(base, remaining):
    y, z, h, _ = base

    def ring(v, axis):
        both = (axis + "0" in remaining, axis + "1" in remaining)
        if all(both):
            return None
        if both[0]:
            return [v, flip4(v, "0")]
        if both[1]:
            return [v, flip4(v, "1")]
        return [v]

    ys, zs = ring(y, "y"), ring(z, "z")
    found = []
    for yy in [0, 1, 2, 3] if ys is None else ys:
        if zs is None and "xh" in remaining:
            found.append((yy * 512, 512))
            continue
        for zz in [0, 1, 2, 3] if zs is None else zs:
            if "xh" in remaining:
                found.append((yy * 512 + zz * 128, 128))
            else:
                found.append((yy * 512 + zz * 128 + h * 64, 64))
    return found


class Piece:
    def __init__(self, me, acc, order, keep, recvs, ssem, rsem, emit, stage=None, lsem=None):
        self.me, self.acc, self.order, self.keep, self.recvs = me, acc, order, keep, recvs
        self.ssem, self.rsem, self.emit, self.stage, self.lsem = ssem, rsem, emit, stage, lsem

    def rest(self, s):
        return self.order[s + 1:] + self.keep

    def send(self, s):
        to, off = partner(self.me, self.order[s]), 0
        for row, n in owner_runs(to, self.rest(s)):
            remote(self.acc(rows_at(row, n)), self.recvs[s].at[pl.ds(off, n)], self.ssem.at[s], self.rsem.at[s], to).start()
            off += n

    def arrived(self, s):
        wait_bytes(self.recvs[s], self.rsem.at[s])

    def load(self, s):
        return pltpu.make_async_copy(self.recvs[s], self.stage.at[pl.ds(0, 1024 >> s)], self.lsem)

    def add(self, s):
        view = self.recvs[s]
        if s < 2 and self.stage is not None:
            view = self.stage
        off = 0
        for i, (row, n) in enumerate(owner_runs(self.me, self.rest(s))):
            step = min(n, 128)

            def body(m, _, row=row, off=off, step=step, i=i):
                acc = self.acc(rows_at(row + m * step, step))
                v = acc[...].astype(F32) + view[pl.ds(pl.multiple_of(off + m * step, 64), step), :].astype(F32)
                if s == len(self.order) - 1:
                    self.emit(i, v)
                else:
                    acc[...] = v.astype(BF)
                return 0

            if n == step:
                body(0, 0)
            else:
                lax.fori_loop(0, n // step, body, 0)
            off += n
        if s < len(self.order) - 1:
            self.send(s + 1)

    def finish(self):
        for s in range(len(self.order)):
            wait_bytes(self.recvs[s], self.ssem.at[s])


def advance(pieces, s):
    if s < 2 and pieces[0].stage is not None:
        pieces[0].arrived(s)
        pieces[0].load(s).start()
        for i, piece in enumerate(pieces):
            if i + 1 < len(pieces):
                pieces[i + 1].arrived(s)
                pieces[i + 1].load(s).start()
            piece.load(s).wait()
            piece.add(s)
        return
    for piece in pieces:
        piece.arrived(s)
        piece.add(s)


class GainSum:
    def __init__(self, me, slots, sems):
        y, z, h, t = me
        self.axes = [(t, 4, lambda i: (y, z, h, i)),
                     (z * 2 + h, 8, lambda i: (y, i // 2, i % 2, t)),
                     (y, 4, lambda i: (i, z, h, t))]
        self.slots, self.sems = slots, sems

    def copies(self, s):
        here, n, place = self.axes[s]
        return [remote(self.slots[s].at[here], self.slots[s].at[here], self.sems[s].at[0, d], self.sems[s].at[1, d],
                       place((here + d) % n)) for d in range(1, n)]

    def start(self, s, value):
        self.slots[s][self.axes[s][0]] = value
        for cp in self.copies(s):
            cp.start()

    def take(self, s):
        for cp in self.copies(s):
            cp.wait_recv()
        total = self.slots[s][0]
        for i in range(1, self.axes[s][1]):
            total = total + self.slots[s][i]
        return total

    def finish(self):
        for s in range(3):
            for cp in self.copies(s):
                cp.wait_send()


class ContextSwap:
    def __init__(self, me, send, recv, sems):
        self.me, self.send, self.recv, self.sems = me, send, recv, sems
        self.ctx = me[1] * 2 + me[2]

    def copy(self, d):
        to = (self.ctx + d) % 8
        return remote(self.send.at[to], self.recv.at[self.ctx], self.sems.at[0, d], self.sems.at[1, d],
                      (self.me[0], to // 2, to % 2, self.me[3]))

    def start(self):
        for d in range(1, 8):
            self.copy(d).start()
        self.recv[self.ctx] = self.send[self.ctx]

    def wait(self):
        for d in range(1, 8):
            self.copy(d).wait_recv()

    def finish(self):
        for d in range(1, 8):
            self.copy(d).wait_send()


def rope_constants():
    frequency = np.float32(ROPE_BASE) ** (-np.arange(0, 128, 2).astype(np.float32) / np.float32(128))
    angles = np.arange(1024, dtype=np.float32)[:, None] * frequency.astype(np.float32)[None, :]
    cosine, sine = np.cos(angles), np.sin(angles)
    return (np.concatenate([cosine, cosine], 1).astype(np.float32),
            np.concatenate([-sine, sine], 1).astype(np.float32))


def half_turn(v):
    return pltpu.roll(v, 64, axis=1)


MLP_PIECES = ((0, 0, ("z0", "y1", "z1", "xh")), (0, 1, ("z1", "y1", "z0", "xh")),
              (1, 0, ("z0", "y1", "z1", "xh")), (1, 1, ("z1", "y1", "z0", "xh")),
              (0, 2, ("y1", "z0", "z1", "xh")), (1, 2, ("y1", "z1", "z0", "xh")),
              (2, 0, ("y1", "z0", "z1", "xh")), (2, 1, ("y1", "z1", "z0", "xh")),
              (2, 2, ("xh", "y1", "z0", "z1")))
OUT_ORDERS = (("y0", "z0", "z1", "y1", "xh"), ("y0", "z1", "z0", "y1", "xh"),
              ("y0", "y1", "z0", "z1", "xh"), ("y0", "z0", "y1", "z1", "xh"))
QKV_ORDERS = (("y0", "z0", "y1", "z1", "xh"), ("z0", "y1", "z1", "y0", "xh"),
              ("y1", "z1", "y0", "z0", "xh"), ("z1", "y0", "z0", "y1", "xh"))


def layer_kernel(x_h, g_h, gain1, gain2, qg, kg, wq_h, wk_h, wv_h, wo_h, wg_h, wu_h, wd_h, cos_h, sin_h,
                 block_ref, tok_ref, gains_ref, down_o, gate_o, up_o, out_o, q_o, k_o, v_o, p_h, mrecv0, mrecv1,
                 x, n1, n2, g2, wq, wk, wv, wo, wgt, wut, wdt, low_a, low_b, ra1, ra2, ra3, rb1, rb2, rb3, hidden,
                 qkv_s, qkv_r, mix_s, mix_r, gm_s, gm_r, dqkv_r, dkv, mix, proj, gqkv, mid_ref, gmid, x_own, cosv, sinv,
                 macc, mrecv2, mrecv3, stage, xsend, xrecv,
                 areca0, areca1, areca2, areca3, areca4, arecb0, arecb1, arecb2, arecb3, arecb4, gpart, gs0, gs1, gs2,
                 lsem, psem, s_qkv, s_mix, s_gm, s_dqkv, s_out, s_n2, s_gn2, s_feed, s_gb, s_blk, s_gn1, s_tok, g_sem,
                 mss, mrs, stsem, xs, ass, ars, bss, brs, gsem0, gsem1, gsem2):
    me = me_place()
    ctx = lax.axis_index("context")
    pair = pair_bit(me[0])
    half = pl.multiple_of(pair * 768, 256)

    def load(i, src, dst):
        return pltpu.make_async_copy(src, dst, lsem.at[i])

    first = [load(0, x_h, x), load(1, wk_h, wk), load(2, wv_h, wv),
             load(3, cos_h.at[rows_at(ctx * 128, 128)], cosv), load(4, sin_h.at[rows_at(ctx * 128, 128)], sinv),
             load(5, wq_h, wq), load(6, wo_h, wo)]
    homes = [rows_at(j * 256 + pair * 128, 128) for j in range(2)]
    first += [load(7 + j, g_h.at[pl.ds(j * 128, 128)], g2.at[homes[j]]) for j in range(2)]
    down_load = load(9, wd_h.at[pl.ds(half, 768)], wdt)
    tiles = []
    for i in range(3):
        c = pl.ds(pl.multiple_of(half + i * 256, 256), 256)
        tiles.append((load(10 + i, wg_h.at[:, c], wgt.at[i]), load(13 + i, wu_h.at[:, c], wut.at[i])))
    for cp in first:
        cp.start()
    bar = pltpu.get_barrier_semaphore()
    for d in range(1, 8):
        pl.semaphore_signal(bar, inc=1, device_id=(me[0], (ctx + d) % 8, me[3]), device_id_type=MESH)
    for d in range(1, 4):
        pl.semaphore_signal(bar, inc=1, device_id=(me[0], ctx, (me[3] + d) % 4), device_id_type=MESH)
        pl.semaphore_signal(bar, inc=1, device_id=((me[0] + d) % 4, ctx, me[3]), device_id_type=MESH)

    first[0].wait()
    g1 = row_of(gain1)

    def norm_rows(i, _):
        r = pl.ds(pl.multiple_of(i * 32, 32), 32)
        xv = x[r, :].astype(F32)
        inv = lax.rsqrt(jnp.mean(xv * xv, axis=-1, keepdims=True) + EPSILON)
        n1[r, :] = (xv * inv * g1).astype(BF)
        return 0

    lax.fori_loop(0, 8, norm_rows, 0)
    for j in range(2):
        x_own[j * 32:(j + 1) * 32, :] = x[own_rows(me, j, False), :]
    for i in (1, 2, 3, 4):
        first[i].wait()
    cos2 = jnp.concatenate([cosv[...], cosv[...]], axis=0)
    sin2 = jnp.concatenate([sinv[...], sinv[...]], axis=0)
    gqf, gkf = row_of(qg), row_of(kg)

    def turned(v, gain):
        hat = v * lax.rsqrt(jnp.mean(v * v, axis=-1, keepdims=True) + EPSILON) * gain
        return (hat * cos2 + half_turn(hat) * sin2).astype(BF)

    def spread(first, width, heads, value):
        for s in range(2):
            for h in range(4):
                c = h * width // 4 * 128
                qkv_s[s * 4 + h, :, first:first + 128] = value[s * 128:(s + 1) * 128, c:c + 128]

    kp = dot(n1[...], wk[...])
    proj[:, 512:768] = kp
    spread(128, 2, 2, jnp.concatenate([turned(kp[:, h * 128:(h + 1) * 128], gkf) for h in range(2)], axis=1))
    spread(256, 2, 2, dot(n1[...], wv[...]).astype(BF))
    first[5].wait()
    qp = dot(n1[...], wq[...])
    proj[:, 0:512] = qp
    spread(0, 4, 4, jnp.concatenate([turned(qp[:, h * 128:(h + 1) * 128], gqf) for h in range(4)], axis=1))
    pl.semaphore_wait(bar, 13)
    swap_qkv = ContextSwap(me, qkv_s, qkv_r, s_qkv)
    swap_qkv.start()
    g_copies = [remote(g2.at[homes[j]], g2.at[homes[j]], g_sem.at[0, j], g_sem.at[1, j], partner(me, "y0")) for j in range(2)]
    for j in range(2):
        first[7 + j].wait()
        g_copies[j].start()
    down_load.start()
    for pair_loads in tiles:
        for cp in pair_loads:
            cp.start()
    first[6].wait()
    swap_qkv.wait()

    def part(ref, n, first):
        return ref[0:n * 2, :, first:first + 128].reshape(n * 256, 128)

    def prob_home(i, j):
        n = i * 4 + j
        return (n // 2, slice((n % 2) * 256, (n % 2 + 1) * 256))

    seen = lax.broadcasted_iota(jnp.int32, (256, 256), 0) >= lax.broadcasted_iota(jnp.int32, (256, 256), 1)
    for i in range(4):
        q = qkv_r[2 * i:2 * i + 2, :, 0:128].reshape(256, 128)
        scores = dot_nt(q, part(qkv_r, i + 1, 128)) * SCALE
        last = jnp.where(seen, scores[:, i * 256:], -1e30)
        scores = last if i == 0 else jnp.concatenate([scores[:, :i * 256], last], axis=1)
        e = jnp.exp(scores - jnp.max(scores, axis=-1, keepdims=True))
        prob = (e / jnp.sum(e, axis=-1, keepdims=True)).astype(BF)
        for j in range(i + 1):
            hidden[prob_home(i, j)] = prob[:, j * 256:(j + 1) * 256]
        mix_s[2 * i:2 * i + 2] = dot(prob, part(qkv_r, i + 1, 256)).astype(BF).reshape(2, 128, 128)
    swap_mix = ContextSwap(me, mix_s, mix_r, s_mix)
    swap_mix.start()
    p_out = pltpu.make_async_copy(hidden.at[pl.ds(0, 8)], p_h, psem.at[0])
    p_out.start()
    for cp in g_copies:
        cp.wait_recv()
    down_load.wait()
    swap_mix.wait()
    for p in range(8):
        mix[(p // 4) * 128:(p // 4 + 1) * 128, (p % 4) * 128:(p % 4 + 1) * 128] = mix_r[p]

    sum_o = GroupSum(me, low_a.at[0:256], (ra1, ra2), s_out, False)
    for j in range(2):
        low_a[j * 128:(j + 1) * 128, :] = dot(mix[j * 128:(j + 1) * 128, :], wo[...]).astype(BF)
        sum_o.send(j)
    p_out.wait()
    for i in range(3):
        hidden[6 + i] = dot_nt(g2[...], wdt[i * 256:(i + 1) * 256, :]).astype(BF)
    for j in range(2):
        sum_o.step(j, 0)
    gather_n = Gather(me, n2, s_n2, True)
    scale2 = row_of(gain2)

    def halves(j):
        return slice(j * 32, (j + 1) * 32)

    for j in range(2):
        mid = x_own[halves(j), :].astype(F32) + sum_o.step(j, 1)
        mid_ref[halves(j), :] = mid
        inv = lax.rsqrt(jnp.mean(mid * mid, axis=-1, keepdims=True) + EPSILON)
        n2[own_rows(me, j, True), :] = (mid * inv * scale2).astype(BF)
        gather_n.start(j)
    for i in range(3):
        for cp in tiles[i]:
            cp.wait()
    sum_o.finish()
    sum2 = GroupSum(me, low_a, (ra1, ra2, ra3), s_gn2, True)
    sumf = GroupSum(me, low_b, (rb1, rb2, rb3), s_feed, True)
    for j in range(2):
        gather_n.relay(j)
    for j in range(2):
        gather_n.wait(j)
        r = slice(j * 256, (j + 1) * 256)
        for i in range(3):
            gate = dot(n2[r, :], wgt[i])
            up = dot(n2[r, :], wut[i])
            gh = hidden[6 + i, r, :].astype(F32)
            sig = 1.0 / (1.0 + jnp.exp(-gate))
            silu = gate * sig
            hidden[i, r, :] = (silu * up).astype(BF)
            hidden[3 + i, r, :] = (gh * up * sig * (1.0 + gate * (1.0 - sig))).astype(BF)
            hidden[6 + i, r, :] = (gh * silu).astype(BF)
        for n in range(4):
            c = slice(n * 512, (n + 1) * 512)
            v = dot_nt(hidden[3, r, :], wgt[0, c, :]) + dot_nt(hidden[6, r, :], wut[0, c, :])
            for i in (1, 2):
                v = v + dot_nt(hidden[3 + i, r, :], wgt[i, c, :]) + dot_nt(hidden[6 + i, r, :], wut[i, c, :])
            low_a[r, c] = v.astype(BF)
        sum2.send(j)

    mlp, slot = [], {}
    for n, (k, i, dims) in enumerate(MLP_PIECES):
        slot[k, i] = n
        out = (down_o, gate_o, up_o)[k]

        def emit(m, v, out=out, i=i, n=n):
            if m == 0:
                out[pair, :, i * 256:(i + 1) * 256] = v
            else:
                xsend[n] = v.astype(BF)

        mlp.append(Piece(me, lambda r, n=n: macc.at[n, r], dims, ("y0",),
                         (mrecv0.at[n], mrecv1.at[n], mrecv2.at[n], mrecv3.at[n]), mss.at[n], mrs.at[n], emit,
                         stage.at[n % 2], stsem.at[n % 2]))
    four = range(4)

    def outer(left, k, c):
        t = left[:, c].T
        for weight in k:
            for i in range(3):
                macc[slot[weight, i], c, :] = dot(t, hidden[weight * 3 + i]).astype(BF)

    for n in four:
        outer(g2, (0,), slice(n * 512, (n + 1) * 512))
        if n % 2:
            sum2.step(n // 2, 0)
    for piece in (mlp[0], mlp[1], mlp[4]):
        piece.send(0)
    for n in four:
        outer(n2, (1, 2), slice(n * 512, (n + 1) * 512))
        if n % 2:
            sum2.step(n // 2, 1)
    for piece in mlp[2:4] + mlp[5:8]:
        piece.send(0)
    p_in = pltpu.make_async_copy(p_h, hidden.at[pl.ds(0, 8)], psem.at[1])
    for n in four:
        c = slice(n * 512, (n + 1) * 512)
        v = dot(hidden[0], wdt[0:256, c])
        for i in (1, 2):
            v = v + dot(hidden[i], wdt[i * 256:(i + 1) * 256, c])
        low_b[:, c] = v.astype(BF)
    p_in.start()

    gb = x
    gather_b = Gather(me, gb, s_gb, False)
    gain_term = jnp.zeros((1, 2048), F32)
    for j in range(2):
        mid = mid_ref[halves(j), :]
        inv = lax.rsqrt(jnp.mean(mid * mid, axis=-1, keepdims=True) + EPSILON)
        hat = mid * inv
        grad = sum2.step(j, 2)
        gain_term = gain_term + jnp.sum(grad * hat, axis=0, keepdims=True)
        u = grad * scale2
        grad = g2[own_rows(me, j, True), :].astype(F32) + inv * (u - hat * jnp.mean(u * hat, axis=-1, keepdims=True))
        gmid[halves(j), :] = grad
        gb[own_rows(me, j, False), :] = grad.astype(BF)
        gather_b.start(j)
    gpart[...] = jnp.zeros((40, 128), F32)

    def put_gain(row, value):
        for i in range(value.shape[1] // 128):
            gpart[row + i:row + i + 1, :] = value[:, i * 128:(i + 1) * 128]

    put_gain(16, gain_term)
    for j in range(2):
        gather_b.relay(j)
    for j in range(2):
        gather_b.wait(j)

    for b in range(2):
        gmix = dot_nt(gb[...], wo[b * 256:(b + 1) * 256, :]).astype(BF)
        for s in range(2):
            for h in range(2):
                gm_s[s * 4 + b * 2 + h] = gmix[s * 128:(s + 1) * 128, h * 128:(h + 1) * 128]
    swap_gm = ContextSwap(me, gm_s, gm_r, s_gm)
    swap_gm.start()
    for j in range(2):
        sumf.send(j)
    mlp[8].send(0)

    att_a, att_b = [], []
    spots = [(lambda r, i=i: wut.at[1 + i // 2, r, pl.ds((i % 2) * 128, 128)]) for i in range(4)]
    spots += [(lambda r, i=i: (wgt.at[i, r] if i < 3 else wut.at[0, r])) for i in range(4)]
    for i in range(4):
        def emit_a(m, v, i=i):
            out_o[:, i * 128:(i + 1) * 128] = v

        def emit_b(m, v, i=i):
            (q_o, q_o, k_o, v_o)[i][:, (i * 256 if i == 1 else 0):(i * 256 if i == 1 else 0) + 256] = v

        att_a.append(Piece(me, spots[i], OUT_ORDERS[i], (), tuple(r.at[i] for r in (areca0, areca1, areca2, areca3, areca4)),
                           ass.at[i], ars.at[i], emit_a))
        att_b.append(Piece(me, spots[4 + i], QKV_ORDERS[i], (), tuple(r.at[i] for r in (arecb0, arecb1, arecb2, arecb3, arecb4)),
                           bss.at[i], brs.at[i], emit_b))
    for j in four:
        c = slice(j * 512, (j + 1) * 512)
        v = dot(gb[:, c].T, mix[...]).astype(BF)
        wut[1, c, :] = v[:, 0:256]
        wut[2, c, :] = v[:, 256:512]
    for j in range(2):
        sumf.step(j, 0)
    for piece in att_a:
        piece.send(0)
    p_in.wait()
    swap_qkv.finish()
    swap_gm.wait()
    for i in range(4):
        n = (i + 1) * 256
        gm = gm_r[2 * i:2 * i + 2].reshape(256, 128)
        prob = jnp.concatenate([hidden[prob_home(i, j)] for j in range(i + 1)], axis=1)
        gp = dot_nt(gm, part(qkv_r, i + 1, 256))
        prob32 = prob.astype(F32)
        gs = (prob32 * (gp - jnp.sum(prob32 * gp, axis=-1, keepdims=True))).astype(BF)
        q = qkv_r[2 * i:2 * i + 2, :, 0:128].reshape(256, 128)
        qkv_s[2 * i:2 * i + 2, :, 0:128] = (dot(gs, part(qkv_r, i + 1, 128)) * SCALE).astype(BF).reshape(2, 128, 128)
        gk = dot_tn(gs, q)
        gv = dot_tn(prob, gm)
        if i:
            dkv[0:n - 256, 0:128] += gk[0:n - 256]
            dkv[0:n - 256, 128:256] += gv[0:n - 256]
        dkv[n - 256:n, 0:128] = gk[n - 256:n]
        dkv[n - 256:n, 128:256] = gv[n - 256:n]
    qkv_s[:, :, 128:256] = (dkv[:, 0:128] * SCALE).astype(BF).reshape(8, 128, 128)
    qkv_s[:, :, 256:384] = dkv[:, 128:256].astype(BF).reshape(8, 128, 128)
    swap_dqkv = ContextSwap(me, qkv_s, dqkv_r, s_dqkv)
    swap_dqkv.start()
    for j in range(2):
        sumf.step(j, 1)
    advance(mlp[0:4], 0)
    gather_o = Gather(me, block_ref, s_blk, False)
    for j in range(2):
        block_ref[own_rows(me, j, False), :] = (mid_ref[halves(j), :] + sumf.step(j, 2)).astype(BF)
        gather_o.start(j)
    advance(mlp[4:6], 0)

    def through_norm(grad_rot, pre, gain):
        grad_normed = grad_rot * cos2 - half_turn(grad_rot) * sin2
        inv = lax.rsqrt(jnp.mean(pre * pre, axis=-1, keepdims=True) + EPSILON)
        hat = pre * inv
        u = grad_normed * gain
        grad_pre = inv * (u - hat * jnp.mean(u * hat, axis=-1, keepdims=True))
        return grad_pre.astype(BF), jnp.sum(grad_normed * hat, axis=0, keepdims=True)

    def arrived(first, heads):
        rows = []
        for s in range(2):
            v = dqkv_r[s * 4 + heads[0], :, first:first + 128].astype(F32)
            for h in heads[1:]:
                v = v + dqkv_r[s * 4 + h, :, first:first + 128].astype(F32)
            rows.append(v)
        return jnp.concatenate(rows, axis=0)

    swap_dqkv.wait()
    gain_sum = jnp.zeros((1, 128), F32)
    for h in range(4):
        c = slice(h * 128, (h + 1) * 128)
        gqkv[:, c], term = through_norm(arrived(0, (h,)), proj[:, c], gqf)
        gain_sum = gain_sum + term
    put_gain(32, gain_sum)
    gain_sum = jnp.zeros((1, 128), F32)
    for h in range(2):
        c = slice(512 + h * 128, 640 + h * 128)
        gqkv[:, c], term = through_norm(arrived(128, (2 * h, 2 * h + 1)), proj[:, c], gkf)
        gain_sum = gain_sum + term
        gqkv[:, 768 + h * 128:896 + h * 128] = arrived(256, (2 * h, 2 * h + 1)).astype(BF)
    put_gain(33, gain_sum)

    sum2.finish()
    sum1 = GroupSum(me, low_a.at[0:256], (ra1, ra2), s_gn1, False)
    for j in range(2):
        r = slice(j * 128, (j + 1) * 128)
        v = dot_nt(gqkv[r, 0:512], wq[...]) + dot_nt(gqkv[r, 512:768], wk[...]) + dot_nt(gqkv[r, 768:1024], wv[...])
        low_a[r, :] = v.astype(BF)
        sum1.send(j)
    for n in four:
        c = slice(n * 512, (n + 1) * 512)
        v = dot(n1[:, c].T, gqkv[...]).astype(BF)
        for i in range(3):
            wgt[i, c, :] = v[:, i * 256:(i + 1) * 256]
        wut[0, c, :] = v[:, 768:1024]
    for piece in att_b:
        piece.send(0)
    for j in range(2):
        sum1.step(j, 0)
    for j in range(2):
        gather_o.relay(j)
    scale1 = row_of(gain1)
    gather_t = Gather(me, tok_ref, s_tok, False)
    gain_term = jnp.zeros((1, 2048), F32)
    for j in range(2):
        xo = x_own[halves(j), :].astype(F32)
        inv = lax.rsqrt(jnp.mean(xo * xo, axis=-1, keepdims=True) + EPSILON)
        hat = xo * inv
        grad = sum1.step(j, 1)
        gain_term = gain_term + jnp.sum(grad * hat, axis=0, keepdims=True)
        u = grad * scale1
        tok_ref[own_rows(me, j, False), :] = (
            gmid[halves(j), :] + inv * (u - hat * jnp.mean(u * hat, axis=-1, keepdims=True))).astype(BF)
        gather_t.start(j)
    put_gain(0, gain_term)
    gains = GainSum(me, (gs0, gs1, gs2), (gsem0, gsem1, gsem2))
    gains.start(0, gpart[...])
    advance(mlp[6:8], 0)
    advance(mlp[8:9], 0)
    advance(mlp[0:4], 1)
    gains.start(1, gains.take(0))
    for j in range(2):
        gather_t.relay(j)
    advance(att_a, 0)
    advance(mlp[4:8], 1)
    advance(att_b, 0)
    gains.start(2, gains.take(1))
    advance(mlp[8:9], 1)
    advance(att_a, 1)
    advance(mlp, 2)
    advance(att_b, 1)
    advance(mlp, 3)
    swap = [remote(xsend.at[n], xrecv.at[n], xs.at[n, 0], xs.at[n, 1], partner(me, "y0")) for n in range(9)]
    for cp in swap:
        cp.start()
    advance(att_a, 2)
    gains_ref[...] = gains.take(2)
    advance(att_b, 2)
    advance(att_a, 3)
    advance(att_b, 3)
    advance(att_a, 4)
    advance(att_b, 4)
    for n, cp in enumerate(swap):
        cp.wait_recv()
        k, i, _ = MLP_PIECES[n]
        (down_o, gate_o, up_o)[k][1 - pair, :, i * 256:(i + 1) * 256] = xrecv[n].astype(F32)

    for cp in swap:
        cp.wait_send()
    for gather in (gather_b, gather_o, gather_t):
        gather.finish()
    for gather in (gather_o, gather_t):
        for j in range(2):
            gather.wait(j)
    gather_n.finish()
    gains.finish()
    sum1.finish()
    for cp in g_copies:
        cp.wait_send()
    swap_mix.finish()
    swap_gm.finish()
    swap_dqkv.finish()
    sumf.finish()
    for piece in mlp + att_a + att_b:
        piece.finish()


def layer(x, g, gain1, gain2, qg, kg, wq, wk, wv, wo, wg, wu, wd):
    cos_t, sin_t = rope_constants()
    V = pl.BlockSpec(memory_space=pltpu.VMEM)
    A = pl.BlockSpec(memory_space=pl.ANY)
    S = jax.ShapeDtypeStruct
    D = pltpu.SemaphoreType.DMA
    M = pltpu.VMEM
    return pl.pallas_call(
        layer_kernel,
        out_shape=(S((256, 2048), BF), S((256, 2048), BF), S((40, 128), F32),
                   S((2, 64, 768), F32), S((2, 64, 768), F32), S((2, 64, 768), F32), S((64, 512), F32), S((64, 512), F32),
                   S((64, 256), F32), S((64, 256), F32), S((8, 512, 256), BF), S((9, 1024, 256), BF), S((9, 512, 256), BF)),
        in_specs=[A, A, V, V, V, V] + [A] * 9,
        out_specs=(V,) * 10 + (A, A, A),
        scratch_shapes=[
            M((256, 2048), BF), M((256, 2048), BF), M((512, 2048), BF), M((512, 2048), BF),
            M((2048, 512), BF), M((2048, 256), BF), M((2048, 256), BF), M((512, 2048), BF),
            M((3, 2048, 256), BF), M((3, 2048, 256), BF), M((768, 2048), BF),
            M((512, 2048), BF), M((512, 2048), BF),
            M((2, 4, 32, 2048), BF), M((2, 2, 32, 2048), BF), M((2, 1, 32, 2048), BF),
            M((2, 4, 32, 2048), BF), M((2, 2, 32, 2048), BF), M((2, 1, 32, 2048), BF), M((9, 512, 256), BF),
            M((8, 128, 384), BF), M((8, 128, 384), BF), M((8, 128, 128), BF), M((8, 128, 128), BF), M((8, 128, 128), BF),
            M((8, 128, 128), BF), M((8, 128, 384), BF), M((1024, 256), F32), M((256, 512), BF), M((256, 768), F32),
            M((256, 1024), BF), M((64, 2048), F32), M((64, 2048), F32),
            M((64, 2048), BF), M((128, 128), F32), M((128, 128), F32),
            M((9, 2048, 256), BF), M((9, 256, 256), BF), M((9, 128, 256), BF),
            M((2, 1024, 256), BF), M((9, 64, 256), BF), M((9, 64, 256), BF)]
        + [M((4, 1024 >> s, 128), BF) for s in range(5)] + [M((4, 1024 >> s, 256), BF) for s in range(5)]
        + [M((40, 128), F32), M((4, 40, 128), F32), M((8, 40, 128), F32), M((4, 40, 128), F32),
           D((16,)), D((2,)), D((2, 8)), D((2, 8)), D((2, 8)), D((2, 8)), D((2, 2, 2, 2)), D((2, 9, 2)), D((3, 2, 4, 2)),
           D((3, 2, 4, 2)), D((2, 3, 2)), D((2, 3, 2)), D((2, 2, 2, 2)), D((2, 3, 2)), D((2, 2)),
           D((9, 4)), D((9, 4)), D((2,)), D((9, 2)), D((4, 5)), D((4, 5)), D((4, 5)), D((4, 5)),
           D((2, 4)), D((2, 8)), D((2, 4))],
        compiler_params=pltpu.CompilerParams(collective_id=3, has_side_effects=True, vmem_limit_bytes=63 * 2**20),
    )(x, g, gain1, gain2, qg, kg, wq, wk, wv, wo, wg, wu, wd, jnp.asarray(cos_t), jnp.asarray(sin_t))


def tail_kernel(block_h, tok_h, gains, down_h, gate_h, up_h, out_h, q_h, k_h, v_h,
                block_o, tok_o, gain1_o, q_o, k_o, v_o, qg_o, kg_o, out_o, gain2_o, gate_o, up_o, down_o, sems):
    pairs = [(block_h, block_o), (tok_h, tok_o), (q_h, q_o), (k_h, k_o), (v_h, v_o), (out_h, out_o)]
    for i in range(2):
        c = pl.ds(i * 768, 768)
        pairs += [(down_h.at[i], down_o.at[:, c]), (gate_h.at[i], gate_o.at[:, c]), (up_h.at[i], up_o.at[:, c])]
    copies = [pltpu.make_async_copy(s, d, sems.at[i]) for i, (s, d) in enumerate(pairs)]
    for cp in copies:
        cp.start()
    gain1_o[...] = gains[0:16]
    gain2_o[...] = gains[16:32]
    qg_o[...] = gains[32:33]
    kg_o[...] = gains[33:34]
    for cp in copies:
        cp.wait()


def tail(block, tok, gains, down, gate, up, out, q, k, v):
    V = pl.BlockSpec(memory_space=pltpu.VMEM)
    A = pl.BlockSpec(memory_space=pl.ANY)
    S = jax.ShapeDtypeStruct
    return pl.pallas_call(
        tail_kernel,
        out_shape=(S((256, 2048), BF), S((256, 2048), BF), S((16, 128), F32), S((64, 512), F32), S((64, 256), F32),
                   S((64, 256), F32), S((1, 128), F32), S((1, 128), F32), S((64, 512), F32), S((16, 128), F32),
                   S((64, 1536), F32), S((64, 1536), F32), S((64, 1536), F32)),
        in_specs=[A, A, V, A, A, A, A, A, A, A],
        out_specs=(V,) * 13,
        scratch_shapes=[pltpu.SemaphoreType.DMA((12,))],
        compiler_params=pltpu.CompilerParams(vmem_limit_bytes=62 * 2**20),
    )(block, tok, gains, down, gate, up, out, q, k, v)


def local(tokens, attn_gain, w_query, w_key, w_value, query_gain, key_gain, w_out, mlp_gain, w_gate, w_up, w_down, out_grad):
    results = layer(tokens.reshape(256, 2048), out_grad.reshape(256, 2048), attn_gain, mlp_gain, query_gain, key_gain,
                    w_query, w_key, w_value, w_out, w_gate, w_up, w_down)
    block, tok, g1, q, k, v, qg, kg, out, g2, gate, up, down = tail(*results[:10])
    return (block.reshape(2, 128, 2048), tok.reshape(2, 128, 2048), g1.reshape(2048), q, k, v, qg.reshape(128),
            kg.reshape(128), out.T, g2.reshape(2048), gate, up, down.T)


def solution(mesh):
    in_specs = (
        P("dp", "context", None),
        P(),
        P(None, "tensor"),
        P(None, "tensor"),
        P(None, "tensor"),
        P(),
        P(),
        P("tensor", None),
        P(),
        P(None, "tensor"),
        P(None, "tensor"),
        P("tensor", None),
        P("dp", "context", None),
    )
    out_specs = (
        P("dp", "context", None),
        P("dp", "context", None),
        P(),
        P(("dp", "context"), "tensor"),
        P(("dp", "context"), "tensor"),
        P(("dp", "context"), "tensor"),
        P(),
        P(),
        P("tensor", ("dp", "context")),
        P(),
        P(("dp", "context"), "tensor"),
        P(("dp", "context"), "tensor"),
        P("tensor", ("dp", "context")),
    )
    return jax.shard_map(local, mesh=mesh, in_specs=in_specs, out_specs=out_specs, check_vma=False)
```

```python
import numpy as np
import jax
import jax.numpy as jnp
from jax import lax
from jax.experimental import pallas as pl
from jax.experimental.pallas import tpu as pltpu
from jax.sharding import PartitionSpec as P

MESH = pl.DeviceIdType.MESH
BF = jnp.bfloat16
F32 = jnp.float32
EPSILON = 1e-06
ROPE_BASE = 1000000.0
SCALE = 128 ** (-0.5)


def me_place():
    c = lax.axis_index("context")
    return (lax.axis_index("dp"), c // 2, c % 2, lax.axis_index("tensor"))


def dev(place):
    y, z, h, t = place
    return (y, z * 2 + h, t)


def flip4(v, which):
    return v + 1 - 2 * (v % 2) if which == "0" else 3 - v


def pair_bit(y):
    return ((y + 1) // 2) % 2


def partner(place, dim):
    y, z, h, t = place
    if dim == "core":
        return (y, z, h, t + 1 - 2 * (t % 2))
    if dim == "xl":
        return (y, z, h, (t + 2) % 4)
    if dim == "xh":
        return (y, z, 1 - h, t)
    if dim[0] == "y":
        return (flip4(y, dim[1]), z, h, t)
    return (y, flip4(z, dim[1]), h, t)


def dot(a, b):
    return jnp.dot(a, b, preferred_element_type=F32)


def dot_nt(a, b):
    return lax.dot_general(a, b, (((1,), (1,)), ((), ())), preferred_element_type=F32)


def dot_tn(a, b):
    return lax.dot_general(a, b, (((0,), (0,)), ((), ())), preferred_element_type=F32)


def row_of(ref):
    return ref[...].astype(F32).reshape(1, -1)


def rows_at(start, n):
    return pl.ds(pl.multiple_of(start, min(n, 64)), n)


def own_rows(place, chunk, wide):
    y, _, _, t = place
    return rows_at(chunk * 256 + pair_bit(y) * 128 + t * 32 if wide else chunk * 128 + t * 32, 32)


def remote(src, dst, send_sem, recv_sem, place):
    return pltpu.make_async_remote_copy(src_ref=src, dst_ref=dst, send_sem=send_sem, recv_sem=recv_sem,
                                        device_id=dev(place), device_id_type=MESH)


def wait_bytes(view, sem):
    pltpu.make_async_copy(view, view, sem).wait()


def subsets(dims, place):
    found = [place]
    for dim in dims:
        found = found + [partner(p, dim) for p in found]
    return found


class GroupSum:
    def __init__(self, me, low, recvs, sems, wide):
        self.me, self.low, self.recvs, self.sems, self.wide = me, low, recvs, sems, wide

    def order(self, j):
        if not self.wide:
            return ("core", "xl")
        return (("core", "xl", "y0"), ("core", "y0", "xl"))[j]

    def copies(self, j, s):
        dims = self.order(j)
        to = partner(self.me, dims[s])
        return [remote(self.low.at[own_rows(block, j, self.wide)], self.recvs[s].at[j, i],
                       self.sems.at[s, j, i, 0], self.sems.at[s, j, i, 1], to)
                for i, block in enumerate(subsets(dims[s + 1:], to))]

    def send(self, j, s=0):
        for cp in self.copies(j, s):
            cp.start()

    def step(self, j, s):
        dims = self.order(j)
        for cp in self.copies(j, s):
            cp.wait_recv()
        for i, block in enumerate(subsets(dims[s + 1:], self.me)):
            r = own_rows(block, j, self.wide)
            v = self.low[r, :].astype(F32) + self.recvs[s][j, i].astype(F32)
            if s == len(dims) - 1:
                return v
            self.low[r, :] = v.astype(BF)
        self.send(j, s + 1)

    def finish(self):
        for j in range(2):
            for s in range(len(self.order(j))):
                for cp in self.copies(j, s):
                    cp.wait_send()


class Gather:
    TENSOR = (((), "xl", 0, 2048), ((), "core", 0, 2048), (("xl",), "core", 0, 2048))
    PAIR = (((), "xl", 0, 2048), ((), "y0", 0, 2048), ((), "core", 0, 2048),
            (("y0",), "xl", 0, 1024), (("xl",), "y0", 1024, 1024),
            (("y0",), "core", 0, 2048), (("xl",), "core", 0, 2048),
            (("xl", "y0"), "core", 0, 1024), (("xl", "y0"), "core", 1024, 1024))

    def __init__(self, me, full, sems, wide):
        self.me, self.full, self.sems, self.wide = me, full, sems, wide
        self.moves = self.PAIR if wide else self.TENSOR

    def copy(self, j, i):
        via, dim, col, width = self.moves[i]
        block = self.me
        for d in via:
            block = partner(block, d)
        view = self.full.at[own_rows(block, j, self.wide), pl.ds(col, width)]
        return remote(view, view, self.sems.at[j, i, 0], self.sems.at[j, i, 1], partner(self.me, dim))

    def start(self, j):
        for i in range(3 if self.wide else 2):
            self.copy(j, i).start()

    def relay(self, j):
        if not self.wide:
            self.copy(j, 0).wait_recv()
            self.copy(j, 2).start()
            return
        for came, onward in ((1, (3, 5)), (0, (4, 6)), (3, (7,)), (4, (8,))):
            self.copy(j, came).wait_recv()
            for i in onward:
                self.copy(j, i).start()

    def wait(self, j):
        for i in (2, 5, 6, 7, 8) if self.wide else (1, 2):
            self.copy(j, i).wait_recv()

    def finish(self):
        for j in range(2):
            for i in range(len(self.moves)):
                self.copy(j, i).wait_send()


def dim_bit(place, dim):
    y, z, h, _ = place
    if dim == "xh":
        return h
    v = y if dim[0] == "y" else z
    return pair_bit(v) if dim[1] == "0" else v // 2


class Piece:
    def __init__(self, me, acc, order, keep, recvs, ssem, rsem, emit, stage=None, lsem=None):
        self.me, self.acc, self.order, self.keep, self.recvs = me, acc, order, keep, recvs
        self.ssem, self.rsem, self.emit, self.stage, self.lsem = ssem, rsem, emit, stage, lsem

    def put(self, y, value):
        dims = self.order + self.keep
        for z in range(4):
            for h in range(2):
                spot = 0
                for i, dim in enumerate(dims):
                    here = dim_bit(self.me, dim)
                    spot = spot + (1 - here if dim_bit((y, z, h, 0), dim) else here) * (1024 >> i)
                b = (z * 2 + h) * 64
                self.acc(rows_at(spot, 64))[...] = value[b:b + 64]

    def send(self, s):
        n = 1024 >> s
        remote(self.acc(pl.ds(n, n)), self.recvs[s], self.ssem.at[s], self.rsem.at[s], partner(self.me, self.order[s])).start()

    def arrived(self, s):
        wait_bytes(self.recvs[s], self.rsem.at[s])

    def loads(self):
        return [pltpu.make_async_copy(self.recvs[0].at[pl.ds(i * 512, 512)], self.stage[i], self.lsem.at[i]) for i in range(2)]

    def add(self, s):
        n = 1024 >> s
        if s == len(self.order) - 1:
            v = self.acc(pl.ds(0, n))[...].astype(F32) + self.recvs[s][...].astype(F32)
            for i in range(n // 64):
                self.emit(i, v[i * 64:(i + 1) * 64])
            return
        parts = [(0, n, self.recvs[s])]
        if s == 0 and self.stage is not None:
            parts = [(0, 512, self.stage[0]), (512, 512, self.stage[1])]
        for first, count, view in parts:
            step = min(count, 128)

            def body(m, _, first=first, step=step, view=view):
                acc = self.acc(rows_at(first + m * step, step))
                acc[...] = (acc[...].astype(F32) + view[rows_at(m * step, step), :].astype(F32)).astype(BF)
                return 0

            if count == step:
                body(0, 0)
            else:
                lax.fori_loop(0, count // step, body, 0)
        self.send(s + 1)

    def finish(self):
        for s in range(len(self.order)):
            wait_bytes(self.recvs[s], self.ssem.at[s])


def advance(pieces, s):
    if s or pieces[0].stage is None:
        for piece in pieces:
            piece.arrived(s)
            piece.add(s)
        return

    def fetch(piece):
        piece.arrived(0)
        for cp in piece.loads():
            cp.start()

    fetch(pieces[0])
    for i, piece in enumerate(pieces):
        if i + 1 < len(pieces):
            fetch(pieces[i + 1])
        for cp in piece.loads():
            cp.wait()
        piece.add(0)


class GainSum:
    def __init__(self, me, slots, sems):
        y, z, h, t = me
        self.axes = [(t, 4, lambda i: (y, z, h, i)),
                     (z * 2 + h, 8, lambda i: (y, i // 2, i % 2, t)),
                     (y, 4, lambda i: (i, z, h, t))]
        self.slots, self.sems = slots, sems

    def copies(self, s):
        here, n, place = self.axes[s]
        return [remote(self.slots[s].at[here], self.slots[s].at[here], self.sems[s].at[0, d], self.sems[s].at[1, d],
                       place((here + d) % n)) for d in range(1, n)]

    def start(self, s, value):
        self.slots[s][self.axes[s][0]] = value
        for cp in self.copies(s):
            cp.start()

    def take(self, s):
        for cp in self.copies(s):
            cp.wait_recv()
        total = self.slots[s][0]
        for i in range(1, self.axes[s][1]):
            total = total + self.slots[s][i]
        return total

    def finish(self):
        for s in range(3):
            for cp in self.copies(s):
                cp.wait_send()


class ContextSwap:
    def __init__(self, me, send, recv, sems):
        self.me, self.send, self.recv, self.sems = me, send, recv, sems
        self.ctx = me[1] * 2 + me[2]

    def copy(self, d):
        to = (self.ctx + d) % 8
        return remote(self.send.at[to], self.recv.at[self.ctx], self.sems.at[0, d], self.sems.at[1, d],
                      (self.me[0], to // 2, to % 2, self.me[3]))

    def start(self):
        for d in range(1, 8):
            self.copy(d).start()
        self.recv[self.ctx] = self.send[self.ctx]

    def wait(self):
        for d in range(1, 8):
            self.copy(d).wait_recv()

    def finish(self):
        for d in range(1, 8):
            self.copy(d).wait_send()


def rope_constants():
    frequency = np.float32(ROPE_BASE) ** (-np.arange(0, 128, 2).astype(np.float32) / np.float32(128))
    angles = np.arange(1024, dtype=np.float32)[:, None] * frequency.astype(np.float32)[None, :]
    cosine, sine = np.cos(angles), np.sin(angles)
    return (np.concatenate([cosine, cosine], 1).astype(np.float32),
            np.concatenate([-sine, sine], 1).astype(np.float32))


def half_turn(v):
    return pltpu.roll(v, 64, axis=1)


MLP_PIECES = ((0, 0, ("z0", "z1", "xh", "y1")), (0, 1, ("z1", "z0", "xh", "y1")),
              (1, 0, ("z0", "z1", "xh", "y1")), (1, 1, ("z1", "z0", "xh", "y1")),
              (0, 2, ("y1", "xh", "z0", "z1")), (1, 2, ("y1", "xh", "z1", "z0")),
              (2, 0, ("y1", "xh", "z0", "z1")), (2, 1, ("y1", "xh", "z1", "z0")),
              (2, 2, ("y1", "xh", "z0", "z1")))
OUT_ORDERS = (("y0", "z0", "z1", "y1", "xh"), ("y0", "z1", "z0", "y1", "xh"),
              ("y0", "z0", "y1", "z1", "xh"), ("y0", "z1", "y1", "z0", "xh"))
QKV_ORDERS = (("y0", "y1", "z0", "z1", "xh"), ("y1", "y0", "z1", "z0", "xh"),
              ("z0", "z1", "y0", "y1", "xh"), ("z1", "z0", "y1", "y0", "xh"))


def layer_kernel(x_h, g_h, gain1, gain2, qg, kg, wq_h, wk_h, wv_h, wo_h, wg_h, wu_h, wd_h, cos_h, sin_h,
                 block_ref, tok_ref, gains_ref, down_o, gate_o, up_o, out_o, q_o, k_o, v_o, p_h, mrecv0,
                 x, n1, n2, g2, wq, wk, wv, wo, wgt, wut, wdt, low_a, low_b, ra1, ra2, ra3, rb1, rb2, rb3, hidden,
                 qkv_s, qkv_r, mix_s, mix_r, gm_r, dqkv_r, dkv, mix, proj, gqkv, mid_ref, gmid, x_own, cosv, sinv,
                 macc, mrecv1, mrecv2, mrecv3, xsend, xrecv,
                 areca0, areca1, areca2, areca3, areca4, arecb0, arecb1, arecb2, arecb3, arecb4, gpart, gs0, gs1, gs2,
                 lsem, psem, s_qkv, s_mix, s_gm, s_dqkv, s_out, s_n2, s_gn2, s_feed, s_gb, s_blk, s_gn1, s_tok, g_sem,
                 mss, mrs, stsem, xs, ass, ars, bss, brs, gsem0, gsem1, gsem2):
    me = me_place()
    ctx = lax.axis_index("context")
    pair = pair_bit(me[0])
    half = pl.multiple_of(pair * 768, 256)

    def load(i, src, dst):
        return pltpu.make_async_copy(src, dst, lsem.at[i])

    first = [load(0, x_h, x), load(1, wk_h, wk), load(2, wv_h, wv),
             load(3, cos_h.at[rows_at(ctx * 128, 128)], cosv), load(4, sin_h.at[rows_at(ctx * 128, 128)], sinv),
             load(5, wq_h, wq), load(6, wo_h, wo)]
    homes = [rows_at(j * 256 + pair * 128, 128) for j in range(2)]
    first += [load(7 + j, g_h.at[pl.ds(j * 128, 128)], g2.at[homes[j]]) for j in range(2)]
    down_load = load(9, wd_h.at[pl.ds(half, 768)], wdt)
    tiles = []
    for i in range(3):
        c = pl.ds(pl.multiple_of(half + i * 256, 256), 256)
        tiles.append((load(10 + i, wg_h.at[:, c], wgt.at[i]), load(13 + i, wu_h.at[:, c], wut.at[i])))
    for cp in first:
        cp.start()
    bar = pltpu.get_barrier_semaphore()
    for d in range(1, 8):
        pl.semaphore_signal(bar, inc=1, device_id=(me[0], (ctx + d) % 8, me[3]), device_id_type=MESH)
    for d in range(1, 4):
        pl.semaphore_signal(bar, inc=1, device_id=(me[0], ctx, (me[3] + d) % 4), device_id_type=MESH)
        pl.semaphore_signal(bar, inc=1, device_id=((me[0] + d) % 4, ctx, me[3]), device_id_type=MESH)

    first[0].wait()
    g1 = row_of(gain1)

    def norm_rows(i, _):
        r = pl.ds(pl.multiple_of(i * 32, 32), 32)
        xv = x[r, :].astype(F32)
        inv = lax.rsqrt(jnp.mean(xv * xv, axis=-1, keepdims=True) + EPSILON)
        n1[r, :] = (xv * inv * g1).astype(BF)
        return 0

    lax.fori_loop(0, 8, norm_rows, 0)
    for j in range(2):
        x_own[j * 32:(j + 1) * 32, :] = x[own_rows(me, j, False), :]
    for i in (1, 2, 3, 4):
        first[i].wait()
    cos2 = jnp.concatenate([cosv[...], cosv[...]], axis=0)
    sin2 = jnp.concatenate([sinv[...], sinv[...]], axis=0)
    gqf, gkf = row_of(qg), row_of(kg)

    def turned(v, gain):
        hat = v * lax.rsqrt(jnp.mean(v * v, axis=-1, keepdims=True) + EPSILON) * gain
        return (hat * cos2 + half_turn(hat) * sin2).astype(BF)

    def spread(first, width, heads, value):
        for s in range(2):
            for h in range(4):
                c = h * width // 4 * 128
                qkv_s[s * 4 + h, :, first:first + 128] = value[s * 128:(s + 1) * 128, c:c + 128]

    kp = dot(n1[...], wk[...])
    proj[:, 512:768] = kp
    spread(128, 2, 2, jnp.concatenate([turned(kp[:, h * 128:(h + 1) * 128], gkf) for h in range(2)], axis=1))
    spread(256, 2, 2, dot(n1[...], wv[...]).astype(BF))
    first[5].wait()
    qp = dot(n1[...], wq[...])
    proj[:, 0:512] = qp
    spread(0, 4, 4, jnp.concatenate([turned(qp[:, h * 128:(h + 1) * 128], gqf) for h in range(4)], axis=1))
    pl.semaphore_wait(bar, 13)
    swap_qkv = ContextSwap(me, qkv_s, qkv_r, s_qkv)
    swap_qkv.start()
    g_copies = [remote(g2.at[homes[j]], g2.at[homes[j]], g_sem.at[0, j], g_sem.at[1, j], partner(me, "y0")) for j in range(2)]
    for j in range(2):
        first[7 + j].wait()
        g_copies[j].start()
    down_load.start()
    for pair_loads in tiles:
        for cp in pair_loads:
            cp.start()
    first[6].wait()
    swap_qkv.wait()

    def part(ref, n, first):
        return ref[0:n * 2, :, first:first + 128].reshape(n * 256, 128)

    def prob_home(i, j):
        n = i * 4 + j
        return (n // 2, slice((n % 2) * 256, (n % 2 + 1) * 256))

    seen = lax.broadcasted_iota(jnp.int32, (256, 256), 0) >= lax.broadcasted_iota(jnp.int32, (256, 256), 1)
    for i in range(4):
        q = qkv_r[2 * i:2 * i + 2, :, 0:128].reshape(256, 128)
        scores = dot_nt(q, part(qkv_r, i + 1, 128)) * SCALE
        last = jnp.where(seen, scores[:, i * 256:], -1e30)
        scores = last if i == 0 else jnp.concatenate([scores[:, :i * 256], last], axis=1)
        e = jnp.exp(scores - jnp.max(scores, axis=-1, keepdims=True))
        prob = (e / jnp.sum(e, axis=-1, keepdims=True)).astype(BF)
        for j in range(i + 1):
            hidden[prob_home(i, j)] = prob[:, j * 256:(j + 1) * 256]
        mix_s[2 * i:2 * i + 2] = dot(prob, part(qkv_r, i + 1, 256)).astype(BF).reshape(2, 128, 128)
    swap_mix = ContextSwap(me, mix_s, mix_r, s_mix)
    swap_mix.start()
    p_out = pltpu.make_async_copy(hidden.at[pl.ds(0, 8)], p_h, psem.at[0])
    p_out.start()
    for cp in g_copies:
        cp.wait_recv()
    down_load.wait()
    swap_mix.wait()
    for p in range(8):
        mix[(p // 4) * 128:(p // 4 + 1) * 128, (p % 4) * 128:(p % 4 + 1) * 128] = mix_r[p]

    sum_o = GroupSum(me, low_a.at[0:256], (ra1, ra2), s_out, False)
    for j in range(2):
        for n in range(4):
            c = slice(n * 512, (n + 1) * 512)
            low_a[j * 128:(j + 1) * 128, c] = dot(mix[j * 128:(j + 1) * 128, :], wo[:, c]).astype(BF)
        sum_o.send(j)
    p_out.wait()
    for i in range(3):
        hidden[6 + i] = dot_nt(g2[...], wdt[i * 256:(i + 1) * 256, :]).astype(BF)
    for j in range(2):
        sum_o.step(j, 0)
    gather_n = Gather(me, n2, s_n2, True)
    scale2 = row_of(gain2)

    def halves(j):
        return slice(j * 32, (j + 1) * 32)

    for j in range(2):
        mid = x_own[halves(j), :].astype(F32) + sum_o.step(j, 1)
        mid_ref[halves(j), :] = mid
        inv = lax.rsqrt(jnp.mean(mid * mid, axis=-1, keepdims=True) + EPSILON)
        n2[own_rows(me, j, True), :] = (mid * inv * scale2).astype(BF)
        gather_n.start(j)
    for i in range(3):
        for cp in tiles[i]:
            cp.wait()
    sum_o.finish()
    sum2 = GroupSum(me, low_a, (ra1, ra2, ra3), s_gn2, True)
    sumf = GroupSum(me, low_b, (rb1, rb2, rb3), s_feed, True)
    for j in range(2):
        gather_n.relay(j)
    for j in range(2):
        gather_n.wait(j)
        r = slice(j * 256, (j + 1) * 256)
        for i in range(3):
            gate = dot(n2[r, :], wgt[i])
            up = dot(n2[r, :], wut[i])
            gh = hidden[6 + i, r, :].astype(F32)
            sig = 1.0 / (1.0 + jnp.exp(-gate))
            silu = gate * sig
            hidden[i, r, :] = (silu * up).astype(BF)
            hidden[3 + i, r, :] = (gh * up * sig * (1.0 + gate * (1.0 - sig))).astype(BF)
            hidden[6 + i, r, :] = (gh * silu).astype(BF)
        for n in range(4):
            c = slice(n * 512, (n + 1) * 512)
            v = dot_nt(hidden[3, r, :], wgt[0, c, :]) + dot_nt(hidden[6, r, :], wut[0, c, :])
            for i in (1, 2):
                v = v + dot_nt(hidden[3 + i, r, :], wgt[i, c, :]) + dot_nt(hidden[6 + i, r, :], wut[i, c, :])
            low_a[r, c] = v.astype(BF)
        sum2.send(j)

    mlp, slot = [], {}
    for n, (k, i, dims) in enumerate(MLP_PIECES):
        slot[k, i] = n
        out = (down_o, gate_o, up_o)[k]

        def emit(m, v, out=out, i=i, n=n):
            if m == 0:
                out[pair, :, i * 256:(i + 1) * 256] = v
            else:
                xsend[n] = v.astype(BF)

        mlp.append(Piece(me, lambda r, n=n: macc.at[n, r], dims, ("y0",),
                         (mrecv0.at[n], mrecv1.at[n], mrecv2.at[n], mrecv3.at[n]), mss.at[n], mrs.at[n], emit,
                         [n2.at[:, pl.ds((n % 4) * 512 + a, 256)] for a in (0, 256)], stsem.at[n % 4]))
    four = range(4)

    def outer(left, k, n):
        t = left[:, n * 512:(n + 1) * 512].T
        for weight in k:
            for i in range(3):
                mlp[slot[weight, i]].put(n, dot(t, hidden[weight * 3 + i]).astype(BF))

    for n in four:
        outer(g2, (0,), n)
        if n % 2:
            sum2.step(n // 2, 0)
    for piece in (mlp[0], mlp[1], mlp[4]):
        piece.send(0)
    for n in four:
        outer(n2, (1, 2), n)
        if n % 2:
            sum2.step(n // 2, 1)
    for piece in mlp[2:4] + mlp[5:9]:
        piece.send(0)
    p_in = pltpu.make_async_copy(p_h, hidden.at[pl.ds(0, 8)], psem.at[1])
    for n in four:
        c = slice(n * 512, (n + 1) * 512)
        v = dot(hidden[0], wdt[0:256, c])
        for i in (1, 2):
            v = v + dot(hidden[i], wdt[i * 256:(i + 1) * 256, c])
        low_b[:, c] = v.astype(BF)
    p_in.start()

    gb = x
    gather_b = Gather(me, gb, s_gb, False)
    gain_term = jnp.zeros((1, 2048), F32)
    for j in range(2):
        mid = mid_ref[halves(j), :]
        inv = lax.rsqrt(jnp.mean(mid * mid, axis=-1, keepdims=True) + EPSILON)
        hat = mid * inv
        grad = sum2.step(j, 2)
        gain_term = gain_term + jnp.sum(grad * hat, axis=0, keepdims=True)
        u = grad * scale2
        grad = g2[own_rows(me, j, True), :].astype(F32) + inv * (u - hat * jnp.mean(u * hat, axis=-1, keepdims=True))
        gmid[halves(j), :] = grad
        gb[own_rows(me, j, False), :] = grad.astype(BF)
        gather_b.start(j)
    gpart[...] = jnp.zeros((40, 128), F32)

    def put_gain(row, value):
        for i in range(value.shape[1] // 128):
            gpart[row + i:row + i + 1, :] = value[:, i * 128:(i + 1) * 128]

    put_gain(16, gain_term)
    for j in range(2):
        gather_b.relay(j)
    for j in range(2):
        gather_b.wait(j)

    swap_mix.finish()
    gm_s = mix_s
    for b in range(2):
        gmix = dot_nt(gb[...], wo[b * 256:(b + 1) * 256, :]).astype(BF)
        for s in range(2):
            for h in range(2):
                gm_s[s * 4 + b * 2 + h] = gmix[s * 128:(s + 1) * 128, h * 128:(h + 1) * 128]
    swap_gm = ContextSwap(me, gm_s, gm_r, s_gm)
    swap_gm.start()
    for j in range(2):
        sumf.send(j)
    gather_n.finish()
    att_a, att_b = [], []
    spots = [(lambda r, i=i: wut.at[1 + i // 2, r, pl.ds((i % 2) * 128, 128)]) for i in range(4)]
    spots += [(lambda r, i=i: (wgt.at[i, r] if i < 3 else wut.at[0, r])) for i in range(4)]
    for i in range(4):
        def emit_a(m, v, i=i):
            out_o[:, i * 128:(i + 1) * 128] = v

        def emit_b(m, v, i=i):
            (q_o, q_o, k_o, v_o)[i][:, (i * 256 if i == 1 else 0):(i * 256 if i == 1 else 0) + 256] = v

        att_a.append(Piece(me, spots[i], OUT_ORDERS[i], (), tuple(r.at[i] for r in (areca0, areca1, areca2, areca3, areca4)),
                           ass.at[i], ars.at[i], emit_a))
        att_b.append(Piece(me, spots[4 + i], QKV_ORDERS[i], (), tuple(r.at[i] for r in (arecb0, arecb1, arecb2, arecb3, arecb4)),
                           bss.at[i], brs.at[i], emit_b))
    for j in four:
        c = slice(j * 512, (j + 1) * 512)
        v = dot(gb[:, c].T, mix[...]).astype(BF)
        for i in range(4):
            att_a[i].put(j, v[:, i * 128:(i + 1) * 128])
    for j in range(2):
        sumf.step(j, 0)
    for piece in att_a:
        piece.send(0)
    p_in.wait()
    swap_qkv.finish()
    swap_gm.wait()
    for i in range(4):
        n = (i + 1) * 256
        gm = gm_r[2 * i:2 * i + 2].reshape(256, 128)
        prob = jnp.concatenate([hidden[prob_home(i, j)] for j in range(i + 1)], axis=1)
        gp = dot_nt(gm, part(qkv_r, i + 1, 256))
        prob32 = prob.astype(F32)
        gs = (prob32 * (gp - jnp.sum(prob32 * gp, axis=-1, keepdims=True))).astype(BF)
        q = qkv_r[2 * i:2 * i + 2, :, 0:128].reshape(256, 128)
        qkv_s[2 * i:2 * i + 2, :, 0:128] = (dot(gs, part(qkv_r, i + 1, 128)) * SCALE).astype(BF).reshape(2, 128, 128)
        gk = dot_tn(gs, q)
        gv = dot_tn(prob, gm)
        if i:
            dkv[0:n - 256, 0:128] += gk[0:n - 256]
            dkv[0:n - 256, 128:256] += gv[0:n - 256]
        dkv[n - 256:n, 0:128] = gk[n - 256:n]
        dkv[n - 256:n, 128:256] = gv[n - 256:n]
    qkv_s[:, :, 128:256] = (dkv[:, 0:128] * SCALE).astype(BF).reshape(8, 128, 128)
    qkv_s[:, :, 256:384] = dkv[:, 128:256].astype(BF).reshape(8, 128, 128)
    swap_dqkv = ContextSwap(me, qkv_s, dqkv_r, s_dqkv)
    swap_dqkv.start()
    for j in range(2):
        sumf.step(j, 1)
    advance(mlp[0:2], 0)
    advance(mlp[2:4], 0)
    advance(mlp[4:6], 0)

    def through_norm(grad_rot, pre, gain):
        grad_normed = grad_rot * cos2 - half_turn(grad_rot) * sin2
        inv = lax.rsqrt(jnp.mean(pre * pre, axis=-1, keepdims=True) + EPSILON)
        hat = pre * inv
        u = grad_normed * gain
        grad_pre = inv * (u - hat * jnp.mean(u * hat, axis=-1, keepdims=True))
        return grad_pre.astype(BF), jnp.sum(grad_normed * hat, axis=0, keepdims=True)

    def arrived(first, heads):
        rows = []
        for s in range(2):
            v = dqkv_r[s * 4 + heads[0], :, first:first + 128].astype(F32)
            for h in heads[1:]:
                v = v + dqkv_r[s * 4 + h, :, first:first + 128].astype(F32)
            rows.append(v)
        return jnp.concatenate(rows, axis=0)

    swap_dqkv.wait()
    gain_sum = jnp.zeros((1, 128), F32)
    for h in range(4):
        c = slice(h * 128, (h + 1) * 128)
        gqkv[:, c], term = through_norm(arrived(0, (h,)), proj[:, c], gqf)
        gain_sum = gain_sum + term
    put_gain(32, gain_sum)
    gain_sum = jnp.zeros((1, 128), F32)
    for h in range(2):
        c = slice(512 + h * 128, 640 + h * 128)
        gqkv[:, c], term = through_norm(arrived(128, (2 * h, 2 * h + 1)), proj[:, c], gkf)
        gain_sum = gain_sum + term
        gqkv[:, 768 + h * 128:896 + h * 128] = arrived(256, (2 * h, 2 * h + 1)).astype(BF)
    put_gain(33, gain_sum)

    for n in four:
        c = slice(n * 512, (n + 1) * 512)
        v = dot(n1[:, c].T, gqkv[...]).astype(BF)
        for i in range(4):
            att_b[i].put(n, v[:, i * 256:(i + 1) * 256])
    for piece in att_b:
        piece.send(0)
    sum2.finish()
    sum1 = GroupSum(me, low_a.at[0:256], (ra1, ra2), s_gn1, False)
    for j in range(2):
        r = slice(j * 128, (j + 1) * 128)
        for n in four:
            c = slice(n * 512, (n + 1) * 512)
            v = dot_nt(gqkv[r, 0:512], wq[c, :]) + dot_nt(gqkv[r, 512:768], wk[c, :]) + dot_nt(gqkv[r, 768:1024], wv[c, :])
            low_a[r, c] = v.astype(BF)
        sum1.send(j)
    advance(mlp[6:7], 0)
    for j in range(2):
        sum1.step(j, 0)
    advance(mlp[0:2] + mlp[4:5], 1)
    advance(mlp[7:8], 0)
    scale1 = row_of(gain1)
    gather_t = Gather(me, tok_ref, s_tok, False)
    gain_term = jnp.zeros((1, 2048), F32)
    for j in range(2):
        xo = x_own[halves(j), :].astype(F32)
        inv = lax.rsqrt(jnp.mean(xo * xo, axis=-1, keepdims=True) + EPSILON)
        hat = xo * inv
        grad = sum1.step(j, 1)
        gain_term = gain_term + jnp.sum(grad * hat, axis=0, keepdims=True)
        u = grad * scale1
        tok_ref[own_rows(me, j, False), :] = (
            gmid[halves(j), :] + inv * (u - hat * jnp.mean(u * hat, axis=-1, keepdims=True))).astype(BF)
        gather_t.start(j)
    put_gain(0, gain_term)
    gains = GainSum(me, (gs0, gs1, gs2), (gsem0, gsem1, gsem2))
    gains.start(0, gpart[...])
    swap = [remote(xsend.at[n], xrecv.at[n], xs.at[n, 0], xs.at[n, 1], partner(me, "y0")) for n in range(9)]

    def complete(first, last):
        advance(mlp[first:last], 3)
        for cp in swap[first:last]:
            cp.start()

    advance(mlp[2:4] + mlp[5:6], 1)
    advance(att_a, 0)
    gains.start(1, gains.take(0))
    for j in range(2):
        gather_t.relay(j)
    advance(mlp[0:2], 2)
    advance(mlp[6:8], 1)
    advance(mlp[8:9], 0)
    advance(att_b[0:1], 0)
    advance(att_b[2:4], 0)
    advance(att_a, 1)
    gains.start(2, gains.take(1))
    advance(mlp[2:6], 2)
    gather_o = Gather(me, block_ref, s_blk, False)
    for j in range(2):
        block_ref[own_rows(me, j, False), :] = (mid_ref[halves(j), :] + sumf.step(j, 2)).astype(BF)
        gather_o.start(j)
    complete(0, 2)
    advance(att_b[1:2], 0)
    advance(mlp[8:9], 1)
    advance(att_b[0:1] + att_b[2:4], 1)
    advance(mlp[6:8], 2)
    advance(att_a, 2)
    complete(2, 6)
    for j in range(2):
        gather_o.relay(j)
    advance(att_b[1:2], 1)
    advance(mlp[8:9], 2)
    advance(att_b, 2)
    complete(6, 9)
    advance(att_a, 3)
    advance(att_b, 3)
    advance(att_a, 4)
    advance(att_b, 4)
    gains_ref[...] = gains.take(2)
    for n, cp in enumerate(swap):
        cp.wait_recv()
        k, i, _ = MLP_PIECES[n]
        (down_o, gate_o, up_o)[k][1 - pair, :, i * 256:(i + 1) * 256] = xrecv[n].astype(F32)

    for cp in swap:
        cp.wait_send()
    for gather in (gather_b, gather_o, gather_t):
        gather.finish()
    for gather in (gather_o, gather_t):
        for j in range(2):
            gather.wait(j)
    gains.finish()
    sum1.finish()
    for cp in g_copies:
        cp.wait_send()
    swap_gm.finish()
    swap_dqkv.finish()
    sumf.finish()
    for piece in mlp + att_a + att_b:
        piece.finish()


def layer(x, g, gain1, gain2, qg, kg, wq, wk, wv, wo, wg, wu, wd):
    cos_t, sin_t = rope_constants()
    V = pl.BlockSpec(memory_space=pltpu.VMEM)
    A = pl.BlockSpec(memory_space=pl.ANY)
    S = jax.ShapeDtypeStruct
    D = pltpu.SemaphoreType.DMA
    M = pltpu.VMEM
    return pl.pallas_call(
        layer_kernel,
        out_shape=(S((256, 2048), BF), S((256, 2048), BF), S((40, 128), F32),
                   S((2, 64, 768), F32), S((2, 64, 768), F32), S((2, 64, 768), F32), S((64, 512), F32), S((64, 512), F32),
                   S((64, 256), F32), S((64, 256), F32), S((8, 512, 256), BF), S((9, 1024, 256), BF)),
        in_specs=[A, A, V, V, V, V] + [A] * 9,
        out_specs=(V,) * 10 + (A, A),
        scratch_shapes=[
            M((256, 2048), BF), M((256, 2048), BF), M((512, 2048), BF), M((512, 2048), BF),
            M((2048, 512), BF), M((2048, 256), BF), M((2048, 256), BF), M((512, 2048), BF),
            M((3, 2048, 256), BF), M((3, 2048, 256), BF), M((768, 2048), BF),
            M((512, 2048), BF), M((512, 2048), BF),
            M((2, 4, 32, 2048), BF), M((2, 2, 32, 2048), BF), M((2, 1, 32, 2048), BF),
            M((2, 4, 32, 2048), BF), M((2, 2, 32, 2048), BF), M((2, 1, 32, 2048), BF), M((9, 512, 256), BF),
            M((8, 128, 384), BF), M((8, 128, 384), BF), M((8, 128, 128), BF), M((8, 128, 128), BF),
            M((8, 128, 128), BF), M((8, 128, 384), BF), M((1024, 256), F32), M((256, 512), BF), M((256, 768), F32),
            M((256, 1024), BF), M((64, 2048), F32), M((64, 2048), F32),
            M((64, 2048), BF), M((128, 128), F32), M((128, 128), F32),
            M((9, 2048, 256), BF), M((9, 512, 256), BF), M((9, 256, 256), BF), M((9, 128, 256), BF),
            M((9, 64, 256), BF), M((9, 64, 256), BF)]
        + [M((4, 1024 >> s, 128), BF) for s in range(5)] + [M((4, 1024 >> s, 256), BF) for s in range(5)]
        + [M((40, 128), F32), M((4, 40, 128), F32), M((8, 40, 128), F32), M((4, 40, 128), F32),
           D((16,)), D((2,)), D((2, 8)), D((2, 8)), D((2, 8)), D((2, 8)), D((2, 2, 2, 2)), D((2, 9, 2)), D((3, 2, 4, 2)),
           D((3, 2, 4, 2)), D((2, 3, 2)), D((2, 3, 2)), D((2, 2, 2, 2)), D((2, 3, 2)), D((2, 2)),
           D((9, 4)), D((9, 4)), D((4, 2)), D((9, 2)), D((4, 5)), D((4, 5)), D((4, 5)), D((4, 5)),
           D((2, 4)), D((2, 8)), D((2, 4))],
        compiler_params=pltpu.CompilerParams(collective_id=3, has_side_effects=True, vmem_limit_bytes=127 * 2**19),
    )(x, g, gain1, gain2, qg, kg, wq, wk, wv, wo, wg, wu, wd, jnp.asarray(cos_t), jnp.asarray(sin_t))


def tail_kernel(block_h, tok_h, gains, down_h, gate_h, up_h, out_h, q_h, k_h, v_h,
                block_o, tok_o, gain1_o, q_o, k_o, v_o, qg_o, kg_o, out_o, gain2_o, gate_o, up_o, down_o, sems):
    pairs = [(block_h, block_o), (tok_h, tok_o), (q_h, q_o), (k_h, k_o), (v_h, v_o), (out_h, out_o)]
    for i in range(2):
        c = pl.ds(i * 768, 768)
        pairs += [(down_h.at[i], down_o.at[:, c]), (gate_h.at[i], gate_o.at[:, c]), (up_h.at[i], up_o.at[:, c])]
    copies = [pltpu.make_async_copy(s, d, sems.at[i]) for i, (s, d) in enumerate(pairs)]
    for cp in copies:
        cp.start()
    gain1_o[...] = gains[0:16]
    gain2_o[...] = gains[16:32]
    qg_o[...] = gains[32:33]
    kg_o[...] = gains[33:34]
    for cp in copies:
        cp.wait()


def tail(block, tok, gains, down, gate, up, out, q, k, v):
    V = pl.BlockSpec(memory_space=pltpu.VMEM)
    A = pl.BlockSpec(memory_space=pl.ANY)
    S = jax.ShapeDtypeStruct
    return pl.pallas_call(
        tail_kernel,
        out_shape=(S((256, 2048), BF), S((256, 2048), BF), S((16, 128), F32), S((64, 512), F32), S((64, 256), F32),
                   S((64, 256), F32), S((1, 128), F32), S((1, 128), F32), S((64, 512), F32), S((16, 128), F32),
                   S((64, 1536), F32), S((64, 1536), F32), S((64, 1536), F32)),
        in_specs=[A, A, V, A, A, A, A, A, A, A],
        out_specs=(V,) * 13,
        scratch_shapes=[pltpu.SemaphoreType.DMA((12,))],
        compiler_params=pltpu.CompilerParams(vmem_limit_bytes=62 * 2**20),
    )(block, tok, gains, down, gate, up, out, q, k, v)


def local(tokens, attn_gain, w_query, w_key, w_value, query_gain, key_gain, w_out, mlp_gain, w_gate, w_up, w_down, out_grad):
    results = layer(tokens.reshape(256, 2048), out_grad.reshape(256, 2048), attn_gain, mlp_gain, query_gain, key_gain,
                    w_query, w_key, w_value, w_out, w_gate, w_up, w_down)
    block, tok, g1, q, k, v, qg, kg, out, g2, gate, up, down = tail(*results[:10])
    return (block.reshape(2, 128, 2048), tok.reshape(2, 128, 2048), g1.reshape(2048), q, k, v, qg.reshape(128),
            kg.reshape(128), out.T, g2.reshape(2048), gate, up, down.T)


def solution(mesh):
    in_specs = (
        P("dp", "context", None),
        P(),
        P(None, "tensor"),
        P(None, "tensor"),
        P(None, "tensor"),
        P(),
        P(),
        P("tensor", None),
        P(),
        P(None, "tensor"),
        P(None, "tensor"),
        P("tensor", None),
        P("dp", "context", None),
    )
    out_specs = (
        P("dp", "context", None),
        P("dp", "context", None),
        P(),
        P(("dp", "context"), "tensor"),
        P(("dp", "context"), "tensor"),
        P(("dp", "context"), "tensor"),
        P(),
        P(),
        P("tensor", ("dp", "context")),
        P(),
        P(("dp", "context"), "tensor"),
        P(("dp", "context"), "tensor"),
        P("tensor", ("dp", "context")),
    )
    return jax.shard_map(local, mesh=mesh, in_specs=in_specs, out_specs=out_specs, check_vma=False)
```

```python
import numpy as np
import jax
import jax.numpy as jnp
from jax import lax
from jax.experimental import pallas as pl
from jax.experimental.pallas import tpu as pltpu
from jax.sharding import PartitionSpec as P

MESH = pl.DeviceIdType.MESH
BF = jnp.bfloat16
F32 = jnp.float32
EPSILON = 1e-06
ROPE_BASE = 1000000.0
SCALE = 128 ** (-0.5)


def me_place():
    c = lax.axis_index("context")
    return (lax.axis_index("dp"), c // 2, c % 2, lax.axis_index("tensor"))


def dev(place):
    y, z, h, t = place
    return (y, z * 2 + h, t)


def flip4(v, which):
    return v + 1 - 2 * (v % 2) if which == "0" else 3 - v


def pair_bit(y):
    return ((y + 1) // 2) % 2


def partner(place, dim):
    y, z, h, t = place
    if dim == "core":
        return (y, z, h, t + 1 - 2 * (t % 2))
    if dim == "xl":
        return (y, z, h, (t + 2) % 4)
    if dim == "xh":
        return (y, z, 1 - h, t)
    if dim[0] == "y":
        return (flip4(y, dim[1]), z, h, t)
    return (y, flip4(z, dim[1]), h, t)


def dot(a, b):
    return jnp.dot(a, b, preferred_element_type=F32)


def dot_nt(a, b):
    return lax.dot_general(a, b, (((1,), (1,)), ((), ())), preferred_element_type=F32)


def dot_tn(a, b):
    return lax.dot_general(a, b, (((0,), (0,)), ((), ())), preferred_element_type=F32)


def row_of(ref):
    return ref[...].astype(F32).reshape(1, -1)


def rows_at(start, n):
    return pl.ds(pl.multiple_of(start, min(n, 64)), n)


def own_rows(place, chunk, wide):
    y, _, _, t = place
    return rows_at(chunk * 256 + pair_bit(y) * 128 + t * 32 if wide else chunk * 128 + t * 32, 32)


def remote(src, dst, send_sem, recv_sem, place):
    return pltpu.make_async_remote_copy(src_ref=src, dst_ref=dst, send_sem=send_sem, recv_sem=recv_sem,
                                        device_id=dev(place), device_id_type=MESH)


def wait_bytes(view, sem):
    pltpu.make_async_copy(view, view, sem).wait()


def subsets(dims, place):
    found = [place]
    for dim in dims:
        found = found + [partner(p, dim) for p in found]
    return found


class GroupSum:
    def __init__(self, me, low, recvs, sems, wide):
        self.me, self.low, self.recvs, self.sems, self.wide = me, low, recvs, sems, wide

    def order(self, j):
        if not self.wide:
            return ("core", "xl")
        return (("core", "xl", "y0"), ("core", "y0", "xl"))[j]

    def copies(self, j, s):
        dims = self.order(j)
        to = partner(self.me, dims[s])
        return [remote(self.low.at[own_rows(block, j, self.wide)], self.recvs[s].at[j, i],
                       self.sems.at[s, j, i, 0], self.sems.at[s, j, i, 1], to)
                for i, block in enumerate(subsets(dims[s + 1:], to))]

    def send(self, j, s=0):
        for cp in self.copies(j, s):
            cp.start()

    def step(self, j, s):
        dims = self.order(j)
        for cp in self.copies(j, s):
            cp.wait_recv()
        for i, block in enumerate(subsets(dims[s + 1:], self.me)):
            r = own_rows(block, j, self.wide)
            v = self.low[r, :].astype(F32) + self.recvs[s][j, i].astype(F32)
            if s == len(dims) - 1:
                return v
            self.low[r, :] = v.astype(BF)
        self.send(j, s + 1)

    def finish(self):
        for j in range(2):
            for s in range(len(self.order(j))):
                for cp in self.copies(j, s):
                    cp.wait_send()


class Gather:
    TENSOR = (((), "xl", 0, 2048), ((), "core", 0, 2048), (("xl",), "core", 0, 2048))
    PAIR = (((), "xl", 0, 2048), ((), "y0", 0, 2048), ((), "core", 0, 2048),
            (("y0",), "xl", 0, 1024), (("xl",), "y0", 1024, 1024),
            (("y0",), "core", 0, 2048), (("xl",), "core", 0, 2048),
            (("xl", "y0"), "core", 0, 1024), (("xl", "y0"), "core", 1024, 1024))

    def __init__(self, me, full, sems, wide):
        self.me, self.full, self.sems, self.wide = me, full, sems, wide
        self.moves = self.PAIR if wide else self.TENSOR

    def copy(self, j, i):
        via, dim, col, width = self.moves[i]
        block = self.me
        for d in via:
            block = partner(block, d)
        view = self.full.at[own_rows(block, j, self.wide), pl.ds(col, width)]
        return remote(view, view, self.sems.at[j, i, 0], self.sems.at[j, i, 1], partner(self.me, dim))

    def start(self, j):
        for i in range(3 if self.wide else 2):
            self.copy(j, i).start()

    def relay(self, j):
        if not self.wide:
            self.copy(j, 0).wait_recv()
            self.copy(j, 2).start()
            return
        for came, onward in ((1, (3, 5)), (0, (4, 6)), (3, (7,)), (4, (8,))):
            self.copy(j, came).wait_recv()
            for i in onward:
                self.copy(j, i).start()

    def wait(self, j):
        for i in (2, 5, 6, 7, 8) if self.wide else (1, 2):
            self.copy(j, i).wait_recv()

    def finish(self):
        for j in range(2):
            for i in range(len(self.moves)):
                self.copy(j, i).wait_send()


def dim_bit(place, dim):
    y, z, h, _ = place
    if dim == "xh":
        return h
    v = y if dim[0] == "y" else z
    return pair_bit(v) if dim[1] == "0" else v // 2


class Piece:
    def __init__(self, me, acc, order, keep, recvs, ssem, rsem, emit, stage=None, lsem=None):
        self.me, self.acc, self.order, self.keep, self.recvs = me, acc, order, keep, recvs
        self.ssem, self.rsem, self.emit, self.stage, self.lsem = ssem, rsem, emit, stage, lsem

    def put(self, y, value):
        dims = self.order + self.keep
        for z in range(4):
            for h in range(2):
                spot = 0
                for i, dim in enumerate(dims):
                    here = dim_bit(self.me, dim)
                    spot = spot + (1 - here if dim_bit((y, z, h, 0), dim) else here) * (1024 >> i)
                b = (z * 2 + h) * 64
                self.acc(rows_at(spot, 64))[...] = value[b:b + 64]

    def send(self, s):
        n = 1024 >> s
        remote(self.acc(pl.ds(n, n)), self.recvs[s], self.ssem.at[s], self.rsem.at[s], partner(self.me, self.order[s])).start()

    def arrived(self, s):
        wait_bytes(self.recvs[s], self.rsem.at[s])

    def loads(self):
        return [pltpu.make_async_copy(self.recvs[0].at[pl.ds(i * 512, 512)], self.stage[i], self.lsem.at[i]) for i in range(2)]

    def add(self, s):
        n = 1024 >> s
        if s == len(self.order) - 1:
            v = self.acc(pl.ds(0, n))[...].astype(F32) + self.recvs[s][...].astype(F32)
            for i in range(n // 64):
                self.emit(i, v[i * 64:(i + 1) * 64])
            return
        parts = [(0, n, self.recvs[s])]
        if s == 0 and self.stage is not None:
            parts = [(0, 512, self.stage[0]), (512, 512, self.stage[1])]
        for first, count, view in parts:
            step = min(count, 128)

            def body(m, _, first=first, step=step, view=view):
                acc = self.acc(rows_at(first + m * step, step))
                acc[...] = (acc[...].astype(F32) + view[rows_at(m * step, step), :].astype(F32)).astype(BF)
                return 0

            if count == step:
                body(0, 0)
            else:
                lax.fori_loop(0, count // step, body, 0)
        self.send(s + 1)

    def finish(self):
        for s in range(len(self.order)):
            wait_bytes(self.recvs[s], self.ssem.at[s])


def advance(pieces, s):
    if s or pieces[0].stage is None:
        for piece in pieces:
            piece.arrived(s)
            piece.add(s)
        return

    def fetch(piece):
        piece.arrived(0)
        for cp in piece.loads():
            cp.start()

    fetch(pieces[0])
    for i, piece in enumerate(pieces):
        if i + 1 < len(pieces):
            fetch(pieces[i + 1])
        for cp in piece.loads():
            cp.wait()
        piece.add(0)


class GainSum:
    def __init__(self, me, slots, sems):
        y, z, h, t = me
        self.axes = [(t, 4, lambda i: (y, z, h, i)),
                     (z * 2 + h, 8, lambda i: (y, i // 2, i % 2, t)),
                     (y, 4, lambda i: (i, z, h, t))]
        self.slots, self.sems = slots, sems

    def copies(self, s):
        here, n, place = self.axes[s]
        return [remote(self.slots[s].at[here], self.slots[s].at[here], self.sems[s].at[0, d], self.sems[s].at[1, d],
                       place((here + d) % n)) for d in range(1, n)]

    def start(self, s, value):
        self.slots[s][self.axes[s][0]] = value
        for cp in self.copies(s):
            cp.start()

    def take(self, s):
        for cp in self.copies(s):
            cp.wait_recv()
        total = self.slots[s][0]
        for i in range(1, self.axes[s][1]):
            total = total + self.slots[s][i]
        return total

    def finish(self):
        for s in range(3):
            for cp in self.copies(s):
                cp.wait_send()


class ContextSwap:
    def __init__(self, me, send, recv, sems):
        self.me, self.send, self.recv, self.sems = me, send, recv, sems
        self.ctx = me[1] * 2 + me[2]

    def copy(self, d):
        to = (self.ctx + d) % 8
        return remote(self.send.at[to], self.recv.at[self.ctx], self.sems.at[0, d], self.sems.at[1, d],
                      (self.me[0], to // 2, to % 2, self.me[3]))

    def start(self):
        for d in range(1, 8):
            self.copy(d).start()
        self.recv[self.ctx] = self.send[self.ctx]

    def wait(self):
        for d in range(1, 8):
            self.copy(d).wait_recv()

    def finish(self):
        for d in range(1, 8):
            self.copy(d).wait_send()


def rope_constants():
    frequency = np.float32(ROPE_BASE) ** (-np.arange(0, 128, 2).astype(np.float32) / np.float32(128))
    angles = np.arange(1024, dtype=np.float32)[:, None] * frequency.astype(np.float32)[None, :]
    cosine, sine = np.cos(angles), np.sin(angles)
    return (np.concatenate([cosine, cosine], 1).astype(np.float32),
            np.concatenate([-sine, sine], 1).astype(np.float32))


def half_turn(v):
    return pltpu.roll(v, 64, axis=1)


MLP_PIECES = ((0, 0, ("z0", "z1", "xh", "y1")), (0, 1, ("z1", "z0", "xh", "y1")),
              (1, 0, ("z0", "z1", "xh", "y1")), (1, 1, ("z1", "z0", "xh", "y1")),
              (0, 2, ("y1", "xh", "z0", "z1")), (1, 2, ("y1", "xh", "z1", "z0")),
              (2, 0, ("y1", "xh", "z0", "z1")), (2, 1, ("y1", "xh", "z1", "z0")),
              (2, 2, ("y1", "xh", "z0", "z1")))
OUT_ORDERS = (("y0", "z0", "z1", "y1", "xh"), ("y0", "z1", "z0", "y1", "xh"),
              ("y0", "z0", "y1", "z1", "xh"), ("y0", "z1", "y1", "z0", "xh"))
QKV_ORDERS = (("y0", "y1", "z0", "z1", "xh"), ("y1", "y0", "z1", "z0", "xh"),
              ("z0", "z1", "y0", "y1", "xh"), ("z1", "z0", "y1", "y0", "xh"))


def layer_kernel(x_h, g_h, gain1, gain2, qg, kg, wq_h, wk_h, wv_h, wo_h, wg_h, wu_h, wd_h, cos_h, sin_h,
                 block_ref, tok_ref, gains_ref, down_o, gate_o, up_o, out_o, q_o, k_o, v_o, p_h, mrecv0,
                 x, n1, n2, g2, wq, wk, wv, wo, wgt, wut, wdt, low_a, low_b, ra1, ra2, ra3, rb1, rb2, rb3, hidden,
                 qkv_s, qkv_r, mix_s, mix_r, gm_r, dqkv_r, dkv, mix, proj, gqkv, mid_ref, gmid, x_own, cosv, sinv,
                 macc, mrecv1, mrecv2, mrecv3, xsend, xrecv,
                 areca0, areca1, areca2, areca3, areca4, arecb0, arecb1, arecb2, arecb3, arecb4, gpart, gs0, gs1, gs2,
                 lsem, psem, s_qkv, s_mix, s_gm, s_dqkv, s_out, s_n2, s_gn2, s_feed, s_gb, s_blk, s_gn1, s_tok, g_sem,
                 mss, mrs, stsem, xs, ass, ars, bss, brs, gsem0, gsem1, gsem2):
    me = me_place()
    ctx = lax.axis_index("context")
    pair = pair_bit(me[0])
    half = pl.multiple_of(pair * 768, 256)

    def load(i, src, dst):
        return pltpu.make_async_copy(src, dst, lsem.at[i])

    first = [load(0, x_h, x), load(1, wk_h, wk), load(2, wv_h, wv),
             load(3, cos_h.at[rows_at(ctx * 128, 128)], cosv), load(4, sin_h.at[rows_at(ctx * 128, 128)], sinv),
             load(5, wq_h, wq), load(6, wo_h, wo)]
    homes = [rows_at(j * 256 + pair * 128, 128) for j in range(2)]
    first += [load(7 + j, g_h.at[pl.ds(j * 128, 128)], g2.at[homes[j]]) for j in range(2)]
    down_load = load(9, wd_h.at[pl.ds(half, 768)], wdt)
    tiles = []
    for i in range(3):
        c = pl.ds(pl.multiple_of(half + i * 256, 256), 256)
        tiles.append((load(10 + i, wg_h.at[:, c], wgt.at[i]), load(13 + i, wu_h.at[:, c], wut.at[i])))
    for cp in first:
        cp.start()
    bar = pltpu.get_barrier_semaphore()
    for d in range(1, 8):
        pl.semaphore_signal(bar, inc=1, device_id=(me[0], (ctx + d) % 8, me[3]), device_id_type=MESH)
    for d in range(1, 4):
        pl.semaphore_signal(bar, inc=1, device_id=(me[0], ctx, (me[3] + d) % 4), device_id_type=MESH)
        pl.semaphore_signal(bar, inc=1, device_id=((me[0] + d) % 4, ctx, me[3]), device_id_type=MESH)

    first[0].wait()
    g1 = row_of(gain1)

    def norm_rows(i, _):
        r = pl.ds(pl.multiple_of(i * 32, 32), 32)
        xv = x[r, :].astype(F32)
        inv = lax.rsqrt(jnp.mean(xv * xv, axis=-1, keepdims=True) + EPSILON)
        n1[r, :] = (xv * inv * g1).astype(BF)
        return 0

    lax.fori_loop(0, 8, norm_rows, 0)
    for j in range(2):
        x_own[j * 32:(j + 1) * 32, :] = x[own_rows(me, j, False), :]
    for i in (1, 2, 3, 4):
        first[i].wait()
    cos2 = jnp.concatenate([cosv[...], cosv[...]], axis=0)
    sin2 = jnp.concatenate([sinv[...], sinv[...]], axis=0)
    gqf, gkf = row_of(qg), row_of(kg)

    def turned(v, gain):
        hat = v * lax.rsqrt(jnp.mean(v * v, axis=-1, keepdims=True) + EPSILON) * gain
        return (hat * cos2 + half_turn(hat) * sin2).astype(BF)

    def spread(first, width, heads, value):
        for s in range(2):
            for h in range(4):
                c = h * width // 4 * 128
                qkv_s[s * 4 + h, :, first:first + 128] = value[s * 128:(s + 1) * 128, c:c + 128]

    kp = dot(n1[...], wk[...])
    proj[:, 512:768] = kp
    spread(128, 2, 2, jnp.concatenate([turned(kp[:, h * 128:(h + 1) * 128], gkf) for h in range(2)], axis=1))
    spread(256, 2, 2, dot(n1[...], wv[...]).astype(BF))
    first[5].wait()
    qp = dot(n1[...], wq[...])
    proj[:, 0:512] = qp
    spread(0, 4, 4, jnp.concatenate([turned(qp[:, h * 128:(h + 1) * 128], gqf) for h in range(4)], axis=1))
    pl.semaphore_wait(bar, 13)
    swap_qkv = ContextSwap(me, qkv_s, qkv_r, s_qkv)
    swap_qkv.start()
    g_copies = [remote(g2.at[homes[j]], g2.at[homes[j]], g_sem.at[0, j], g_sem.at[1, j], partner(me, "y0")) for j in range(2)]
    for j in range(2):
        first[7 + j].wait()
        g_copies[j].start()
    down_load.start()
    for pair_loads in tiles:
        for cp in pair_loads:
            cp.start()
    first[6].wait()
    swap_qkv.wait()

    def part(ref, n, first):
        return ref[0:n * 2, :, first:first + 128].reshape(n * 256, 128)

    def prob_home(i, j):
        n = i * 4 + j
        return (n // 2, slice((n % 2) * 256, (n % 2 + 1) * 256))

    seen = lax.broadcasted_iota(jnp.int32, (256, 256), 0) >= lax.broadcasted_iota(jnp.int32, (256, 256), 1)
    for i in range(4):
        q = qkv_r[2 * i:2 * i + 2, :, 0:128].reshape(256, 128)
        scores = dot_nt(q, part(qkv_r, i + 1, 128)) * SCALE
        last = jnp.where(seen, scores[:, i * 256:], -1e30)
        scores = last if i == 0 else jnp.concatenate([scores[:, :i * 256], last], axis=1)
        e = jnp.exp(scores - jnp.max(scores, axis=-1, keepdims=True))
        prob = (e / jnp.sum(e, axis=-1, keepdims=True)).astype(BF)
        for j in range(i + 1):
            hidden[prob_home(i, j)] = prob[:, j * 256:(j + 1) * 256]
        mix_s[2 * i:2 * i + 2] = dot(prob, part(qkv_r, i + 1, 256)).astype(BF).reshape(2, 128, 128)
    swap_mix = ContextSwap(me, mix_s, mix_r, s_mix)
    swap_mix.start()
    p_out = pltpu.make_async_copy(hidden.at[pl.ds(0, 8)], p_h, psem.at[0])
    p_out.start()
    for cp in g_copies:
        cp.wait_recv()
    down_load.wait()
    swap_mix.wait()
    for p in range(8):
        mix[(p // 4) * 128:(p // 4 + 1) * 128, (p % 4) * 128:(p % 4 + 1) * 128] = mix_r[p]

    sum_o = GroupSum(me, low_a.at[0:256], (ra1, ra2), s_out, False)
    for j in range(2):
        for n in range(4):
            c = slice(n * 512, (n + 1) * 512)
            low_a[j * 128:(j + 1) * 128, c] = dot(mix[j * 128:(j + 1) * 128, :], wo[:, c]).astype(BF)
        sum_o.send(j)
    p_out.wait()
    for i in range(3):
        hidden[6 + i] = dot_nt(g2[...], wdt[i * 256:(i + 1) * 256, :]).astype(BF)
    for j in range(2):
        sum_o.step(j, 0)
    gather_n = Gather(me, n2, s_n2, True)
    scale2 = row_of(gain2)

    def halves(j):
        return slice(j * 32, (j + 1) * 32)

    for j in range(2):
        mid = x_own[halves(j), :].astype(F32) + sum_o.step(j, 1)
        mid_ref[halves(j), :] = mid
        inv = lax.rsqrt(jnp.mean(mid * mid, axis=-1, keepdims=True) + EPSILON)
        n2[own_rows(me, j, True), :] = (mid * inv * scale2).astype(BF)
        gather_n.start(j)
    for i in range(3):
        for cp in tiles[i]:
            cp.wait()
    sum_o.finish()
    sum2 = GroupSum(me, low_a, (ra1, ra2, ra3), s_gn2, True)
    sumf = GroupSum(me, low_b, (rb1, rb2, rb3), s_feed, True)
    for j in range(2):
        gather_n.relay(j)
    for j in range(2):
        gather_n.wait(j)
        r = slice(j * 256, (j + 1) * 256)
        for i in range(3):
            gate = dot(n2[r, :], wgt[i])
            up = dot(n2[r, :], wut[i])
            gh = hidden[6 + i, r, :].astype(F32)
            sig = 1.0 / (1.0 + jnp.exp(-gate))
            silu = gate * sig
            hidden[i, r, :] = (silu * up).astype(BF)
            hidden[3 + i, r, :] = (gh * up * sig * (1.0 + gate * (1.0 - sig))).astype(BF)
            hidden[6 + i, r, :] = (gh * silu).astype(BF)
        for n in range(4):
            c = slice(n * 512, (n + 1) * 512)
            v = dot_nt(hidden[3, r, :], wgt[0, c, :]) + dot_nt(hidden[6, r, :], wut[0, c, :])
            for i in (1, 2):
                v = v + dot_nt(hidden[3 + i, r, :], wgt[i, c, :]) + dot_nt(hidden[6 + i, r, :], wut[i, c, :])
            low_a[r, c] = v.astype(BF)
        sum2.send(j)

    mlp, slot = [], {}
    for n, (k, i, dims) in enumerate(MLP_PIECES):
        slot[k, i] = n
        out = (down_o, gate_o, up_o)[k]

        def emit(m, v, out=out, i=i, n=n):
            if m == 0:
                out[pair, :, i * 256:(i + 1) * 256] = v
            else:
                xsend[n] = v.astype(BF)

        mlp.append(Piece(me, lambda r, n=n: macc.at[n, r], dims, ("y0",),
                         (mrecv0.at[n], mrecv1.at[n], mrecv2.at[n], mrecv3.at[n]), mss.at[n], mrs.at[n], emit,
                         [n2.at[:, pl.ds((n % 4) * 512 + a, 256)] for a in (0, 256)], stsem.at[n % 4]))
    four = range(4)

    def outer(left, k, n):
        t = left[:, n * 512:(n + 1) * 512].T
        for weight in k:
            for i in range(3):
                mlp[slot[weight, i]].put(n, dot(t, hidden[weight * 3 + i]).astype(BF))

    for n in four:
        outer(g2, (0,), n)
        if n % 2:
            sum2.step(n // 2, 0)
    for piece in (mlp[0], mlp[1], mlp[4]):
        piece.send(0)
    for n in four:
        outer(n2, (1, 2), n)
        if n % 2:
            sum2.step(n // 2, 1)
    for piece in mlp[2:4] + mlp[5:9]:
        piece.send(0)
    p_in = pltpu.make_async_copy(p_h, hidden.at[pl.ds(0, 8)], psem.at[1])
    for n in four:
        c = slice(n * 512, (n + 1) * 512)
        v = dot(hidden[0], wdt[0:256, c])
        for i in (1, 2):
            v = v + dot(hidden[i], wdt[i * 256:(i + 1) * 256, c])
        low_b[:, c] = v.astype(BF)
    p_in.start()

    gb = x
    gather_b = Gather(me, gb, s_gb, False)
    gain_term = jnp.zeros((1, 2048), F32)
    for j in range(2):
        mid = mid_ref[halves(j), :]
        inv = lax.rsqrt(jnp.mean(mid * mid, axis=-1, keepdims=True) + EPSILON)
        hat = mid * inv
        grad = sum2.step(j, 2)
        gain_term = gain_term + jnp.sum(grad * hat, axis=0, keepdims=True)
        u = grad * scale2
        grad = g2[own_rows(me, j, True), :].astype(F32) + inv * (u - hat * jnp.mean(u * hat, axis=-1, keepdims=True))
        gmid[halves(j), :] = grad
        gb[own_rows(me, j, False), :] = grad.astype(BF)
        gather_b.start(j)
    gpart[...] = jnp.zeros((40, 128), F32)

    def put_gain(row, value):
        for i in range(value.shape[1] // 128):
            gpart[row + i:row + i + 1, :] = value[:, i * 128:(i + 1) * 128]

    put_gain(16, gain_term)
    for j in range(2):
        gather_b.relay(j)
    for j in range(2):
        gather_b.wait(j)

    swap_mix.finish()
    gm_s = mix_s
    for b in range(2):
        gmix = dot_nt(gb[...], wo[b * 256:(b + 1) * 256, :]).astype(BF)
        for s in range(2):
            for h in range(2):
                gm_s[s * 4 + b * 2 + h] = gmix[s * 128:(s + 1) * 128, h * 128:(h + 1) * 128]
    swap_gm = ContextSwap(me, gm_s, gm_r, s_gm)
    swap_gm.start()
    for j in range(2):
        sumf.send(j)
    gather_n.finish()
    att_a, att_b = [], []
    spots = [(lambda r, i=i: wut.at[1 + i // 2, r, pl.ds((i % 2) * 128, 128)]) for i in range(4)]
    spots += [(lambda r, i=i: (wgt.at[i, r] if i < 3 else wut.at[0, r])) for i in range(4)]
    for i in range(4):
        def emit_a(m, v, i=i):
            out_o[:, i * 128:(i + 1) * 128] = v

        def emit_b(m, v, i=i):
            (q_o, q_o, k_o, v_o)[i][:, (i * 256 if i == 1 else 0):(i * 256 if i == 1 else 0) + 256] = v

        att_a.append(Piece(me, spots[i], OUT_ORDERS[i], (), tuple(r.at[i] for r in (areca0, areca1, areca2, areca3, areca4)),
                           ass.at[i], ars.at[i], emit_a))
        att_b.append(Piece(me, spots[4 + i], QKV_ORDERS[i], (), tuple(r.at[i] for r in (arecb0, arecb1, arecb2, arecb3, arecb4)),
                           bss.at[i], brs.at[i], emit_b))
    for j in four:
        c = slice(j * 512, (j + 1) * 512)
        v = dot(gb[:, c].T, mix[...]).astype(BF)
        for i in range(4):
            att_a[i].put(j, v[:, i * 128:(i + 1) * 128])
    for j in range(2):
        sumf.step(j, 0)
    for piece in att_a:
        piece.send(0)
    p_in.wait()
    swap_qkv.finish()
    swap_gm.wait()
    for i in range(4):
        n = (i + 1) * 256
        gm = gm_r[2 * i:2 * i + 2].reshape(256, 128)
        prob = jnp.concatenate([hidden[prob_home(i, j)] for j in range(i + 1)], axis=1)
        gp = dot_nt(gm, part(qkv_r, i + 1, 256))
        prob32 = prob.astype(F32)
        gs = (prob32 * (gp - jnp.sum(prob32 * gp, axis=-1, keepdims=True))).astype(BF)
        q = qkv_r[2 * i:2 * i + 2, :, 0:128].reshape(256, 128)
        qkv_s[2 * i:2 * i + 2, :, 0:128] = (dot(gs, part(qkv_r, i + 1, 128)) * SCALE).astype(BF).reshape(2, 128, 128)
        gk = dot_tn(gs, q)
        gv = dot_tn(prob, gm)
        if i:
            dkv[0:n - 256, 0:128] += gk[0:n - 256]
            dkv[0:n - 256, 128:256] += gv[0:n - 256]
        dkv[n - 256:n, 0:128] = gk[n - 256:n]
        dkv[n - 256:n, 128:256] = gv[n - 256:n]
    qkv_s[:, :, 128:256] = (dkv[:, 0:128] * SCALE).astype(BF).reshape(8, 128, 128)
    qkv_s[:, :, 256:384] = dkv[:, 128:256].astype(BF).reshape(8, 128, 128)
    swap_dqkv = ContextSwap(me, qkv_s, dqkv_r, s_dqkv)
    swap_dqkv.start()
    for j in range(2):
        sumf.step(j, 1)
    advance(mlp[0:2], 0)
    advance(mlp[2:4], 0)
    advance(mlp[4:6], 0)

    def through_norm(grad_rot, pre, gain):
        grad_normed = grad_rot * cos2 - half_turn(grad_rot) * sin2
        inv = lax.rsqrt(jnp.mean(pre * pre, axis=-1, keepdims=True) + EPSILON)
        hat = pre * inv
        u = grad_normed * gain
        grad_pre = inv * (u - hat * jnp.mean(u * hat, axis=-1, keepdims=True))
        return grad_pre.astype(BF), jnp.sum(grad_normed * hat, axis=0, keepdims=True)

    def arrived(first, heads):
        rows = []
        for s in range(2):
            v = dqkv_r[s * 4 + heads[0], :, first:first + 128].astype(F32)
            for h in heads[1:]:
                v = v + dqkv_r[s * 4 + h, :, first:first + 128].astype(F32)
            rows.append(v)
        return jnp.concatenate(rows, axis=0)

    swap_dqkv.wait()
    gain_sum = jnp.zeros((1, 128), F32)
    for h in range(4):
        c = slice(h * 128, (h + 1) * 128)
        gqkv[:, c], term = through_norm(arrived(0, (h,)), proj[:, c], gqf)
        gain_sum = gain_sum + term
    put_gain(32, gain_sum)
    gain_sum = jnp.zeros((1, 128), F32)
    for h in range(2):
        c = slice(512 + h * 128, 640 + h * 128)
        gqkv[:, c], term = through_norm(arrived(128, (2 * h, 2 * h + 1)), proj[:, c], gkf)
        gain_sum = gain_sum + term
        gqkv[:, 768 + h * 128:896 + h * 128] = arrived(256, (2 * h, 2 * h + 1)).astype(BF)
    put_gain(33, gain_sum)

    for n in four:
        c = slice(n * 512, (n + 1) * 512)
        v = dot(n1[:, c].T, gqkv[...]).astype(BF)
        for i in range(4):
            att_b[i].put(n, v[:, i * 256:(i + 1) * 256])
    for piece in att_b:
        piece.send(0)
    sum2.finish()
    sum1 = GroupSum(me, low_a.at[0:256], (ra1, ra2), s_gn1, False)
    for j in range(2):
        r = slice(j * 128, (j + 1) * 128)
        for n in four:
            c = slice(n * 512, (n + 1) * 512)
            v = dot_nt(gqkv[r, 0:512], wq[c, :]) + dot_nt(gqkv[r, 512:768], wk[c, :]) + dot_nt(gqkv[r, 768:1024], wv[c, :])
            low_a[r, c] = v.astype(BF)
        sum1.send(j)
    advance(mlp[6:7], 0)
    for j in range(2):
        sum1.step(j, 0)
    advance(mlp[0:2] + mlp[4:5], 1)
    advance(mlp[7:8], 0)
    scale1 = row_of(gain1)
    gather_t = Gather(me, tok_ref, s_tok, False)
    gain_term = jnp.zeros((1, 2048), F32)
    for j in range(2):
        xo = x_own[halves(j), :].astype(F32)
        inv = lax.rsqrt(jnp.mean(xo * xo, axis=-1, keepdims=True) + EPSILON)
        hat = xo * inv
        grad = sum1.step(j, 1)
        gain_term = gain_term + jnp.sum(grad * hat, axis=0, keepdims=True)
        u = grad * scale1
        tok_ref[own_rows(me, j, False), :] = (
            gmid[halves(j), :] + inv * (u - hat * jnp.mean(u * hat, axis=-1, keepdims=True))).astype(BF)
        gather_t.start(j)
    put_gain(0, gain_term)
    gains = GainSum(me, (gs0, gs1, gs2), (gsem0, gsem1, gsem2))
    gains.start(0, gpart[...])
    swap = [remote(xsend.at[n], xrecv.at[n], xs.at[n, 0], xs.at[n, 1], partner(me, "y0")) for n in range(9)]

    def complete(first, last):
        advance(mlp[first:last], 3)
        for cp in swap[first:last]:
            cp.start()

    advance(mlp[2:4] + mlp[5:6], 1)
    advance(att_a, 0)
    advance(mlp[0:2], 2)
    advance(mlp[6:8], 1)
    gains.start(1, gains.take(0))
    for j in range(2):
        gather_t.relay(j)
    advance(mlp[8:9], 0)
    advance(att_b[0:1], 0)
    advance(att_b[2:4], 0)
    advance(att_a, 1)
    gains.start(2, gains.take(1))
    advance(mlp[2:6], 2)
    gather_o = Gather(me, block_ref, s_blk, False)
    for j in range(2):
        block_ref[own_rows(me, j, False), :] = (mid_ref[halves(j), :] + sumf.step(j, 2)).astype(BF)
        gather_o.start(j)
    complete(0, 2)
    advance(att_b[1:2], 0)
    advance(mlp[8:9], 1)
    advance(att_b[0:1] + att_b[2:4], 1)
    advance(mlp[6:8], 2)
    advance(att_a, 2)
    complete(2, 6)
    for j in range(2):
        gather_o.relay(j)
    advance(att_b[1:2], 1)
    advance(mlp[8:9], 2)
    advance(att_b, 2)
    complete(6, 9)
    advance(att_a, 3)
    advance(att_b, 3)
    advance(att_a, 4)
    advance(att_b, 4)
    gains_ref[...] = gains.take(2)
    for n, cp in enumerate(swap):
        cp.wait_recv()
        k, i, _ = MLP_PIECES[n]
        (down_o, gate_o, up_o)[k][1 - pair, :, i * 256:(i + 1) * 256] = xrecv[n].astype(F32)

    for cp in swap:
        cp.wait_send()
    for gather in (gather_b, gather_o, gather_t):
        gather.finish()
    for gather in (gather_o, gather_t):
        for j in range(2):
            gather.wait(j)
    gains.finish()
    sum1.finish()
    for cp in g_copies:
        cp.wait_send()
    swap_gm.finish()
    swap_dqkv.finish()
    sumf.finish()
    for piece in mlp + att_a + att_b:
        piece.finish()


def layer(x, g, gain1, gain2, qg, kg, wq, wk, wv, wo, wg, wu, wd):
    cos_t, sin_t = rope_constants()
    V = pl.BlockSpec(memory_space=pltpu.VMEM)
    A = pl.BlockSpec(memory_space=pl.ANY)
    S = jax.ShapeDtypeStruct
    D = pltpu.SemaphoreType.DMA
    M = pltpu.VMEM
    return pl.pallas_call(
        layer_kernel,
        out_shape=(S((256, 2048), BF), S((256, 2048), BF), S((40, 128), F32),
                   S((2, 64, 768), F32), S((2, 64, 768), F32), S((2, 64, 768), F32), S((64, 512), F32), S((64, 512), F32),
                   S((64, 256), F32), S((64, 256), F32), S((8, 512, 256), BF), S((9, 1024, 256), BF)),
        in_specs=[A, A, V, V, V, V] + [A] * 9,
        out_specs=(V,) * 10 + (A, A),
        scratch_shapes=[
            M((256, 2048), BF), M((256, 2048), BF), M((512, 2048), BF), M((512, 2048), BF),
            M((2048, 512), BF), M((2048, 256), BF), M((2048, 256), BF), M((512, 2048), BF),
            M((3, 2048, 256), BF), M((3, 2048, 256), BF), M((768, 2048), BF),
            M((512, 2048), BF), M((512, 2048), BF),
            M((2, 4, 32, 2048), BF), M((2, 2, 32, 2048), BF), M((2, 1, 32, 2048), BF),
            M((2, 4, 32, 2048), BF), M((2, 2, 32, 2048), BF), M((2, 1, 32, 2048), BF), M((9, 512, 256), BF),
            M((8, 128, 384), BF), M((8, 128, 384), BF), M((8, 128, 128), BF), M((8, 128, 128), BF),
            M((8, 128, 128), BF), M((8, 128, 384), BF), M((1024, 256), F32), M((256, 512), BF), M((256, 768), F32),
            M((256, 1024), BF), M((64, 2048), F32), M((64, 2048), F32),
            M((64, 2048), BF), M((128, 128), F32), M((128, 128), F32),
            M((9, 2048, 256), BF), M((9, 512, 256), BF), M((9, 256, 256), BF), M((9, 128, 256), BF),
            M((9, 64, 256), BF), M((9, 64, 256), BF)]
        + [M((4, 1024 >> s, 128), BF) for s in range(5)] + [M((4, 1024 >> s, 256), BF) for s in range(5)]
        + [M((40, 128), F32), M((4, 40, 128), F32), M((8, 40, 128), F32), M((4, 40, 128), F32),
           D((16,)), D((2,)), D((2, 8)), D((2, 8)), D((2, 8)), D((2, 8)), D((2, 2, 2, 2)), D((2, 9, 2)), D((3, 2, 4, 2)),
           D((3, 2, 4, 2)), D((2, 3, 2)), D((2, 3, 2)), D((2, 2, 2, 2)), D((2, 3, 2)), D((2, 2)),
           D((9, 4)), D((9, 4)), D((4, 2)), D((9, 2)), D((4, 5)), D((4, 5)), D((4, 5)), D((4, 5)),
           D((2, 4)), D((2, 8)), D((2, 4))],
        compiler_params=pltpu.CompilerParams(collective_id=3, has_side_effects=True, vmem_limit_bytes=127 * 2**19),
    )(x, g, gain1, gain2, qg, kg, wq, wk, wv, wo, wg, wu, wd, jnp.asarray(cos_t), jnp.asarray(sin_t))


def tail_kernel(block_h, tok_h, gains, down_h, gate_h, up_h, out_h, q_h, k_h, v_h,
                block_o, tok_o, gain1_o, q_o, k_o, v_o, qg_o, kg_o, out_o, gain2_o, gate_o, up_o, down_o, sems):
    pairs = [(block_h, block_o), (tok_h, tok_o), (q_h, q_o), (k_h, k_o), (v_h, v_o), (out_h, out_o)]
    for i in range(2):
        c = pl.ds(i * 768, 768)
        pairs += [(down_h.at[i], down_o.at[:, c]), (gate_h.at[i], gate_o.at[:, c]), (up_h.at[i], up_o.at[:, c])]
    copies = [pltpu.make_async_copy(s, d, sems.at[i]) for i, (s, d) in enumerate(pairs)]
    for cp in copies:
        cp.start()
    gain1_o[...] = gains[0:16]
    gain2_o[...] = gains[16:32]
    qg_o[...] = gains[32:33]
    kg_o[...] = gains[33:34]
    for cp in copies:
        cp.wait()


def tail(block, tok, gains, down, gate, up, out, q, k, v):
    V = pl.BlockSpec(memory_space=pltpu.VMEM)
    A = pl.BlockSpec(memory_space=pl.ANY)
    S = jax.ShapeDtypeStruct
    return pl.pallas_call(
        tail_kernel,
        out_shape=(S((256, 2048), BF), S((256, 2048), BF), S((16, 128), F32), S((64, 512), F32), S((64, 256), F32),
                   S((64, 256), F32), S((1, 128), F32), S((1, 128), F32), S((64, 512), F32), S((16, 128), F32),
                   S((64, 1536), F32), S((64, 1536), F32), S((64, 1536), F32)),
        in_specs=[A, A, V, A, A, A, A, A, A, A],
        out_specs=(V,) * 13,
        scratch_shapes=[pltpu.SemaphoreType.DMA((12,))],
        compiler_params=pltpu.CompilerParams(vmem_limit_bytes=62 * 2**20),
    )(block, tok, gains, down, gate, up, out, q, k, v)


def local(tokens, attn_gain, w_query, w_key, w_value, query_gain, key_gain, w_out, mlp_gain, w_gate, w_up, w_down, out_grad):
    results = layer(tokens.reshape(256, 2048), out_grad.reshape(256, 2048), attn_gain, mlp_gain, query_gain, key_gain,
                    w_query, w_key, w_value, w_out, w_gate, w_up, w_down)
    block, tok, g1, q, k, v, qg, kg, out, g2, gate, up, down = tail(*results[:10])
    return (block.reshape(2, 128, 2048), tok.reshape(2, 128, 2048), g1.reshape(2048), q, k, v, qg.reshape(128),
            kg.reshape(128), out.T, g2.reshape(2048), gate, up, down.T)


def solution(mesh):
    in_specs = (
        P("dp", "context", None),
        P(),
        P(None, "tensor"),
        P(None, "tensor"),
        P(None, "tensor"),
        P(),
        P(),
        P("tensor", None),
        P(),
        P(None, "tensor"),
        P(None, "tensor"),
        P("tensor", None),
        P("dp", "context", None),
    )
    out_specs = (
        P("dp", "context", None),
        P("dp", "context", None),
        P(),
        P(("dp", "context"), "tensor"),
        P(("dp", "context"), "tensor"),
        P(("dp", "context"), "tensor"),
        P(),
        P(),
        P("tensor", ("dp", "context")),
        P(),
        P(("dp", "context"), "tensor"),
        P(("dp", "context"), "tensor"),
        P("tensor", ("dp", "context")),
    )
    return jax.shard_map(local, mesh=mesh, in_specs=in_specs, out_specs=out_specs, check_vma=False)
```
